32 devices in a mesh: slab: 8 (over z, x), cross: 4 (over y, core).
Axes of the slice: x: 2, y: 2, z: 4, core: 2. Of those that a mesh axis runs over, the one named last changes fastest.
Arguments:
- velocity: float32 [3, 128, 256, 256], P(None, 'slab', 'cross'), may hold values from -6 to 6
- shape_weight: float32 [32, 384], replicated, may hold values from -6 to 6
- w_in: bfloat16 [384, 1024], replicated, may hold values from -0.3125 to 0.3125
- w_out: bfloat16 [1024, 4096], replicated, may hold values from -0.1875 to 0.1875
- decay: float32 [1024], replicated, may hold values from 0.1 to 2
- rotor_states: float32 [32, 1024], P('slab'), may hold values from -6 to 6
- slot_of_rotor: int32 [32], replicated, may hold values from 0 to 31, each once
- entry_rotor: int32 [32768, 1], P(('slab', 'cross')), may hold values from 0 to 31; in each aligned block of 1024 rows (0 to 1023, 1024 to 2047, ...) at most 64 rows name the same one
- entry_tile: int32 [32768], P(('slab', 'cross')), may hold values from 0 to 2047
- entry_sub: int32 [32768], P(('slab', 'cross')), may hold values from 0 to 31
Outputs:
- advanced: float32 [3, 128, 256, 256], P(None, 'slab', 'cross')
- new_states: float32 [32, 1024], P('slab')
The draws below stay inside these ranges and needn't reach their ends.
Inputs may be any that keep to these rules, and one draw needn't show every extreme that they name: `entry_rotor`: in the rows of one device no rotor is named more than 64 times, a bound that some block reaches; every rotor is named by some entry. Each slot once; rotor r is owned by slab slot_of_rotor[r] // 4.
All inputs are finite; a program needn't handle non-finite values.
Results may differ from the reference program's by a relative error of at most 0.0026.
Values may be sent and summed in bfloat16 or wider, within the bound.
No kernel may reach another device: no remote copies, remote signals or barrier semaphores. Data moves between devices by JAX's collectives and lax.ppermute only.
A program may use at most 64 MiB of HBM per device.

```python
import math
import jax
import jax.numpy as jnp
import numpy as np
from jax import lax

CX = 16
CY = 64
NZ = 256
TILE = 128
R = 32
S = 1024
NSRC = 4096
E_DEV = 1024
CAP = 64
NSUB = 32
TILES_DEV = 2048
NX = 128
NY = 256
ENTRIES = 32768
N_CROSS = 4


def set_ends(values, own_key, smallest, high):
    dims = values.shape
    place = [jax.random.randint(jax.random.fold_in(own_key, axis), (), 0, dims[axis]) for axis in range(len(dims))]
    values = values.at[tuple(place)].set(smallest)
    longest = dims.index(max(dims))
    place[longest] = (place[longest] + 1) % dims[longest]
    return values.at[tuple(place)].set(high)


def level_of(stream_key, shape, split, smallest, top_value):
    factor_of, own = 1.0, jax.random.fold_in(stream_key, 6)
    for dim, parts in split:
        heights = jnp.exp(jax.random.uniform(jax.random.fold_in(own, dim), (parts,), jnp.float32, smallest / len(split), top_value / len(split)))
        factor_of = factor_of * jnp.repeat(heights, shape[dim] // parts).reshape([-1 if axis == dim else 1 for axis in range(len(shape))])
    return factor_of


def deal_out(key, own, number, rows, amount, top, limit, skew):
    order = jax.random.permutation(key, amount)
    heavy_load, usual = load_shares(amount, rows * top, limit, skew, True), load_shares(amount, rows * top, limit, skew, False)
    places = jnp.arange(amount)

    def named(lengths, turn):
        used = int((lengths > 0).sum())
        fixed = max(1, used // 4)
        shifted = fixed + (places - fixed + turn * (used - fixed)) % max(1, amount - fixed)
        return jnp.zeros((amount,), jnp.int32).at[order[jnp.where(places < fixed, places, shifted)]].set(jnp.asarray(lengths, jnp.int32))

    lengths = jnp.where(number % 4 == 0, named(heavy_load, number // 4), named(usual, number - number // 4 - 1))
    mixed = jax.random.permutation(jax.random.fold_in(own, 3), amount)
    giver, taker = mixed[0:amount // 2 * 2:2], mixed[1:amount // 2 * 2:2]
    room = jnp.minimum(lengths[giver] - 1, limit - lengths[taker]) // 2
    room = jnp.where((giver == order[0]) | (taker == order[0]) | (lengths[taker] == 0), 0, jnp.maximum(room, 0))
    shifted = jax.random.randint(jax.random.fold_in(own, 4), (amount // 2,), 0, 1 << 20) % (room + 1)
    lengths = lengths.at[giver].add(-shifted).at[taker].add(shifted)
    items = jnp.searchsorted(jnp.cumsum(lengths), jnp.arange(rows * top), side="right").astype(jnp.int32)
    listing = items.reshape(top, rows).T
    listing = listing[jax.random.permutation(jax.random.fold_in(own, 1), rows)]
    turn = jax.random.randint(jax.random.fold_in(own, 2), (rows, 1), 0, top)
    return jnp.take_along_axis(listing, (jnp.arange(top)[None, :] + turn) % top, axis=1)


def load_shares(number_of, total, most, lean, full):
    loads = [(1 << 20) // math.isqrt(rank ** lean) + 1 for rank in range(1, number_of + 1)]
    largest = most if full else min(most, max(-(-total // number_of), total * loads[0] // sum(loads)))
    least = 1 if total - largest >= number_of - 1 else 0
    counts, rest = [largest] + [least] * (number_of - 1), total - largest - least * (number_of - 1)
    while rest > 0:
        candidates = [i for i in range(1, number_of) if counts[i] < largest] or [i for i in range(1, number_of) if counts[i] < most]
        pool, remaining = sum([loads[i] for i in candidates]), rest
        for i in candidates:
            addition = min(most - counts[i], max(1, remaining * loads[i] // pool), rest)
            counts[i] = counts[i] + addition
            rest = rest - addition
    return np.array(counts)


def noise(stream_key, extent, scale, reach, split=(), kind=jnp.bfloat16):
    loudness = level_of(stream_key, extent, split, -0.22, 0.18) if split else 1.0
    values = jax.random.normal(stream_key, extent, jnp.float32) * scale * loudness
    return jnp.minimum(jnp.maximum(values, -reach), reach).astype(kind)


def setup_inputs(seed: int = 0) -> dict:
    key_of = jax.random.split(jax.random.key(seed), 11)
    velocity = noise(key_of[0], (3, NX, NY, NZ), 1.0, 6.0, ((1, 8), (2, 4)), jnp.float32)
    shape_weight = noise(key_of[1], (NSUB, 3 * TILE), 1.0, 6.0, (), jnp.float32)
    w_in = noise(key_of[2], (3 * TILE, S), (3 * TILE) ** -0.5, 0.3125)
    w_out = noise(key_of[3], (S, NSRC), S ** -0.5, 0.1875)
    decay = jnp.clip(jnp.exp(jax.random.uniform(key_of[4], (S,), jnp.float32, math.log(0.1), math.log(2.0))), 0.1, 2.0)
    rotor_states = noise(key_of[5], (R, S), 1.0, 6.0, ((0, 8),), jnp.float32)
    slot_of_rotor = jax.random.permutation(key_of[6], R).astype(jnp.int32)
    entry_rotor_keys = jax.random.split(jax.random.fold_in(key_of[7], 1), ENTRIES // E_DEV)
    entry_rotor_turns = jax.random.permutation(jax.random.fold_in(key_of[7], 3), ENTRIES // E_DEV)
    entry_rotor = jax.vmap(lambda own, number: deal_out(jax.random.fold_in(key_of[7], 2), own, number, E_DEV, R, 1, CAP, 2))(entry_rotor_keys, entry_rotor_turns).reshape((ENTRIES, 1))
    entry_tile = set_ends(jax.random.randint(key_of[8], (ENTRIES,), 0, TILES_DEV), jax.random.fold_in(key_of[8], 1), 0, TILES_DEV - 1).astype(jnp.int32)
    entry_sub = set_ends(jax.random.randint(key_of[9], (ENTRIES,), 0, NSUB), jax.random.fold_in(key_of[9], 1), 0, NSUB - 1).astype(jnp.int32)
    return dict(velocity=velocity, shape_weight=shape_weight, w_in=w_in, w_out=w_out, decay=decay, rotor_states=rotor_states, slot_of_rotor=slot_of_rotor, entry_rotor=entry_rotor, entry_tile=entry_tile, entry_sub=entry_sub)


time_step = 0.1
viscosity = 0.3
pool_scale = 1.0 / 64.0
state_step = 0.5
force_scale = 0.5


def stencil_core(velocity, padded):
    east = padded[:, 2:, 1:-1, 1:-1]
    west = padded[:, :-2, 1:-1, 1:-1]
    north = padded[:, 1:-1, 2:, 1:-1]
    south = padded[:, 1:-1, :-2, 1:-1]
    upper = padded[:, 1:-1, 1:-1, 2:]
    lower = padded[:, 1:-1, 1:-1, :-2]
    laplace = east + west + north + south + upper + lower - 6.0 * velocity
    advect = velocity[0:1] * ((east - west) * 0.5) + velocity[1:2] * ((north - south) * 0.5) + velocity[2:3] * ((upper - lower) * 0.5)
    return velocity + time_step * (viscosity * laplace - advect)


def reference(velocity, shape_weight, w_in, w_out, decay, rotor_states, slot_of_rotor, entry_rotor, entry_tile, entry_sub):
    ztiles = NZ // TILE
    entries = entry_tile.shape[0]
    position = jnp.arange(entries, dtype=jnp.int32)
    device = position // E_DEV
    slab_id = device // N_CROSS
    cross_id = device % N_CROSS
    xpos = slab_id * CX + entry_tile // (CY * ztiles)
    ypos = cross_id * CY + (entry_tile // ztiles) % CY
    zpos = entry_tile % ztiles
    cells = velocity.reshape(3, NX, NY, ztiles, TILE)
    picked = cells[:, xpos, ypos, zpos, :].astype(jnp.bfloat16)
    picked = lax.optimization_barrier(picked).astype(jnp.float32)
    samples = jnp.transpose(picked, (1, 0, 2)).reshape(entries, 3 * TILE)
    weighted = shape_weight[entry_sub] * samples
    slots = slot_of_rotor[entry_rotor[:, 0]]
    pooled = jax.ops.segment_sum(weighted, slots, num_segments=R)
    pooled_b = (pooled * pool_scale).astype(jnp.bfloat16)
    drive = jnp.dot(pooled_b, w_in, preferred_element_type=jnp.float32)
    new_states = rotor_states + state_step * (drive - decay[None, :] * rotor_states)
    sources = jnp.dot(new_states.astype(jnp.bfloat16), w_out, preferred_element_type=jnp.float32).astype(jnp.bfloat16)
    rows = sources.reshape(R * NSUB, TILE)[slots * NSUB + entry_sub].astype(jnp.float32)
    forcing = jnp.zeros((NX, NY, ztiles, TILE), jnp.float32).at[xpos, ypos, zpos].add(rows)
    padded = jnp.pad(velocity, ((0, 0), (1, 1), (1, 1), (1, 1)))
    advanced = stencil_core(velocity, padded)
    advanced = advanced.at[0].add(-force_scale * forcing.reshape(NX, NY, NZ))
    return advanced, new_states
```

```python
import functools

import jax
import jax.numpy as jnp
from jax import lax
from jax.experimental import pallas as pl
from jax.experimental.pallas import tpu as pltpu
from jax.sharding import PartitionSpec as P

TILE = 128

time_step = 0.1
viscosity = 0.3
pool_scale = 1.0 / 64.0
state_step = 0.5
force_scale = 0.5

BOTH = ("slab", "cross")
F32 = jnp.float32
BF16 = jnp.bfloat16


def lanes(rows):
    return lax.broadcasted_iota(jnp.int32, (rows, TILE), 1)


def sublanes(rows):
    return lax.broadcasted_iota(jnp.int32, (rows, TILE), 0)


def as_column(row):
    return jnp.transpose(jnp.broadcast_to(row, (TILE, TILE)))


def hot(mask):
    return jnp.where(mask, 1.0, 0.0).astype(BF16)


def slots_of(rotor_ref, slot_ref):
    rotors = rotor_ref[...]
    slots = jnp.zeros_like(rotors)
    for rotor in range(slot_ref.shape[0]):
        slots = jnp.where(rotors == rotor, slot_ref[rotor], slots)
    return slots


def pool_kernel(
    tile_ref,
    rotor_ref,
    sub_ref,
    slot_ref,
    weight_ref,
    velocity_ref,
    part_ref,
    west_ref,
    east_ref,
    south_ref,
    north_ref,
    cells,
    place_hot,
    gains,
    half_column,
    sems,
):
    parts, size_x, size_y, size_z = velocity_ref.shape
    columns = size_x * size_y
    halves = size_z // TILE
    groups = tile_ref.shape[0]
    entries = groups * TILE
    rotors = slot_ref.shape[0]
    subs = weight_ref.shape[0]
    copies = [
        pltpu.make_async_copy(velocity_ref.at[c], cells.at[c], sems.at[c]) for c in range(parts)
    ]
    for copy in copies:
        copy.start()
    weight = weight_ref[...]
    high = weight.astype(BF16)
    rest = weight - high.astype(F32)
    middle = rest.astype(BF16)
    low = (rest - middle.astype(F32)).astype(BF16)
    weight_parts = jnp.concatenate([high, middle, low], axis=0)
    sub_hot = []
    place_rows = tile_ref[...] // halves
    half_rows = tile_ref[...] % halves
    for group in range(groups):
        half_column[pl.ds(group * TILE, TILE), :] = as_column(half_rows[group : group + 1, :])
        place = as_column(place_rows[group : group + 1, :])
        for block in range(columns // TILE):
            place_hot[pl.ds(group * TILE, TILE), pl.ds(block * TILE, TILE)] = hot(
                place == lanes(TILE) + block * TILE
            )
        sub = as_column(sub_ref[group : group + 1, :])
        wide = jnp.concatenate([sub[:, :subs]] * 3, axis=1)
        index = lax.broadcasted_iota(jnp.int32, (TILE, subs), 1)
        sub_hot.append(hot(wide == jnp.concatenate([index] * 3, axis=1)))
    gains[...] = jnp.dot(
        jnp.concatenate(sub_hot, axis=0), weight_parts, preferred_element_type=F32
    )
    slots = slots_of(rotor_ref, slot_ref)
    slot_hot = jnp.concatenate(
        [hot(slots[g : g + 1, :] == sublanes(rotors)) for g in range(groups)], axis=1
    )
    half = half_column[...]
    for c in range(parts):
        copies[c].wait()
        flat = cells[c].reshape(columns, size_z).astype(BF16)
        found = jnp.dot(place_hot[...], flat, preferred_element_type=F32)
        sample = found[:, :TILE]
        for h in range(1, halves):
            sample = jnp.where(half == h, found[:, h * TILE : (h + 1) * TILE], sample)
        weighted = sample * gains[:, c * TILE : (c + 1) * TILE]
        high = weighted.astype(BF16)
        rest = weighted - high.astype(F32)
        middle = rest.astype(BF16)
        low = (rest - middle.astype(F32)).astype(BF16)
        sums = jnp.dot(
            slot_hot, jnp.concatenate([high, middle, low], axis=1), preferred_element_type=F32
        )
        part_ref[:, c * TILE : (c + 1) * TILE] = (
            sums[:, 2 * TILE :] + sums[:, TILE : 2 * TILE] + sums[:, :TILE]
        )
        west_ref[c] = cells[c, 0].astype(BF16)
        east_ref[c] = cells[c, size_x - 1].astype(BF16)
        south_ref[c] = cells[c, :, 0, :].astype(BF16)
        north_ref[c] = cells[c, :, size_y - 1, :].astype(BF16)


def stencil_kernel(velocity_ref, west_ref, east_ref, south_ref, north_ref, out_ref, cells, result, sems, out_sems):
    parts, size_x, size_y, size_z = velocity_ref.shape
    chunks = sems.shape[0]
    depth = size_x // chunks

    def load(chunk):
        at = pl.ds(chunk * depth, depth)
        return pltpu.make_async_copy(velocity_ref.at[:, at], cells.at[:, at], sems.at[chunk])

    def store(chunk):
        at = pl.ds(chunk * depth, depth)
        return pltpu.make_async_copy(result.at[:, at], out_ref.at[:, at], out_sems.at[chunk])

    for chunk in range(chunks):
        load(chunk).start()
    row = lax.broadcasted_iota(jnp.int32, (size_y, size_z), 0)
    lane = lax.broadcasted_iota(jnp.int32, (size_y, size_z), 1)
    load(0).wait()
    for chunk in range(chunks):
        if chunk + 1 < chunks:
            load(chunk + 1).wait()
        for x in range(chunk * depth, (chunk + 1) * depth):
            wind = [cells[c, x] for c in range(parts)]
            for c in range(parts):
                here = wind[c]
                west = cells[c, x - 1] if x > 0 else west_ref[c].astype(F32)
                east = cells[c, x + 1] if x + 1 < size_x else east_ref[c].astype(F32)
                south = jnp.where(
                    row == 0, south_ref[c, x : x + 1, :].astype(F32), pltpu.roll(here, 1, 0)
                )
                north = jnp.where(
                    row == size_y - 1,
                    north_ref[c, x : x + 1, :].astype(F32),
                    pltpu.roll(here, size_y - 1, 0),
                )
                lower = jnp.where(lane == 0, 0.0, pltpu.roll(here, 1, 1))
                upper = jnp.where(lane == size_z - 1, 0.0, pltpu.roll(here, size_z - 1, 1))
                laplace = east + west + north + south + upper + lower - 6.0 * here
                advect = (
                    wind[0] * ((east - west) * 0.5)
                    + wind[1] * ((north - south) * 0.5)
                    + wind[2] * ((upper - lower) * 0.5)
                )
                result[c, x] = here + time_step * (viscosity * laplace - advect)
        store(chunk).start()
    for chunk in range(chunks):
        store(chunk).wait()


def rotor_kernel(
    index_ref,
    slot_ref,
    tile_ref,
    rotor_ref,
    sub_ref,
    pooled_ref,
    w_in_ref,
    w_out_ref,
    decay_ref,
    states_ref,
    field_ref,
    out_ref,
    new_ref,
    wind,
    states,
    by_slab,
    source_rows,
    key_hot,
    place_hot,
    sems,
):
    slabs, rows, width = states_ref.shape
    rotors = slabs * rows
    _, size_x, size_y, size_z = field_ref.shape
    columns = size_x * size_y
    halves = size_z // TILE
    groups = tile_ref.shape[0]
    subs = w_out_ref.shape[1] // TILE
    me = index_ref[0]
    load = pltpu.make_async_copy(field_ref.at[0], wind, sems.at[0])
    load.start()
    slots = slots_of(rotor_ref, slot_ref)
    for j in range(slabs):
        states[j * rows : (j + 1) * rows, :] = states_ref[me ^ j]
    pooled = (pooled_ref[...] * pool_scale).astype(BF16)
    drive = jnp.dot(pooled, w_in_ref[...], preferred_element_type=F32)
    old = states[...]
    new = old + state_step * (drive - decay_ref[...] * old)
    for j in range(slabs):
        by_slab[j] = new[j * rows : (j + 1) * rows, :]
    new_ref[...] = by_slab[me]
    new_b = new.astype(BF16)
    keys = sub_ref[...] * rotors + slots
    tiles = tile_ref[...]
    place_rows = tiles // halves
    half_rows = tiles % halves
    for group in range(groups):
        key = as_column(keys[group : group + 1, :])
        at = pl.ds(group * TILE, TILE)
        for block in range(subs * rotors // TILE):
            key_hot[at, pl.ds(block * TILE, TILE)] = hot(key == lanes(TILE) + block * TILE)
        for block in range(columns // TILE):
            place_hot[pl.ds(block * TILE, TILE), at] = hot(
                place_rows[group : group + 1, :] == sublanes(TILE) + block * TILE
            )
    sources = jnp.dot(new_b, w_out_ref[...], preferred_element_type=F32).astype(BF16)
    for sub in range(subs):
        source_rows[sub * rotors : (sub + 1) * rotors, :] = sources[:, sub * TILE : (sub + 1) * TILE]
    taken = jnp.dot(key_hot[...], source_rows[...], preferred_element_type=F32).astype(BF16)
    half = jnp.concatenate([as_column(half_rows[g : g + 1, :]) for g in range(groups)], axis=0)
    spread = jnp.concatenate(
        [jnp.where(half == h, taken.astype(F32), 0.0).astype(BF16) for h in range(halves)], axis=1
    )
    forcing = jnp.dot(place_hot[...], spread, preferred_element_type=F32)
    load.wait()
    wind[...] = wind[...] - force_scale * forcing.reshape(size_x, size_y, size_z)
    store = pltpu.make_async_copy(wind, out_ref.at[0], sems.at[1])
    store.start()
    store.wait()


def xor_groups(bits):
    first = bits % 2
    groups = [(0,)] if first else []
    return groups + [(b, b + 1) for b in range(first, bits, 2)]


def offsets_of(group):
    found = [0]
    for bit in group:
        found = found + [offset | (1 << bit) for offset in found]
    return found[1:]


def exchange(value, axis, count, offset):
    return lax.ppermute(value, axis, [(i, i ^ offset) for i in range(count)])


def sum_all(value, axis, count):
    for group in xor_groups(count.bit_length() - 1):
        received = [exchange(value, axis, count, offset) for offset in offsets_of(group)]
        for other in received:
            value = value + other
    return value


def gather_xor(value, axis, count):
    blocks = value[None]
    for bit in range(count.bit_length() - 1):
        blocks = jnp.concatenate([blocks, exchange(blocks, axis, count, 1 << bit)], axis=0)
    return blocks


def vmem(count):
    return [pl.BlockSpec(memory_space=pltpu.VMEM)] * count


SMEM = pl.BlockSpec(memory_space=pltpu.SMEM)
ANY = pl.BlockSpec(memory_space=pl.ANY)


def on_device(
    slabs,
    crosses,
    velocity,
    shape_weight,
    w_in,
    w_out,
    decay,
    rotor_states,
    slot_of_rotor,
    entry_rotor,
    entry_tile,
    entry_sub,
):
    parts, size_x, size_y, size_z = velocity.shape
    columns = size_x * size_y
    entries = entry_tile.shape[0]
    groups = entries // TILE
    rotors = slot_of_rotor.shape[0]
    subs = shape_weight.shape[0]
    width = w_in.shape[1]
    rows = rotor_states.shape[0]
    tile = entry_tile.reshape(groups, TILE)
    rotor = entry_rotor.reshape(groups, TILE)
    sub = entry_sub.reshape(groups, TILE)

    gathered = gather_xor(rotor_states, "slab", slabs)
    part, west, east, south, north = pl.pallas_call(
        pool_kernel,
        out_shape=(
            jax.ShapeDtypeStruct((rotors, parts * TILE), F32),
            jax.ShapeDtypeStruct((parts, size_y, size_z), BF16),
            jax.ShapeDtypeStruct((parts, size_y, size_z), BF16),
            jax.ShapeDtypeStruct((parts, size_x, size_z), BF16),
            jax.ShapeDtypeStruct((parts, size_x, size_z), BF16),
        ),
        in_specs=vmem(3) + [SMEM] + vmem(1) + [ANY],
        out_specs=tuple(vmem(5)),
        scratch_shapes=[
            pltpu.VMEM(velocity.shape, F32),
            pltpu.VMEM((entries, columns), BF16),
            pltpu.VMEM((entries, parts * TILE), F32),
            pltpu.VMEM((entries, TILE), jnp.int32),
            pltpu.SemaphoreType.DMA((parts,)),
        ],
        compiler_params=pltpu.CompilerParams(vmem_limit_bytes=24 << 20),
        cost_estimate=pl.CostEstimate(
            flops=2 * entries * columns * parts * size_z,
            bytes_accessed=velocity.size * 4,
            transcendentals=0,
        ),
        name="pool",
    )(tile, rotor, sub, slot_of_rotor, shape_weight, velocity)

    pooled = sum_all(part, BOTH, slabs * crosses)

    up = lambda count: [(i, i + 1) for i in range(count - 1)]
    down = lambda count: [(i + 1, i) for i in range(count - 1)]
    from_west = lax.ppermute(east, "slab", up(slabs))
    from_east = lax.ppermute(west, "slab", down(slabs))
    from_south = lax.ppermute(north, "cross", up(crosses))
    from_north = lax.ppermute(south, "cross", down(crosses))
    chunks = 4
    field = pl.pallas_call(
        stencil_kernel,
        out_shape=jax.ShapeDtypeStruct(velocity.shape, F32),
        in_specs=[ANY] + vmem(4),
        out_specs=ANY,
        scratch_shapes=[
            pltpu.VMEM(velocity.shape, F32),
            pltpu.VMEM(velocity.shape, F32),
            pltpu.SemaphoreType.DMA((chunks,)),
            pltpu.SemaphoreType.DMA((chunks,)),
        ],
        compiler_params=pltpu.CompilerParams(vmem_limit_bytes=16 << 20),
        cost_estimate=pl.CostEstimate(
            flops=30 * velocity.size, bytes_accessed=velocity.size * 8, transcendentals=0
        ),
        name="stencil",
    )(velocity, from_west, from_east, from_south, from_north)

    index = lax.axis_index("slab").astype(jnp.int32).reshape(1)
    return pl.pallas_call(
        rotor_kernel,
        out_shape=(
            jax.ShapeDtypeStruct(velocity.shape, F32),
            jax.ShapeDtypeStruct(rotor_states.shape, F32),
        ),
        in_specs=[SMEM, SMEM] + vmem(8) + [ANY],
        out_specs=(ANY, pl.BlockSpec(memory_space=pltpu.VMEM)),
        scratch_shapes=[
            pltpu.VMEM((size_x, size_y, size_z), F32),
            pltpu.VMEM((rotors, width), F32),
            pltpu.VMEM((slabs, rows, width), F32),
            pltpu.VMEM((subs * rotors, TILE), BF16),
            pltpu.VMEM((entries, subs * rotors), BF16),
            pltpu.VMEM((columns, entries), BF16),
            pltpu.SemaphoreType.DMA((2,)),
        ],
        input_output_aliases={10: 0},
        compiler_params=pltpu.CompilerParams(vmem_limit_bytes=32 << 20),
        cost_estimate=pl.CostEstimate(
            flops=4 * entries * columns * size_z, bytes_accessed=w_out.size * 2, transcendentals=0
        ),
        name="rotors",
    )(index, slot_of_rotor, tile, rotor, sub, pooled, w_in, w_out, decay[None, :], gathered, field)


def solution(mesh):
    slabs, crosses = mesh.shape["slab"], mesh.shape["cross"]
    in_specs = (
        P(None, "slab", "cross", None),
        P(),
        P(),
        P(),
        P(),
        P("slab", None),
        P(),
        P(("slab", "cross"), None),
        P(("slab", "cross")),
        P(("slab", "cross")),
    )
    out_specs = (P(None, "slab", "cross", None), P("slab", None))
    return jax.shard_map(
        functools.partial(on_device, slabs, crosses),
        mesh=mesh,
        in_specs=in_specs,
        out_specs=out_specs,
        check_vma=False,
    )
```

```python
import functools

import jax
import jax.numpy as jnp
from jax import lax
from jax.experimental import pallas as pl
from jax.experimental.pallas import tpu as pltpu
from jax.sharding import PartitionSpec as P

TILE = 128

time_step = 0.1
viscosity = 0.3
pool_scale = 1.0 / 64.0
state_step = 0.5
force_scale = 0.5

BOTH = ("slab", "cross")
F32 = jnp.float32
BF16 = jnp.bfloat16


def lanes(rows):
    return lax.broadcasted_iota(jnp.int32, (rows, TILE), 1)


def sublanes(rows):
    return lax.broadcasted_iota(jnp.int32, (rows, TILE), 0)


def as_column(row):
    return jnp.transpose(jnp.broadcast_to(row, (TILE, TILE)))


def hot(mask):
    return jnp.where(mask, 1.0, 0.0).astype(BF16)


def slots_of(rotors, slot_ref):
    slots = jnp.zeros_like(rotors)
    for rotor in range(slot_ref.shape[0]):
        slots = jnp.where(rotors == rotor, slot_ref[rotor], slots)
    return slots


def pool_kernel(
    tile_ref,
    rotor_ref,
    sub_ref,
    slot_ref,
    weight_ref,
    velocity_ref,
    part_ref,
    west_ref,
    east_ref,
    south_ref,
    north_ref,
    cells,
    tiles,
    rotor_rows,
    sub_rows,
    slot_table,
    weights,
    place_hot,
    gains,
    half_column,
    sems,
    small_sems,
):
    parts, size_x, size_y, size_z = velocity_ref.shape
    columns = size_x * size_y
    halves = size_z // TILE
    groups = tile_ref.shape[0]
    entries = groups * TILE
    rotors = slot_ref.shape[0]
    subs = weight_ref.shape[0]
    small = [
        pltpu.make_async_copy(source, target, small_sems.at[i])
        for i, (source, target) in enumerate(
            (
                (tile_ref, tiles),
                (sub_ref, sub_rows),
                (weight_ref, weights),
                (rotor_ref, rotor_rows),
                (slot_ref, slot_table),
            )
        )
    ]
    copies = [
        pltpu.make_async_copy(velocity_ref.at[c], cells.at[c], sems.at[c]) for c in range(parts)
    ]
    for copy in small + copies:
        copy.start()
    for copy in small:
        copy.wait()
    weight = weights[...]
    high = weight.astype(BF16)
    rest = weight - high.astype(F32)
    middle = rest.astype(BF16)
    low = (rest - middle.astype(F32)).astype(BF16)
    weight_parts = jnp.concatenate([high, middle, low], axis=0)
    sub_hot = []
    place_rows = tiles[...] // halves
    half_rows = tiles[...] % halves
    for group in range(groups):
        half_column[pl.ds(group * TILE, TILE), :] = as_column(half_rows[group : group + 1, :])
        place = as_column(place_rows[group : group + 1, :])
        for block in range(columns // TILE):
            place_hot[pl.ds(group * TILE, TILE), pl.ds(block * TILE, TILE)] = hot(
                place == lanes(TILE) + block * TILE
            )
        sub = as_column(sub_rows[group : group + 1, :])
        wide = jnp.concatenate([sub[:, :subs]] * 3, axis=1)
        index = lax.broadcasted_iota(jnp.int32, (TILE, subs), 1)
        sub_hot.append(hot(wide == jnp.concatenate([index] * 3, axis=1)))
    gains[...] = jnp.dot(
        jnp.concatenate(sub_hot, axis=0), weight_parts, preferred_element_type=F32
    )
    slots = slots_of(rotor_rows[...], slot_table)
    slot_hot = jnp.concatenate(
        [hot(slots[g : g + 1, :] == sublanes(rotors)) for g in range(groups)], axis=1
    )
    half = half_column[...]
    for c in range(parts):
        copies[c].wait()
        flat = cells[c].reshape(columns, size_z).astype(BF16)
        found = jnp.dot(place_hot[...], flat, preferred_element_type=F32)
        sample = found[:, :TILE]
        for h in range(1, halves):
            sample = jnp.where(half == h, found[:, h * TILE : (h + 1) * TILE], sample)
        weighted = sample * gains[:, c * TILE : (c + 1) * TILE]
        high = weighted.astype(BF16)
        rest = weighted - high.astype(F32)
        middle = rest.astype(BF16)
        low = (rest - middle.astype(F32)).astype(BF16)
        sums = jnp.dot(
            slot_hot, jnp.concatenate([high, middle, low], axis=1), preferred_element_type=F32
        )
        part_ref[:, c * TILE : (c + 1) * TILE] = (
            sums[:, 2 * TILE :] + sums[:, TILE : 2 * TILE] + sums[:, :TILE]
        )
        west_ref[c] = cells[c, 0].astype(BF16)
        east_ref[c] = cells[c, size_x - 1].astype(BF16)
        south_ref[c] = cells[c, :, 0, :].astype(BF16)
        north_ref[c] = cells[c, :, size_y - 1, :].astype(BF16)


def stencil_kernel(
    slot_ref,
    tile_ref,
    rotor_ref,
    sub_ref,
    velocity_ref,
    west_ref,
    east_ref,
    south_ref,
    north_ref,
    w_out_ref,
    out_ref,
    wind_ref,
    key_ref,
    place_ref,
    w_out_here,
    result,
    w_sem,
    out_sems,
):
    parts, size_x, size_y, size_z = velocity_ref.shape
    columns = size_x * size_y
    halves = size_z // TILE
    groups = tile_ref.shape[0]
    rotors = slot_ref.shape[0]
    keys_size = key_ref.shape[1]
    chunks = out_sems.shape[0]
    depth = size_x // chunks
    bring = pltpu.make_async_copy(w_out_ref, w_out_here, w_sem)
    bring.start()

    def store(chunk):
        at = pl.ds(chunk * depth, depth)
        return pltpu.make_async_copy(result.at[:, at], out_ref.at[1:, at], out_sems.at[chunk])

    row = lax.broadcasted_iota(jnp.int32, (size_y, size_z), 0)
    lane = lax.broadcasted_iota(jnp.int32, (size_y, size_z), 1)
    for chunk in range(chunks):
        for x in range(chunk * depth, (chunk + 1) * depth):
            wind = [velocity_ref[c, x] for c in range(parts)]
            for c in range(parts):
                here = wind[c]
                west = velocity_ref[c, x - 1] if x > 0 else west_ref[c].astype(F32)
                east = velocity_ref[c, x + 1] if x + 1 < size_x else east_ref[c].astype(F32)
                south = jnp.where(
                    row == 0, south_ref[c, x : x + 1, :].astype(F32), pltpu.roll(here, 1, 0)
                )
                north = jnp.where(
                    row == size_y - 1,
                    north_ref[c, x : x + 1, :].astype(F32),
                    pltpu.roll(here, size_y - 1, 0),
                )
                lower = jnp.where(lane == 0, 0.0, pltpu.roll(here, 1, 1))
                upper = jnp.where(lane == size_z - 1, 0.0, pltpu.roll(here, size_z - 1, 1))
                laplace = east + west + north + south + upper + lower - 6.0 * here
                advect = (
                    wind[0] * ((east - west) * 0.5)
                    + wind[1] * ((north - south) * 0.5)
                    + wind[2] * ((upper - lower) * 0.5)
                )
                value = here + time_step * (viscosity * laplace - advect)
                if c == 0:
                    wind_ref[x] = value
                else:
                    result[c - 1, x] = value
        store(chunk).start()
    slots = slots_of(rotor_ref[...], slot_ref)
    keys = sub_ref[...] * rotors + slots
    places = tile_ref[...] // halves
    for group in range(groups):
        key = as_column(keys[group : group + 1, :])
        at = pl.ds(group * TILE, TILE)
        for block in range(keys_size // TILE):
            key_ref[at, pl.ds(block * TILE, TILE)] = hot(key == lanes(TILE) + block * TILE)
        for block in range(columns // TILE):
            place_ref[pl.ds(block * TILE, TILE), at] = hot(
                places[group : group + 1, :] == sublanes(TILE) + block * TILE
            )
    for chunk in range(chunks):
        store(chunk).wait()
    bring.wait()


def rotor_kernel(
    index_ref,
    tile_ref,
    pooled_ref,
    w_in_ref,
    w_out_ref,
    decay_ref,
    states_ref,
    wind_ref,
    key_ref,
    place_ref,
    field_ref,
    out_ref,
    new_ref,
    states,
    by_slab,
    source_rows,
    wind,
    sems,
):
    slabs, rows, width = states_ref.shape
    rotors = slabs * rows
    size_x, size_y, size_z = wind_ref.shape
    halves = size_z // TILE
    groups = tile_ref.shape[0]
    subs = w_out_ref.shape[1] // TILE
    me = index_ref[0]
    for j in range(slabs):
        states[j * rows : (j + 1) * rows, :] = states_ref[me ^ j]
    pooled = (pooled_ref[...] * pool_scale).astype(BF16)
    drive = jnp.dot(pooled, w_in_ref[...], preferred_element_type=F32)
    old = states[...]
    new = old + state_step * (drive - decay_ref[...] * old)
    for j in range(slabs):
        by_slab[j] = new[j * rows : (j + 1) * rows, :]
    new_ref[...] = by_slab[me]
    new_b = new.astype(BF16)
    half_rows = tile_ref[...] % halves
    sources = jnp.dot(new_b, w_out_ref[...], preferred_element_type=F32).astype(BF16)
    for sub in range(subs):
        source_rows[sub * rotors : (sub + 1) * rotors, :] = sources[:, sub * TILE : (sub + 1) * TILE]
    taken = jnp.dot(key_ref[...], source_rows[...], preferred_element_type=F32)
    half = jnp.concatenate([as_column(half_rows[g : g + 1, :]) for g in range(groups)], axis=0)
    spread = jnp.concatenate(
        [jnp.where(half == h, taken, 0.0).astype(BF16) for h in range(halves)], axis=1
    )
    chunks = sems.shape[0]
    depth = size_x // chunks
    stores = []
    for chunk in range(chunks):
        at = pl.ds(chunk * depth, depth)
        forcing = jnp.dot(
            place_ref[pl.ds(chunk * depth * size_y, depth * size_y), :],
            spread,
            preferred_element_type=F32,
        )
        wind[at] = wind_ref[at] - force_scale * forcing.reshape(depth, size_y, size_z)
        stores.append(pltpu.make_async_copy(wind.at[at], out_ref.at[0, at], sems.at[chunk]))
        stores[-1].start()
    for store in stores:
        store.wait()


def xor_groups(bits):
    first = bits % 2
    groups = [(0,)] if first else []
    return groups + [(b, b + 1) for b in range(first, bits, 2)]


def offsets_of(group):
    found = [0]
    for bit in group:
        found = found + [offset | (1 << bit) for offset in found]
    return found[1:]


def exchange(value, axis, count, offset):
    return lax.ppermute(value, axis, [(i, i ^ offset) for i in range(count)])


def sum_all(value, axis, count):
    for group in xor_groups(count.bit_length() - 1):
        received = [exchange(value, axis, count, offset) for offset in offsets_of(group)]
        for other in received:
            value = value + other
    return value


def gather_xor(value, axis, count):
    blocks = value[None]
    for bit in range(count.bit_length() - 1):
        blocks = jnp.concatenate([blocks, exchange(blocks, axis, count, 1 << bit)], axis=0)
    return blocks


def vmem(count):
    return [pl.BlockSpec(memory_space=pltpu.VMEM)] * count


def in_hbm(value):
    return pltpu.with_memory_space_constraint(value, pltpu.HBM)


SMEM = pl.BlockSpec(memory_space=pltpu.SMEM)
HBM = pl.BlockSpec(memory_space=pltpu.HBM)


def on_device(
    slabs,
    crosses,
    velocity,
    shape_weight,
    w_in,
    w_out,
    decay,
    rotor_states,
    slot_of_rotor,
    entry_rotor,
    entry_tile,
    entry_sub,
):
    parts, size_x, size_y, size_z = velocity.shape
    columns = size_x * size_y
    entries = entry_tile.shape[0]
    groups = entries // TILE
    rotors = slot_of_rotor.shape[0]
    subs = shape_weight.shape[0]
    width = w_in.shape[1]
    rows = rotor_states.shape[0]
    tile = entry_tile.reshape(groups, TILE)
    rotor = entry_rotor.reshape(groups, TILE)
    sub = entry_sub.reshape(groups, TILE)

    gathered = gather_xor(rotor_states, "slab", slabs)
    part, west, east, south, north, cells = pl.pallas_call(
        pool_kernel,
        out_shape=(
            jax.ShapeDtypeStruct((rotors, parts * TILE), F32),
            jax.ShapeDtypeStruct((parts, size_y, size_z), BF16),
            jax.ShapeDtypeStruct((parts, size_y, size_z), BF16),
            jax.ShapeDtypeStruct((parts, size_x, size_z), BF16),
            jax.ShapeDtypeStruct((parts, size_x, size_z), BF16),
            jax.ShapeDtypeStruct(velocity.shape, F32),
        ),
        in_specs=[HBM] * 6,
        out_specs=tuple(vmem(6)),
        scratch_shapes=[
            pltpu.VMEM((groups, TILE), jnp.int32),
            pltpu.VMEM((groups, TILE), jnp.int32),
            pltpu.VMEM((groups, TILE), jnp.int32),
            pltpu.SMEM((rotors,), jnp.int32),
            pltpu.VMEM(shape_weight.shape, F32),
            pltpu.VMEM((entries, columns), BF16),
            pltpu.VMEM((entries, parts * TILE), F32),
            pltpu.VMEM((entries, TILE), jnp.int32),
            pltpu.SemaphoreType.DMA((parts,)),
            pltpu.SemaphoreType.DMA((5,)),
        ],
        compiler_params=pltpu.CompilerParams(vmem_limit_bytes=20 << 20),
        cost_estimate=pl.CostEstimate(
            flops=2 * entries * columns * parts * size_z,
            bytes_accessed=velocity.size * 4,
            transcendentals=0,
        ),
        name="pool",
    )(*(in_hbm(value) for value in (tile, rotor, sub, slot_of_rotor, shape_weight, velocity)))

    pooled = sum_all(part, BOTH, slabs * crosses)

    up = lambda count: [(i, i + 1) for i in range(count - 1)]
    down = lambda count: [(i + 1, i) for i in range(count - 1)]
    from_west = lax.ppermute(east, "slab", up(slabs))
    from_east = lax.ppermute(west, "slab", down(slabs))
    from_south = lax.ppermute(north, "cross", up(crosses))
    from_north = lax.ppermute(south, "cross", down(crosses))
    chunks = 4
    keys = subs * rotors
    field, wind, key_hot, place_hot, w_out_here = pl.pallas_call(
        stencil_kernel,
        out_shape=(
            jax.ShapeDtypeStruct(velocity.shape, F32),
            jax.ShapeDtypeStruct(velocity.shape[1:], F32),
            jax.ShapeDtypeStruct((entries, keys), BF16),
            jax.ShapeDtypeStruct((columns, entries), BF16),
            jax.ShapeDtypeStruct(w_out.shape, BF16),
        ),
        in_specs=[SMEM] + vmem(8) + [HBM],
        out_specs=(HBM, *vmem(4)),
        scratch_shapes=[
            pltpu.VMEM((parts - 1, size_x, size_y, size_z), F32),
            pltpu.SemaphoreType.DMA,
            pltpu.SemaphoreType.DMA((chunks,)),
        ],
        compiler_params=pltpu.CompilerParams(vmem_limit_bytes=24 << 20),
        cost_estimate=pl.CostEstimate(
            flops=30 * velocity.size, bytes_accessed=velocity.size * 8, transcendentals=0
        ),
        name="stencil",
    )(slot_of_rotor, tile, rotor, sub, cells, from_west, from_east, from_south, from_north, in_hbm(w_out))

    index = lax.axis_index("slab").astype(jnp.int32).reshape(1)
    return pl.pallas_call(
        rotor_kernel,
        out_shape=(
            jax.ShapeDtypeStruct(velocity.shape, F32),
            jax.ShapeDtypeStruct(rotor_states.shape, F32),
        ),
        in_specs=[SMEM] + vmem(9) + [HBM],
        out_specs=(HBM, pl.BlockSpec(memory_space=pltpu.VMEM)),
        scratch_shapes=[
            pltpu.VMEM((rotors, width), F32),
            pltpu.VMEM((slabs, rows, width), F32),
            pltpu.VMEM((keys, TILE), BF16),
            pltpu.VMEM((size_x, size_y, size_z), F32),
            pltpu.SemaphoreType.DMA((chunks,)),
        ],
        input_output_aliases={10: 0},
        compiler_params=pltpu.CompilerParams(vmem_limit_bytes=24 << 20),
        cost_estimate=pl.CostEstimate(
            flops=4 * entries * columns * size_z, bytes_accessed=w_out.size * 2, transcendentals=0
        ),
        name="rotors",
    )(
        index,
        tile,
        pooled,
        w_in,
        w_out_here,
        decay[None, :],
        gathered,
        wind,
        key_hot,
        place_hot,
        field,
    )


def solution(mesh):
    slabs, crosses = mesh.shape["slab"], mesh.shape["cross"]
    in_specs = (
        P(None, "slab", "cross", None),
        P(),
        P(),
        P(),
        P(),
        P("slab", None),
        P(),
        P(("slab", "cross"), None),
        P(("slab", "cross")),
        P(("slab", "cross")),
    )
    out_specs = (P(None, "slab", "cross", None), P("slab", None))
    return jax.shard_map(
        functools.partial(on_device, slabs, crosses),
        mesh=mesh,
        in_specs=in_specs,
        out_specs=out_specs,
        check_vma=False,
    )
```

```python
import functools

import jax
import jax.numpy as jnp
from jax import lax
from jax.experimental import pallas as pl
from jax.experimental.pallas import tpu as pltpu
from jax.sharding import PartitionSpec as P

TILE = 128

time_step = 0.1
viscosity = 0.3
pool_scale = 1.0 / 64.0
state_step = 0.5
force_scale = 0.5

BOTH = ("slab", "cross")
F32 = jnp.float32
BF16 = jnp.bfloat16


def lanes(rows):
    return lax.broadcasted_iota(jnp.int32, (rows, TILE), 1)


def sublanes(rows):
    return lax.broadcasted_iota(jnp.int32, (rows, TILE), 0)


def as_column(row):
    return jnp.transpose(jnp.broadcast_to(row, (TILE, TILE)))


def hot(mask):
    return jnp.where(mask, 1.0, 0.0).astype(BF16)


def slots_of(rotors, slot_ref):
    slots = jnp.zeros_like(rotors)
    for rotor in range(slot_ref.shape[0]):
        slots = jnp.where(rotors == rotor, slot_ref[rotor], slots)
    return slots


def pool_kernel(
    tile_ref,
    rotor_ref,
    sub_ref,
    slot_ref,
    weight_ref,
    velocity_ref,
    part_ref,
    x_even_ref,
    x_odd_ref,
    y_even_ref,
    y_odd_ref,
    cells,
    tiles,
    rotor_rows,
    sub_rows,
    slot_table,
    weights,
    place_hot,
    gains,
    half_column,
    sems,
    small_sems,
):
    parts, size_x, size_y, size_z = velocity_ref.shape
    columns = size_x * size_y
    halves = size_z // TILE
    groups = tile_ref.shape[0]
    entries = groups * TILE
    rotors = slot_ref.shape[0]
    subs = weight_ref.shape[0]
    small = [
        pltpu.make_async_copy(source, target, small_sems.at[i])
        for i, (source, target) in enumerate(
            (
                (tile_ref, tiles),
                (sub_ref, sub_rows),
                (weight_ref, weights),
                (rotor_ref, rotor_rows),
                (slot_ref, slot_table),
            )
        )
    ]
    copies = [
        pltpu.make_async_copy(velocity_ref.at[c], cells.at[c], sems.at[c]) for c in range(parts)
    ]
    for copy in small + copies:
        copy.start()
    for copy in small:
        copy.wait()
    weight = weights[...]
    high = weight.astype(BF16)
    rest = weight - high.astype(F32)
    middle = rest.astype(BF16)
    low = (rest - middle.astype(F32)).astype(BF16)
    weight_parts = jnp.concatenate([high, middle, low], axis=0)
    sub_hot = []
    place_rows = tiles[...] // halves
    half_rows = tiles[...] % halves
    for group in range(groups):
        half_column[pl.ds(group * TILE, TILE), :] = as_column(half_rows[group : group + 1, :])
        place = as_column(place_rows[group : group + 1, :])
        for block in range(columns // TILE):
            place_hot[pl.ds(group * TILE, TILE), pl.ds(block * TILE, TILE)] = hot(
                place == lanes(TILE) + block * TILE
            )
        sub = as_column(sub_rows[group : group + 1, :])
        wide = jnp.concatenate([sub[:, :subs]] * 3, axis=1)
        index = lax.broadcasted_iota(jnp.int32, (TILE, subs), 1)
        sub_hot.append(hot(wide == jnp.concatenate([index] * 3, axis=1)))
    gains[...] = jnp.dot(
        jnp.concatenate(sub_hot, axis=0), weight_parts, preferred_element_type=F32
    )
    slots = slots_of(rotor_rows[...], slot_table)
    slot_hot = jnp.concatenate(
        [hot(slots[g : g + 1, :] == sublanes(rotors)) for g in range(groups)], axis=1
    )
    half = half_column[...]
    even_x = lax.axis_index("slab") % 2 == 0
    even_y = lax.axis_index("cross") % 2 == 0
    for c in range(parts):
        copies[c].wait()
        flat = cells[c].reshape(columns, size_z).astype(BF16)
        found = jnp.dot(place_hot[...], flat, preferred_element_type=F32)
        sample = found[:, :TILE]
        for h in range(1, halves):
            sample = jnp.where(half == h, found[:, h * TILE : (h + 1) * TILE], sample)
        weighted = sample * gains[:, c * TILE : (c + 1) * TILE]
        high = weighted.astype(BF16)
        rest = weighted - high.astype(F32)
        middle = rest.astype(BF16)
        low = (rest - middle.astype(F32)).astype(BF16)
        sums = jnp.dot(
            slot_hot, jnp.concatenate([high, middle, low], axis=1), preferred_element_type=F32
        )
        part_ref[c * rotors : (c + 1) * rotors, :] = (
            sums[:, 2 * TILE :] + sums[:, TILE : 2 * TILE] + sums[:, :TILE]
        )
        first, last = cells[c, 0].astype(BF16), cells[c, size_x - 1].astype(BF16)
        x_even_ref[c] = jnp.where(even_x, last, first)
        x_odd_ref[c] = jnp.where(even_x, first, last)
        first, last = cells[c, :, 0, :].astype(BF16), cells[c, :, size_y - 1, :].astype(BF16)
        y_even_ref[c] = jnp.where(even_y, last, first)
        y_odd_ref[c] = jnp.where(even_y, first, last)


def pack_rows(target_ref, start, blocks):
    rows, width = blocks[0].shape
    count = rows * len(blocks)
    for j in range(width // TILE):
        for k, block in enumerate(blocks):
            at = start + j * count + k * rows
            target_ref[at : at + rows, :] = block[:, j * TILE : (j + 1) * TILE]


def unpack_rows(source_ref, start, width):
    count = (source_ref.shape[0] - start) // (width // TILE)
    return jnp.concatenate(
        [source_ref[start + j * count : start + (j + 1) * count, :] for j in range(width // TILE)],
        axis=1,
    )


def stencil_kernel(begin, depth, fences, *refs):
    velocity_ref, out_ref = refs[fences], refs[-1]
    parts, size_x, size_y, size_z = velocity_ref.shape
    row = lax.broadcasted_iota(jnp.int32, (size_y, size_z), 0)
    lane = lax.broadcasted_iota(jnp.int32, (size_y, size_z), 1)
    zero = jnp.zeros((size_y, size_z), F32)
    for x in range(begin, begin + depth):
        wind = [velocity_ref[c, x] for c in range(parts)]
        for c in range(parts):
            here = wind[c]
            west = velocity_ref[c, x - 1] if x > 0 else zero
            east = velocity_ref[c, x + 1] if x + 1 < size_x else zero
            south = jnp.where(row == 0, 0.0, pltpu.roll(here, 1, 0))
            north = jnp.where(row == size_y - 1, 0.0, pltpu.roll(here, size_y - 1, 0))
            lower = jnp.where(lane == 0, 0.0, pltpu.roll(here, 1, 1))
            upper = jnp.where(lane == size_z - 1, 0.0, pltpu.roll(here, size_z - 1, 1))
            laplace = east + west + north + south + upper + lower - 6.0 * here
            advect = (
                wind[0] * ((east - west) * 0.5)
                + wind[1] * ((north - south) * 0.5)
                + wind[2] * ((upper - lower) * 0.5)
            )
            out_ref[c, x - begin] = here + time_step * (viscosity * laplace - advect)


def join_kernel(fences, *refs):
    refs, out_ref = refs[fences:-1], refs[-1]
    pooled_refs, state_refs = refs[:-2], refs[-2:]
    rows = pooled_refs[0].shape[0]
    total = pooled_refs[0][...]
    for other in pooled_refs[1:]:
        total = total + other[...]
    out_ref[:rows, :] = total
    even = lax.axis_index("slab") % 2 == 0
    mine, other = state_refs[0][...], state_refs[1][...]
    pack_rows(out_ref, rows, [jnp.where(even, mine, other), jnp.where(even, other, mine)])


def merge_kernel(shift, pooled_rows, width, *refs):
    packed, out_ref = refs[:-1], refs[-1]
    total = packed[0][:pooled_rows, :]
    for other in packed[1:]:
        total = total + other[:pooled_rows, :]
    out_ref[:pooled_rows, :] = total
    pack_rows(out_ref, pooled_rows, in_order(packed, shift, pooled_rows, width))


def in_order(packed, shift, pooled_rows, width):
    count = len(packed)
    mine = (lax.axis_index("slab") >> shift) % count
    blocks = [unpack_rows(ref, pooled_rows, width) for ref in packed]
    ordered = []
    for place in range(count):
        block = blocks[0]
        for k in range(1, count):
            block = jnp.where((mine ^ k) == place, blocks[k], block)
        ordered.append(block)
    return ordered


def add_halo(field, wind, halo, sign):
    return field + halo.astype(F32) * (time_step * (viscosity - sign * 0.5 * wind))


def rotor_kernel(
    packs,
    planes,
    shift,
    slot_ref,
    tile_ref,
    rotor_ref,
    sub_ref,
    w_in_ref,
    w_out_ref,
    decay_ref,
    cells_ref,
    x_even_ref,
    x_odd_ref,
    y_even_ref,
    y_odd_ref,
    *rest,
):
    packed, rest = rest[:packs], rest[packs:]
    field_refs, rest = rest[:planes], rest[planes:]
    out_ref, new_ref, by_slab, source_rows, key_hot, place_hot, field, sems = rest
    slabs, rows, width = by_slab.shape
    rotors = slabs * rows
    parts, size_x, size_y, size_z = cells_ref.shape
    columns = size_x * size_y
    halves = size_z // TILE
    groups = tile_ref.shape[0]
    subs = w_out_ref.shape[1] // TILE
    pooled = packed[0][: parts * rotors, :]
    for other in packed[1:]:
        pooled = pooled + other[: parts * rotors, :]
    pooled = (pooled * pool_scale).astype(BF16)
    pooled = jnp.concatenate([pooled[c * rotors : (c + 1) * rotors] for c in range(parts)], axis=1)
    old = jnp.concatenate(in_order(packed, shift, parts * rotors, width), axis=0)
    drive = jnp.dot(pooled, w_in_ref[...], preferred_element_type=F32)
    new = old + state_step * (drive - decay_ref[...] * old)
    for j in range(slabs):
        by_slab[j] = new[j * rows : (j + 1) * rows, :]
    new_ref[...] = by_slab[lax.axis_index("slab")]
    new_b = new.astype(BF16)

    depth = size_x // planes
    even_x = lax.axis_index("slab") % 2 == 0
    even_y = lax.axis_index("cross") % 2 == 0
    stores = []
    for c in range(parts - 1, -1, -1):
        for k in range(planes):
            field[c, k * depth : (k + 1) * depth] = field_refs[k][c]
        near, far = x_even_ref[c], x_odd_ref[c]
        west, east = jnp.where(even_x, far, near), jnp.where(even_x, near, far)
        wind = cells_ref[0, 0]
        field[c, 0] = add_halo(field[c, 0], wind, west, -1)
        wind = cells_ref[0, size_x - 1]
        field[c, size_x - 1] = add_halo(field[c, size_x - 1], wind, east, 1)
        near, far = y_even_ref[c], y_odd_ref[c]
        south, north = jnp.where(even_y, far, near), jnp.where(even_y, near, far)
        wind = cells_ref[1, :, 0, :]
        field[c, :, 0, :] = add_halo(field[c, :, 0, :], wind, south, -1)
        wind = cells_ref[1, :, size_y - 1, :]
        field[c, :, size_y - 1, :] = add_halo(field[c, :, size_y - 1, :], wind, north, 1)
        if c > 0:
            stores.append(pltpu.make_async_copy(field.at[c], out_ref.at[c], sems.at[c]))
            stores[-1].start()

    slots = slots_of(rotor_ref[...], slot_ref)
    keys = sub_ref[...] * rotors + slots
    places = tile_ref[...] // halves
    half_rows = tile_ref[...] % halves
    for group in range(groups):
        key = as_column(keys[group : group + 1, :])
        at = pl.ds(group * TILE, TILE)
        for block in range(subs * rotors // TILE):
            key_hot[at, pl.ds(block * TILE, TILE)] = hot(key == lanes(TILE) + block * TILE)
        for block in range(columns // TILE):
            place_hot[pl.ds(block * TILE, TILE), at] = hot(
                places[group : group + 1, :] == sublanes(TILE) + block * TILE
            )
    sources = jnp.dot(new_b, w_out_ref[...], preferred_element_type=F32).astype(BF16)
    for sub in range(subs):
        source_rows[sub * rotors : (sub + 1) * rotors, :] = sources[:, sub * TILE : (sub + 1) * TILE]
    taken = jnp.dot(key_hot[...], source_rows[...], preferred_element_type=F32)
    half = jnp.concatenate([as_column(half_rows[g : g + 1, :]) for g in range(groups)], axis=0)
    spread = jnp.concatenate(
        [jnp.where(half == h, taken, 0.0).astype(BF16) for h in range(halves)], axis=1
    )
    chunks = sems.shape[0] - parts
    depth = size_x // chunks
    for chunk in range(chunks):
        at = pl.ds(chunk * depth, depth)
        forcing = jnp.dot(
            place_hot[pl.ds(chunk * depth * size_y, depth * size_y), :],
            spread,
            preferred_element_type=F32,
        )
        field[0, at] = field[0, at] - force_scale * forcing.reshape(depth, size_y, size_z)
        stores.append(
            pltpu.make_async_copy(field.at[0, at], out_ref.at[0, at], sems.at[parts + chunk])
        )
        stores[-1].start()
    for store in stores:
        store.wait()


def bit_groups(bits):
    first = bits % 2
    return ([(0,)] if first else []) + [(b, b + 1) for b in range(first, bits, 2)]


def offsets_of(group):
    found = [0]
    for bit in group:
        found = found + [offset | (1 << bit) for offset in found]
    return found[1:]


def swap(value, axis, count, offset):
    return lax.ppermute(value, axis, [(i, i ^ offset) for i in range(count)])


def swap_pairs(value, axis, count, first):
    pairs = [(i, i + 1) for i in range(first, count - 1, 2)]
    return lax.ppermute(value, axis, pairs + [(j, i) for i, j in pairs])


def vmem(count):
    return [pl.BlockSpec(memory_space=pltpu.VMEM)] * count


def in_hbm(value):
    return pltpu.with_memory_space_constraint(value, pltpu.HBM)


SMEM = pl.BlockSpec(memory_space=pltpu.SMEM)
HBM = pl.BlockSpec(memory_space=pltpu.HBM)
ANY = pl.BlockSpec(memory_space=pl.ANY)


def pool(tile, rotor, sub, slot_of_rotor, shape_weight, velocity):
    parts, size_x, size_y, size_z = velocity.shape
    columns = size_x * size_y
    groups = tile.shape[0]
    entries = groups * TILE
    rotors = slot_of_rotor.shape[0]
    return pl.pallas_call(
        pool_kernel,
        out_shape=(
            jax.ShapeDtypeStruct((parts * rotors, TILE), F32),
            jax.ShapeDtypeStruct((parts, size_y, size_z), BF16),
            jax.ShapeDtypeStruct((parts, size_y, size_z), BF16),
            jax.ShapeDtypeStruct((parts, size_x, size_z), BF16),
            jax.ShapeDtypeStruct((parts, size_x, size_z), BF16),
            jax.ShapeDtypeStruct(velocity.shape, F32),
        ),
        in_specs=[HBM] * 6,
        out_specs=tuple(vmem(6)),
        scratch_shapes=[
            pltpu.VMEM((groups, TILE), jnp.int32),
            pltpu.VMEM((groups, TILE), jnp.int32),
            pltpu.VMEM((groups, TILE), jnp.int32),
            pltpu.SMEM((rotors,), jnp.int32),
            pltpu.VMEM(shape_weight.shape, F32),
            pltpu.VMEM((entries, columns), BF16),
            pltpu.VMEM((entries, parts * TILE), F32),
            pltpu.VMEM((entries, TILE), jnp.int32),
            pltpu.SemaphoreType.DMA((parts,)),
            pltpu.SemaphoreType.DMA((5,)),
        ],
        compiler_params=pltpu.CompilerParams(vmem_limit_bytes=12 << 20),
        cost_estimate=pl.CostEstimate(
            flops=2 * entries * columns * parts * size_z,
            bytes_accessed=velocity.size * 4,
            transcendentals=0,
        ),
        name="pool",
    )(*(in_hbm(value) for value in (tile, rotor, sub, slot_of_rotor, shape_weight, velocity)))


def stencil(begin, depth, fences, velocity):
    parts, size_x, size_y, size_z = velocity.shape
    return pl.pallas_call(
        functools.partial(stencil_kernel, begin, depth, len(fences)),
        out_shape=jax.ShapeDtypeStruct((parts, depth, size_y, size_z), F32),
        in_specs=[ANY] * len(fences) + vmem(1),
        out_specs=vmem(1)[0],
        compiler_params=pltpu.CompilerParams(vmem_limit_bytes=4 << 20),
        cost_estimate=pl.CostEstimate(
            flops=1000 * velocity.size * depth // size_x,
            bytes_accessed=8 * velocity.size * depth // size_x,
            transcendentals=0,
        ),
        name="stencil",
    )(*fences, velocity)


def join(fences, pooled, states):
    rows = pooled[0].shape[0] + 2 * states[0].size // TILE
    return pl.pallas_call(
        functools.partial(join_kernel, len(fences)),
        out_shape=jax.ShapeDtypeStruct((rows, TILE), F32),
        in_specs=[ANY] * len(fences) + vmem(len(pooled) + 2),
        out_specs=vmem(1)[0],
        compiler_params=pltpu.CompilerParams(vmem_limit_bytes=4 << 20),
        name="join",
    )(*fences, *pooled, *states)


def merge(shift, pooled_rows, width, packed):
    rows = pooled_rows + len(packed) * (packed[0].shape[0] - pooled_rows)
    return pl.pallas_call(
        functools.partial(merge_kernel, shift, pooled_rows, width),
        out_shape=jax.ShapeDtypeStruct((rows, TILE), F32),
        in_specs=vmem(len(packed)),
        out_specs=vmem(1)[0],
        compiler_params=pltpu.CompilerParams(vmem_limit_bytes=4 << 20),
        name="merge",
    )(*packed)


def rotors_step(
    slabs, shift, slot_of_rotor, tile, rotor, sub, w_in, w_out, decay, velocity, halos, packed, fields
):
    width = w_in.shape[1]
    rows = slot_of_rotor.shape[0] // slabs
    parts, size_x, size_y, size_z = velocity.shape
    columns = size_x * size_y
    entries = tile.shape[0] * TILE
    keys = w_out.shape[1] // TILE * slabs * rows
    chunks = 4
    return pl.pallas_call(
        functools.partial(rotor_kernel, len(packed), len(fields), shift),
        out_shape=(
            jax.ShapeDtypeStruct(velocity.shape, F32),
            jax.ShapeDtypeStruct((rows, width), F32),
        ),
        in_specs=[SMEM] + vmem(11 + len(packed) + len(fields)),
        out_specs=(HBM, vmem(1)[0]),
        scratch_shapes=[
            pltpu.VMEM((slabs, rows, width), F32),
            pltpu.VMEM((keys, TILE), BF16),
            pltpu.VMEM((entries, keys), BF16),
            pltpu.VMEM((columns, entries), BF16),
            pltpu.VMEM(velocity.shape, F32),
            pltpu.SemaphoreType.DMA((parts + chunks,)),
        ],
        compiler_params=pltpu.CompilerParams(vmem_limit_bytes=16 << 20),
        cost_estimate=pl.CostEstimate(
            flops=4 * entries * columns * size_z, bytes_accessed=w_out.size * 2, transcendentals=0
        ),
        name="rotors",
    )(slot_of_rotor, tile, rotor, sub, w_in, w_out, decay, velocity, *halos, *packed, *fields)


def on_device(
    slabs,
    crosses,
    velocity,
    shape_weight,
    w_in,
    w_out,
    decay,
    rotor_states,
    slot_of_rotor,
    entry_rotor,
    entry_tile,
    entry_sub,
):
    entries = entry_tile.shape[0]
    width = w_in.shape[1]
    count = slabs * crosses
    tile = entry_tile.reshape(entries // TILE, TILE)
    rotor = entry_rotor.reshape(entries // TILE, TILE)
    sub = entry_sub.reshape(entries // TILE, TILE)

    states = [rotor_states, swap(rotor_states, "slab", slabs, 1)]
    part, x_even, x_odd, y_even, y_odd, cells = pool(
        tile, rotor, sub, slot_of_rotor, shape_weight, velocity
    )
    pooled_rows = part.shape[0]
    groups = bit_groups(count.bit_length() - 1)
    cross_bits = crosses.bit_length() - 1
    planes = 2
    depth = velocity.shape[1] // planes

    def exchanged(value, group):
        return [value] + [swap(value, BOTH, count, offset) for offset in offsets_of(group)]

    y_even = swap_pairs(y_even, "cross", crosses, 0)
    pooled = exchanged(part, groups[0])
    total = pooled[0] + pooled[1]
    x_even = swap_pairs(x_even, "slab", slabs, 0)
    pooled = exchanged(total, groups[1])
    fields = [stencil(0, depth, (total, x_even, y_even, states[1]), cells)]
    packed = join(fields, pooled, states)
    for group in groups[2:-1]:
        packed = merge(group[0] - cross_bits, pooled_rows, width, exchanged(packed, group))
    y_odd = swap_pairs(y_odd, "cross", crosses, 1)
    x_odd = swap_pairs(x_odd, "slab", slabs, 1)
    fields.append(stencil(depth, depth, (packed,), cells))
    packed = exchanged(packed, groups[-1])

    return rotors_step(
        slabs,
        groups[-1][0] - cross_bits,
        slot_of_rotor,
        tile,
        rotor,
        sub,
        w_in,
        w_out,
        decay[None, :],
        cells,
        (x_even, x_odd, y_even, y_odd),
        packed,
        fields,
    )


def solution(mesh):
    slabs, crosses = mesh.shape["slab"], mesh.shape["cross"]
    in_specs = (
        P(None, "slab", "cross", None),
        P(),
        P(),
        P(),
        P(),
        P("slab", None),
        P(),
        P(("slab", "cross"), None),
        P(("slab", "cross")),
        P(("slab", "cross")),
    )
    out_specs = (P(None, "slab", "cross", None), P("slab", None))
    return jax.shard_map(
        functools.partial(on_device, slabs, crosses),
        mesh=mesh,
        in_specs=in_specs,
        out_specs=out_specs,
        check_vma=False,
    )
```

```python
import functools

import jax
import jax.numpy as jnp
from jax import lax
from jax.experimental import pallas as pl
from jax.experimental.pallas import tpu as pltpu
from jax.sharding import PartitionSpec as P

TILE = 128

time_step = 0.1
viscosity = 0.3
pool_scale = 1.0 / 64.0
state_step = 0.5
force_scale = 0.5

BOTH = ("slab", "cross")
F32 = jnp.float32
BF16 = jnp.bfloat16


def lanes(rows):
    return lax.broadcasted_iota(jnp.int32, (rows, TILE), 1)


def sublanes(rows):
    return lax.broadcasted_iota(jnp.int32, (rows, TILE), 0)


def as_column(row):
    return jnp.transpose(jnp.broadcast_to(row, (TILE, TILE)))


def hot(mask):
    return jnp.where(mask, 1.0, 0.0).astype(BF16)


def slots_of(rotors, slot_ref):
    slots = jnp.zeros_like(rotors)
    for rotor in range(slot_ref.shape[0]):
        slots = jnp.where(rotors == rotor, slot_ref[rotor], slots)
    return slots


def load_kernel(
    tile_ref,
    rotor_ref,
    sub_ref,
    slot_ref,
    weight_ref,
    velocity_ref,
    x_odd_ref,
    cells,
    place_hot,
    gains,
    half_column,
    slot_hot,
    tiles,
    rotor_rows,
    sub_rows,
    slot_table,
    weights,
    sems,
    small_sems,
):
    parts, size_x, size_y, size_z = velocity_ref.shape
    columns = size_x * size_y
    halves = size_z // TILE
    groups = tile_ref.shape[0]
    rotors = slot_ref.shape[0]
    subs = weight_ref.shape[0]
    small = [
        pltpu.make_async_copy(source, target, small_sems.at[i])
        for i, (source, target) in enumerate(
            (
                (tile_ref, tiles),
                (sub_ref, sub_rows),
                (weight_ref, weights),
                (rotor_ref, rotor_rows),
                (slot_ref, slot_table),
            )
        )
    ]
    copies = [
        pltpu.make_async_copy(velocity_ref.at[c], cells.at[c], sems.at[c]) for c in range(parts)
    ]
    for copy in small + copies:
        copy.start()
    for copy in small:
        copy.wait()
    weight = weights[...]
    high = weight.astype(BF16)
    rest = weight - high.astype(F32)
    middle = rest.astype(BF16)
    low = (rest - middle.astype(F32)).astype(BF16)
    weight_parts = jnp.concatenate([high, middle, low], axis=0)
    sub_hot = []
    place_rows = tiles[...] // halves
    half_rows = tiles[...] % halves
    for group in range(groups):
        half_column[pl.ds(group * TILE, TILE), :] = as_column(half_rows[group : group + 1, :])
        place = as_column(place_rows[group : group + 1, :])
        for block in range(columns // TILE):
            place_hot[pl.ds(group * TILE, TILE), pl.ds(block * TILE, TILE)] = hot(
                place == lanes(TILE) + block * TILE
            )
        sub = as_column(sub_rows[group : group + 1, :])
        wide = jnp.concatenate([sub[:, :subs]] * 3, axis=1)
        index = lax.broadcasted_iota(jnp.int32, (TILE, subs), 1)
        sub_hot.append(hot(wide == jnp.concatenate([index] * 3, axis=1)))
    gains[...] = jnp.dot(
        jnp.concatenate(sub_hot, axis=0), weight_parts, preferred_element_type=F32
    )
    slots = slots_of(rotor_rows[...], slot_table)
    slot_hot[...] = jnp.concatenate(
        [hot(slots[g : g + 1, :] == sublanes(rotors)) for g in range(groups)], axis=1
    )
    even_x = lax.axis_index("slab") % 2 == 0
    for c in range(parts):
        copies[c].wait()
        first, last = cells[c, 0], cells[c, size_x - 1]
        x_odd_ref[c] = jnp.where(even_x, first, last).astype(BF16)


def first_half(bits):
    index = lax.axis_index("slab") * lax.axis_size("cross") + lax.axis_index("cross")
    parity = index
    for bit in range(1, bits):
        parity = parity ^ (index >> bit)
    return parity % 2 == 0


def pool_kernel(
    bits,
    cells,
    place_hot,
    gains,
    half_column,
    slot_hot,
    keep_ref,
    send_ref,
    y_even_ref,
    y_odd_ref,
    total,
):
    parts, size_x, size_y, size_z = cells.shape
    columns = size_x * size_y
    halves = size_z // TILE
    rotors = slot_hot.shape[0]
    half = half_column[...]
    even_y = lax.axis_index("cross") % 2 == 0
    for c in range(parts):
        flat = cells[c].reshape(columns, size_z).astype(BF16)
        found = jnp.dot(place_hot[...], flat, preferred_element_type=F32)
        sample = found[:, :TILE]
        for h in range(1, halves):
            sample = jnp.where(half == h, found[:, h * TILE : (h + 1) * TILE], sample)
        weighted = sample * gains[:, c * TILE : (c + 1) * TILE]
        high = weighted.astype(BF16)
        rest = weighted - high.astype(F32)
        middle = rest.astype(BF16)
        low = (rest - middle.astype(F32)).astype(BF16)
        sums = jnp.dot(
            slot_hot[...],
            jnp.concatenate([high, middle, low], axis=1),
            preferred_element_type=F32,
        )
        total[c * rotors : (c + 1) * rotors, :] = (
            sums[:, 2 * TILE :] + sums[:, TILE : 2 * TILE] + sums[:, :TILE]
        )
        first, last = cells[c, :, 0, :], cells[c, :, size_y - 1, :]
        y_even_ref[c] = jnp.where(even_y, last, first).astype(BF16)
        y_odd_ref[c] = jnp.where(even_y, first, last).astype(BF16)
    rows = keep_ref.shape[0]
    first, second = total[:rows, :], total[rows:, :]
    keep_ref[...] = jnp.where(first_half(bits), first, second)
    send_ref[...] = jnp.where(first_half(bits), second, first)


def pack_rows(target_ref, start, blocks):
    rows, width = blocks[0].shape
    count = rows * len(blocks)
    for j in range(width // TILE):
        for k, block in enumerate(blocks):
            at = start + j * count + k * rows
            target_ref[at : at + rows, :] = block[:, j * TILE : (j + 1) * TILE]


def unpack_rows(source_ref, start, width):
    count = (source_ref.shape[0] - start) // (width // TILE)
    return jnp.concatenate(
        [source_ref[start + j * count : start + (j + 1) * count, :] for j in range(width // TILE)],
        axis=1,
    )


def stencil_kernel(begin, depth, fences, slabs, crosses, *refs):
    refs, out_ref = refs[fences:-1], refs[-1]
    velocity_ref, x_even_ref, x_odd_ref, y_even_ref, y_odd_ref = refs
    parts, size_x, size_y, size_z = velocity_ref.shape
    row = lax.broadcasted_iota(jnp.int32, (size_y, size_z), 0)
    lane = lax.broadcasted_iota(jnp.int32, (size_y, size_z), 1)
    slab, cross = lax.axis_index("slab"), lax.axis_index("cross")
    even_x, even_y = slab % 2 == 0, cross % 2 == 0
    inner_x = jnp.logical_and(slab > 0, slab < slabs - 1)
    inner_y = jnp.logical_and(cross > 0, cross < crosses - 1)
    for c in range(parts):
        near = y_even_ref[c].astype(F32)
        far = jnp.where(inner_y, y_odd_ref[c].astype(F32), 0.0)
        souths, norths = jnp.where(even_y, far, near), jnp.where(even_y, near, far)
        for x in range(begin, begin + depth):
            wind = [velocity_ref[d, x] for d in range(parts)]
            here = wind[c]
            if x > 0:
                west = velocity_ref[c, x - 1]
            else:
                far_x = jnp.where(inner_x, x_odd_ref[c].astype(F32), 0.0)
                west = jnp.where(even_x, far_x, x_even_ref[c].astype(F32))
            if x + 1 < size_x:
                east = velocity_ref[c, x + 1]
            else:
                far_x = jnp.where(inner_x, x_odd_ref[c].astype(F32), 0.0)
                east = jnp.where(even_x, x_even_ref[c].astype(F32), far_x)
            south = jnp.where(row == 0, souths[x : x + 1, :], pltpu.roll(here, 1, 0))
            north = jnp.where(
                row == size_y - 1, norths[x : x + 1, :], pltpu.roll(here, size_y - 1, 0)
            )
            lower = jnp.where(lane == 0, 0.0, pltpu.roll(here, 1, 1))
            upper = jnp.where(lane == size_z - 1, 0.0, pltpu.roll(here, size_z - 1, 1))
            laplace = east + west + north + south + upper + lower - 6.0 * here
            advect = (
                wind[0] * ((east - west) * 0.5)
                + wind[1] * ((north - south) * 0.5)
                + wind[2] * ((upper - lower) * 0.5)
            )
            out_ref[c, x - begin] = here + time_step * (viscosity * laplace - advect)


def key_kernel(fence_ref, cells, slot_ref, rotor_ref, sub_ref, key_ref, x_even_ref):
    del fence_ref
    even_x = lax.axis_index("slab") % 2 == 0
    for c in range(cells.shape[0]):
        face = jnp.where(even_x, cells[c, cells.shape[1] - 1], cells[c, 0])
        x_even_ref[c] = face.astype(BF16)
    rotors = slot_ref.shape[0]
    keys = sub_ref[...] * rotors + slots_of(rotor_ref[...], slot_ref)
    for group in range(keys.shape[0]):
        key = as_column(keys[group : group + 1, :])
        for block in range(key_ref.shape[1] // TILE):
            key_ref[pl.ds(group * TILE, TILE), pl.ds(block * TILE, TILE)] = hot(
                key == lanes(TILE) + block * TILE
            )


def place_kernel(halves, fence_ref, tile_ref, place_ref):
    del fence_ref
    places = tile_ref[...] // halves
    for group in range(places.shape[0]):
        for block in range(place_ref.shape[0] // TILE):
            place_ref[pl.ds(block * TILE, TILE), pl.ds(group * TILE, TILE)] = hot(
                places[group : group + 1, :] == sublanes(TILE) + block * TILE
            )


def join_kernel(bits, fences, *refs):
    keep_ref, other_ref, states_ref, out_ref = refs[fences:]
    rows = keep_ref.shape[0]
    out_ref[:rows, :] = keep_ref[...] + other_ref[...]
    half = states_ref.shape[1] // 2
    pack_rows(
        out_ref, rows, [jnp.where(first_half(bits), states_ref[:, :half], states_ref[:, half:])]
    )


def merge_kernel(fences, shift, rows, width, pooled_rows, *refs):
    mine_ref, other_ref, out_ref = refs[fences:]
    out_ref[:pooled_rows, :] = mine_ref[:pooled_rows, :] + other_ref[:pooled_rows, :]
    if shift is None:
        out_ref[pooled_rows:, :] = mine_ref[pooled_rows:, :]
        return
    first = (lax.axis_index("slab") >> shift) % 2 == 0
    mine, other = [unpack_rows(ref, pooled_rows, width) for ref in (mine_ref, other_ref)]
    low, high = jnp.where(first, mine, other), jnp.where(first, other, mine)
    pieces = []
    for at in range(0, low.shape[0], rows):
        pieces += [low[at : at + rows], high[at : at + rows]]
    pack_rows(out_ref, pooled_rows, pieces)


def rotor_kernel(
    bits,
    planes,
    tile_ref,
    w_in_ref,
    w_out_ref,
    decay_ref,
    key_hot,
    place_hot,
    keep_ref,
    other_ref,
    *rest,
):
    field_refs, rest = rest[:planes], rest[planes:]
    out_ref, new_ref, by_slab, source_rows, wind, sems = rest
    slabs, rows, width = by_slab.shape
    rotors = slabs * rows
    size_x, size_y, size_z = wind.shape
    parts = w_in_ref.shape[0] // TILE
    halves = size_z // TILE
    groups = tile_ref.shape[0]
    subs = w_out_ref.shape[1] // TILE
    depth = size_x // planes
    stores = []
    for k in range(planes):
        for c in range(1, parts):
            stores.append(
                pltpu.make_async_copy(
                    field_refs[k].at[c],
                    out_ref.at[c, pl.ds(k * depth, depth)],
                    sems.at[k * (parts - 1) + c - 1],
                )
            )
            stores[-1].start()
    split = parts * rotors // 2
    first = first_half(bits)
    keep, other = keep_ref[:split, :], other_ref[:split, :]
    pooled = jnp.concatenate(
        [jnp.where(first, keep, other), jnp.where(first, other, keep)], axis=0
    )
    pooled = (pooled * pool_scale).astype(BF16)
    pooled = jnp.concatenate([pooled[c * rotors : (c + 1) * rotors] for c in range(parts)], axis=1)
    keep, other = [unpack_rows(ref, split, width // 2) for ref in (keep_ref, other_ref)]
    old = jnp.concatenate(
        [jnp.where(first, keep, other), jnp.where(first, other, keep)], axis=1
    )
    drive = jnp.dot(pooled, w_in_ref[...], preferred_element_type=F32)
    new = old + state_step * (drive - decay_ref[...] * old)
    for j in range(slabs):
        by_slab[j] = new[j * rows : (j + 1) * rows, :]
    new_ref[...] = by_slab[lax.axis_index("slab")]
    new_b = new.astype(BF16)

    half_rows = tile_ref[...] % halves
    sources = jnp.dot(new_b, w_out_ref[...], preferred_element_type=F32).astype(BF16)
    for sub in range(subs):
        source_rows[sub * rotors : (sub + 1) * rotors, :] = sources[:, sub * TILE : (sub + 1) * TILE]
    taken = jnp.dot(key_hot[...], source_rows[...], preferred_element_type=F32)
    half = jnp.concatenate([as_column(half_rows[g : g + 1, :]) for g in range(groups)], axis=0)
    spread = jnp.concatenate(
        [jnp.where(half == h, taken, 0.0).astype(BF16) for h in range(halves)], axis=1
    )
    for k in range(planes):
        forcing = jnp.dot(
            place_hot[pl.ds(k * depth * size_y, depth * size_y), :],
            spread,
            preferred_element_type=F32,
        )
        at = pl.ds(k * depth, depth)
        wind[at] = field_refs[k][0] - force_scale * forcing.reshape(depth, size_y, size_z)
        stores.append(
            pltpu.make_async_copy(wind.at[at], out_ref.at[0, at], sems.at[planes * (parts - 1) + k])
        )
        stores[-1].start()
    for store in stores:
        store.wait()


def swap(value, axis, count, offset):
    return lax.ppermute(value, axis, [(i, i ^ offset) for i in range(count)])


def swap_pairs(value, axis, count, first):
    pairs = [(i, (i + 1) % count) for i in range(first, count, 2)]
    return lax.ppermute(value, axis, pairs + [(j, i) for i, j in pairs])


def vmem(count):
    return [pl.BlockSpec(memory_space=pltpu.VMEM)] * count


def in_hbm(value):
    return pltpu.with_memory_space_constraint(value, pltpu.HBM)


SMEM = pl.BlockSpec(memory_space=pltpu.SMEM)
HBM = pl.BlockSpec(memory_space=pltpu.HBM)
ANY = pl.BlockSpec(memory_space=pl.ANY)


def load(tile, rotor, sub, slot_of_rotor, shape_weight, velocity):
    parts, size_x, size_y, size_z = velocity.shape
    columns = size_x * size_y
    groups = tile.shape[0]
    entries = groups * TILE
    rotors = slot_of_rotor.shape[0]
    return pl.pallas_call(
        load_kernel,
        out_shape=(
            jax.ShapeDtypeStruct((parts, size_y, size_z), BF16),
            jax.ShapeDtypeStruct(velocity.shape, F32),
            jax.ShapeDtypeStruct((entries, columns), BF16),
            jax.ShapeDtypeStruct((entries, parts * TILE), F32),
            jax.ShapeDtypeStruct((entries, TILE), jnp.int32),
            jax.ShapeDtypeStruct((rotors, entries), BF16),
        ),
        in_specs=[HBM] * 6,
        out_specs=tuple(vmem(6)),
        scratch_shapes=[
            pltpu.VMEM((groups, TILE), jnp.int32),
            pltpu.VMEM((groups, TILE), jnp.int32),
            pltpu.VMEM((groups, TILE), jnp.int32),
            pltpu.SMEM((rotors,), jnp.int32),
            pltpu.VMEM(shape_weight.shape, F32),
            pltpu.SemaphoreType.DMA((parts,)),
            pltpu.SemaphoreType.DMA((5,)),
        ],
        compiler_params=pltpu.CompilerParams(vmem_limit_bytes=8 << 20),
        cost_estimate=pl.CostEstimate(
            flops=2 * entries * columns * size_z,
            bytes_accessed=velocity.size * 4,
            transcendentals=0,
        ),
        name="load",
    )(*(in_hbm(value) for value in (tile, rotor, sub, slot_of_rotor, shape_weight, velocity)))


def pool(bits, cells, place_hot, gains, half_column, slot_hot):
    parts, size_x, size_y, size_z = cells.shape
    rows = parts * slot_hot.shape[0]
    part = jax.ShapeDtypeStruct((rows // 2, TILE), F32)
    return pl.pallas_call(
        functools.partial(pool_kernel, bits),
        out_shape=(
            part,
            part,
            jax.ShapeDtypeStruct((parts, size_x, size_z), BF16),
            jax.ShapeDtypeStruct((parts, size_x, size_z), BF16),
        ),
        in_specs=vmem(5),
        out_specs=tuple(vmem(4)),
        scratch_shapes=[pltpu.VMEM((rows, TILE), F32)],
        compiler_params=pltpu.CompilerParams(vmem_limit_bytes=8 << 20),
        cost_estimate=pl.CostEstimate(
            flops=2 * place_hot.size * parts * size_z, bytes_accessed=cells.size * 4, transcendentals=0
        ),
        name="pool",
    )(cells, place_hot, gains, half_column, slot_hot)


def stencil(begin, depth, fences, slabs, crosses, velocity, halos):
    parts, size_x, size_y, size_z = velocity.shape
    return pl.pallas_call(
        functools.partial(stencil_kernel, begin, depth, len(fences), slabs, crosses),
        out_shape=jax.ShapeDtypeStruct((parts, depth, size_y, size_z), F32),
        in_specs=[ANY] * len(fences) + vmem(5),
        out_specs=vmem(1)[0],
        compiler_params=pltpu.CompilerParams(vmem_limit_bytes=4 << 20),
        cost_estimate=pl.CostEstimate(
            flops=1000 * velocity.size * depth // size_x,
            bytes_accessed=8 * velocity.size * depth // size_x,
            transcendentals=0,
        ),
        name="stencil",
    )(*fences, velocity, *halos)


def key_matrix(fence, cells, slot_of_rotor, rotor, sub, keys):
    parts, _, size_y, size_z = cells.shape
    entries = rotor.shape[0] * TILE
    return pl.pallas_call(
        key_kernel,
        out_shape=(
            jax.ShapeDtypeStruct((entries, keys), BF16),
            jax.ShapeDtypeStruct((parts, size_y, size_z), BF16),
        ),
        in_specs=[ANY] + vmem(1) + [SMEM] + vmem(2),
        out_specs=tuple(vmem(2)),
        compiler_params=pltpu.CompilerParams(vmem_limit_bytes=4 << 20),
        cost_estimate=pl.CostEstimate(
            flops=1000 * entries * keys, bytes_accessed=2 * entries * keys, transcendentals=0
        ),
        name="keys",
    )(fence, cells, slot_of_rotor, rotor, sub)


def place_matrix(fence, tile, columns, halves):
    entries = tile.shape[0] * TILE
    return pl.pallas_call(
        functools.partial(place_kernel, halves),
        out_shape=jax.ShapeDtypeStruct((columns, entries), BF16),
        in_specs=[ANY] + vmem(1),
        out_specs=vmem(1)[0],
        compiler_params=pltpu.CompilerParams(vmem_limit_bytes=4 << 20),
        cost_estimate=pl.CostEstimate(
            flops=1000 * entries * columns, bytes_accessed=2 * entries * columns, transcendentals=0
        ),
        name="places",
    )(fence, tile)


def join(bits, fences, keep, other, states):
    rows = keep.shape[0] + states.size // 2 // TILE
    return pl.pallas_call(
        functools.partial(join_kernel, bits, len(fences)),
        out_shape=jax.ShapeDtypeStruct((rows, TILE), F32),
        in_specs=[ANY] * len(fences) + vmem(3),
        out_specs=vmem(1)[0],
        compiler_params=pltpu.CompilerParams(vmem_limit_bytes=4 << 20),
        name="join",
    )(*fences, keep, other, states)


def merge(fences, shift, rows, width, pooled_rows, mine, other):
    total = mine.shape[0] + (other.shape[0] - pooled_rows if shift is not None else 0)
    return pl.pallas_call(
        functools.partial(merge_kernel, len(fences), shift, rows, width, pooled_rows),
        out_shape=jax.ShapeDtypeStruct((total, TILE), F32),
        in_specs=[ANY] * len(fences) + vmem(2),
        out_specs=vmem(1)[0],
        compiler_params=pltpu.CompilerParams(vmem_limit_bytes=4 << 20),
        name="merge",
    )(*fences, mine, other)


def rotors_step(slabs, bits, tile, w_in, w_out, decay, key_hot, place_hot, keep, other, fields):
    width = w_in.shape[1]
    planes = len(fields)
    parts, depth, size_y, size_z = fields[0].shape
    size_x = planes * depth
    entries, keys = key_hot.shape
    rows = keys // (w_out.shape[1] // TILE) // slabs
    return pl.pallas_call(
        functools.partial(rotor_kernel, bits, planes),
        out_shape=(
            jax.ShapeDtypeStruct((parts, size_x, size_y, size_z), F32),
            jax.ShapeDtypeStruct((rows, width), F32),
        ),
        in_specs=vmem(8 + planes),
        out_specs=(HBM, vmem(1)[0]),
        scratch_shapes=[
            pltpu.VMEM((slabs, rows, width), F32),
            pltpu.VMEM((keys, TILE), BF16),
            pltpu.VMEM((size_x, size_y, size_z), F32),
            pltpu.SemaphoreType.DMA((planes * parts,)),
        ],
        compiler_params=pltpu.CompilerParams(vmem_limit_bytes=10 << 20),
        cost_estimate=pl.CostEstimate(
            flops=4 * place_hot.size * size_z, bytes_accessed=w_out.size * 2, transcendentals=0
        ),
        name="rotors",
    )(tile, w_in, w_out, decay, key_hot, place_hot, keep, other, *fields)


def on_device(
    slabs,
    crosses,
    velocity,
    shape_weight,
    w_in,
    w_out,
    decay,
    rotor_states,
    slot_of_rotor,
    entry_rotor,
    entry_tile,
    entry_sub,
):
    size_x, size_y, size_z = velocity.shape[1:]
    entries = entry_tile.shape[0]
    width = w_in.shape[1]
    count = slabs * crosses
    tile = entry_tile.reshape(entries // TILE, TILE)
    rotor = entry_rotor.reshape(entries // TILE, TILE)
    sub = entry_sub.reshape(entries // TILE, TILE)

    bits = count.bit_length() - 1
    x_odd, cells, *loaded = load(tile, rotor, sub, slot_of_rotor, shape_weight, velocity)
    x_odd = swap_pairs(x_odd, "slab", slabs, 1)
    keep, send, y_even, y_odd = pool(bits, cells, *loaded)
    y_even = swap_pairs(y_even, "cross", crosses, 0)
    y_odd = swap_pairs(y_odd, "cross", crosses, 1)
    pooled_rows = keep.shape[0]

    planes = 2
    depth = size_x // planes
    halos = [None, x_odd, y_even, y_odd]

    def make_keys(fence):
        made, face = key_matrix(
            fence,
            cells,
            slot_of_rotor,
            rotor,
            sub,
            w_out.shape[1] // TILE * slot_of_rotor.shape[0],
        )
        halos[0] = swap_pairs(face, "slab", slabs, 0)
        return made

    def make_places(fence):
        return place_matrix(fence, tile, size_x * size_y, size_z // TILE)

    def make_field(k, fence):
        return stencil(k * depth, depth, (fence,), slabs, crosses, cells, halos)

    work = [make_keys, make_places] + [functools.partial(make_field, k) for k in range(planes)]
    done = []
    packed = join(bits, (x_odd,), keep, swap(send, BOTH, count, 1), rotor_states)
    steps = range(bits - 1, 0, -1)
    for bit in steps:
        beside = 1 if bit > steps[-1] else len(work) - len(done)
        made = [item(packed) for item in work[len(done) : len(done) + beside]]
        done += made
        if 1 << bit >= crosses:
            other, shift = packed, bit - (crosses.bit_length() - 1)
        else:
            other, shift = packed[:pooled_rows], None
        other = swap(other, BOTH, count, 1 << bit | 1)
        packed = merge(made, shift, rotor_states.shape[0], width // 2, pooled_rows, packed, other)
    other = swap(packed, BOTH, count, 1)
    key_hot, place_hot, *fields = done
    return rotors_step(
        slabs, bits, tile, w_in, w_out, decay[None, :], key_hot, place_hot, packed, other, fields
    )


def solution(mesh):
    slabs, crosses = mesh.shape["slab"], mesh.shape["cross"]
    in_specs = (
        P(None, "slab", "cross", None),
        P(),
        P(),
        P(),
        P(),
        P("slab", None),
        P(),
        P(("slab", "cross"), None),
        P(("slab", "cross")),
        P(("slab", "cross")),
    )
    out_specs = (P(None, "slab", "cross", None), P("slab", None))
    return jax.shard_map(
        functools.partial(on_device, slabs, crosses),
        mesh=mesh,
        in_specs=in_specs,
        out_specs=out_specs,
        check_vma=False,
    )
```

```python
import functools

import jax
import jax.numpy as jnp
from jax import lax
from jax.experimental import pallas as pl
from jax.experimental.pallas import tpu as pltpu
from jax.sharding import PartitionSpec as P

TILE = 128

time_step = 0.1
viscosity = 0.3
pool_scale = 1.0 / 64.0
state_step = 0.5
force_scale = 0.5

BOTH = ("slab", "cross")
F32 = jnp.float32
BF16 = jnp.bfloat16


def lanes(rows):
    return lax.broadcasted_iota(jnp.int32, (rows, TILE), 1)


def sublanes(rows):
    return lax.broadcasted_iota(jnp.int32, (rows, TILE), 0)


def as_column(row):
    return jnp.transpose(jnp.broadcast_to(row, (TILE, TILE)))


def hot(mask):
    return jnp.where(mask, 1.0, 0.0).astype(BF16)


def slots_of(rotors, slot_ref):
    slots = jnp.zeros_like(rotors)
    for rotor in range(slot_ref.shape[0]):
        slots = jnp.where(rotors == rotor, slot_ref[rotor], slots)
    return slots


def load_kernel(
    tile_ref,
    rotor_ref,
    sub_ref,
    slot_ref,
    weight_ref,
    velocity_ref,
    x_odd_ref,
    cells,
    place_hot,
    gains,
    half_column,
    slot_hot,
    tiles,
    rotor_rows,
    sub_rows,
    slot_table,
    weights,
    sems,
    small_sems,
):
    parts, size_x, size_y, size_z = velocity_ref.shape
    columns = size_x * size_y
    halves = size_z // TILE
    groups = tile_ref.shape[0]
    rotors = slot_ref.shape[0]
    subs = weight_ref.shape[0]
    small = [
        pltpu.make_async_copy(source, target, small_sems.at[i])
        for i, (source, target) in enumerate(
            (
                (tile_ref, tiles),
                (sub_ref, sub_rows),
                (weight_ref, weights),
                (rotor_ref, rotor_rows),
                (slot_ref, slot_table),
            )
        )
    ]
    copies = [
        pltpu.make_async_copy(velocity_ref.at[c], cells.at[c], sems.at[c]) for c in range(parts)
    ]
    for copy in small + copies:
        copy.start()
    for copy in small:
        copy.wait()
    weight = weights[...]
    high = weight.astype(BF16)
    rest = weight - high.astype(F32)
    middle = rest.astype(BF16)
    low = (rest - middle.astype(F32)).astype(BF16)
    weight_parts = jnp.concatenate([high, middle, low], axis=0)
    sub_hot = []
    place_rows = tiles[...] // halves
    half_rows = tiles[...] % halves
    for group in range(groups):
        half_column[pl.ds(group * TILE, TILE), :] = as_column(half_rows[group : group + 1, :])
        place = as_column(place_rows[group : group + 1, :])
        for block in range(columns // TILE):
            place_hot[pl.ds(group * TILE, TILE), pl.ds(block * TILE, TILE)] = hot(
                place == lanes(TILE) + block * TILE
            )
        sub = as_column(sub_rows[group : group + 1, :])
        wide = jnp.concatenate([sub[:, :subs]] * 3, axis=1)
        index = lax.broadcasted_iota(jnp.int32, (TILE, subs), 1)
        sub_hot.append(hot(wide == jnp.concatenate([index] * 3, axis=1)))
    gains[...] = jnp.dot(
        jnp.concatenate(sub_hot, axis=0), weight_parts, preferred_element_type=F32
    )
    slots = slots_of(rotor_rows[...], slot_table)
    slot_hot[...] = jnp.concatenate(
        [hot(slots[g : g + 1, :] == sublanes(rotors)) for g in range(groups)], axis=1
    )
    even_x = lax.axis_index("slab") % 2 == 0
    for c in range(parts):
        copies[c].wait()
        first, last = cells[c, 0], cells[c, size_x - 1]
        x_odd_ref[c] = jnp.where(even_x, first, last).astype(BF16)


def first_half(bits):
    index = lax.axis_index("slab") * lax.axis_size("cross") + lax.axis_index("cross")
    parity = index
    for bit in range(1, bits):
        parity = parity ^ (index >> bit)
    return parity % 2 == 0


def pool_kernel(
    bits,
    cells,
    place_hot,
    gains,
    half_column,
    slot_hot,
    keep_ref,
    send_ref,
    y_even_ref,
    y_odd_ref,
    total,
):
    parts, size_x, size_y, size_z = cells.shape
    columns = size_x * size_y
    halves = size_z // TILE
    rotors = slot_hot.shape[0]
    half = half_column[...]
    even_y = lax.axis_index("cross") % 2 == 0
    flat = jnp.concatenate(
        [cells[c].reshape(columns, size_z).astype(BF16) for c in range(parts)], axis=1
    )
    found = jnp.dot(place_hot[...], flat, preferred_element_type=F32)
    for c in range(parts):
        sample = found[:, c * size_z : c * size_z + TILE]
        for h in range(1, halves):
            at = c * size_z + h * TILE
            sample = jnp.where(half == h, found[:, at : at + TILE], sample)
        weighted = sample * gains[:, c * TILE : (c + 1) * TILE]
        high = weighted.astype(BF16)
        low = (weighted - high.astype(F32)).astype(BF16)
        sums = jnp.dot(
            slot_hot[...], jnp.concatenate([high, low], axis=1), preferred_element_type=F32
        )
        total[c * rotors : (c + 1) * rotors, :] = sums[:, TILE:] + sums[:, :TILE]
        first, last = cells[c, :, 0, :], cells[c, :, size_y - 1, :]
        y_even_ref[c] = jnp.where(even_y, last, first).astype(BF16)
        y_odd_ref[c] = jnp.where(even_y, first, last).astype(BF16)
    rows = keep_ref.shape[0]
    first, second = total[:rows, :], total[rows:, :]
    keep_ref[...] = jnp.where(first_half(bits), first, second)
    send_ref[...] = jnp.where(first_half(bits), second, first)


def pack_rows(target_ref, start, blocks):
    rows, width = blocks[0].shape
    count = rows * len(blocks)
    for j in range(width // TILE):
        for k, block in enumerate(blocks):
            at = start + j * count + k * rows
            target_ref[at : at + rows, :] = block[:, j * TILE : (j + 1) * TILE]


def unpack_rows(source_ref, start, width):
    count = (source_ref.shape[0] - start) // (width // TILE)
    return jnp.concatenate(
        [source_ref[start + j * count : start + (j + 1) * count, :] for j in range(width // TILE)],
        axis=1,
    )


def stencil_kernel(begin, depth, fences, slabs, crosses, *refs):
    refs, out_ref = refs[fences:-1], refs[-1]
    velocity_ref, x_even_ref, x_odd_ref, y_even_ref, y_odd_ref = refs
    parts, size_x, size_y, size_z = velocity_ref.shape
    row = lax.broadcasted_iota(jnp.int32, (size_y, size_z), 0)
    lane = lax.broadcasted_iota(jnp.int32, (size_y, size_z), 1)
    slab, cross = lax.axis_index("slab"), lax.axis_index("cross")
    even_x, even_y = slab % 2 == 0, cross % 2 == 0
    inner_x = jnp.logical_and(slab > 0, slab < slabs - 1)
    inner_y = jnp.logical_and(cross > 0, cross < crosses - 1)
    souths, norths = [], []
    for c in range(parts):
        near = y_even_ref[c].astype(F32)
        far = jnp.where(inner_y, y_odd_ref[c].astype(F32), 0.0)
        souths.append(jnp.where(even_y, far, near))
        norths.append(jnp.where(even_y, near, far))
    spread = time_step * viscosity
    for x in range(begin, begin + depth):
        drift = [(0.5 * time_step) * velocity_ref[d, x] for d in range(parts)]
        to_east, to_west = spread - drift[0], spread + drift[0]
        to_north, to_south = spread - drift[1], spread + drift[1]
        to_upper = jnp.where(lane == size_z - 1, 0.0, spread - drift[2])
        to_lower = jnp.where(lane == 0, 0.0, spread + drift[2])
        for c in range(parts):
            here = velocity_ref[c, x]
            if x > 0:
                west = velocity_ref[c, x - 1]
            else:
                far_x = jnp.where(inner_x, x_odd_ref[c].astype(F32), 0.0)
                west = jnp.where(even_x, far_x, x_even_ref[c].astype(F32))
            if x + 1 < size_x:
                east = velocity_ref[c, x + 1]
            else:
                far_x = jnp.where(inner_x, x_odd_ref[c].astype(F32), 0.0)
                east = jnp.where(even_x, x_even_ref[c].astype(F32), far_x)
            south = jnp.where(row == 0, souths[c][x : x + 1, :], pltpu.roll(here, 1, 0))
            north = jnp.where(
                row == size_y - 1, norths[c][x : x + 1, :], pltpu.roll(here, size_y - 1, 0)
            )
            out_ref[c, x - begin] = (
                (1.0 - 6.0 * spread) * here
                + (to_east * east + to_west * west)
                + (to_north * north + to_south * south)
                + (to_upper * pltpu.roll(here, size_z - 1, 1) + to_lower * pltpu.roll(here, 1, 1))
            )


def key_kernel(fences, *refs):
    cells, slot_ref, rotor_ref, sub_ref, key_ref, x_even_ref = refs[fences:]
    even_x = lax.axis_index("slab") % 2 == 0
    for c in range(cells.shape[0]):
        face = jnp.where(even_x, cells[c, cells.shape[1] - 1], cells[c, 0])
        x_even_ref[c] = face.astype(BF16)
    rotors = slot_ref.shape[0]
    keys = sub_ref[...] // 2 * rotors + slots_of(rotor_ref[...], slot_ref)
    for group in range(keys.shape[0]):
        key = as_column(keys[group : group + 1, :])
        for block in range(key_ref.shape[1] // TILE):
            key_ref[pl.ds(group * TILE, TILE), pl.ds(block * TILE, TILE)] = hot(
                key == lanes(TILE) + block * TILE
            )


def place_kernel(halves, fence_ref, tile_ref, place_ref):
    del fence_ref
    places = tile_ref[...] // halves
    for group in range(places.shape[0]):
        for block in range(place_ref.shape[0] // TILE):
            place_ref[pl.ds(block * TILE, TILE), pl.ds(group * TILE, TILE)] = hot(
                places[group : group + 1, :] == sublanes(TILE) + block * TILE
            )


def join_kernel(bits, fences, *refs):
    keep_ref, other_ref, states_ref, out_ref = refs[fences:]
    rows = keep_ref.shape[0]
    out_ref[:rows, :] = keep_ref[...] + other_ref[...]
    half = states_ref.shape[1] // 2
    pack_rows(
        out_ref, rows, [jnp.where(first_half(bits), states_ref[:, :half], states_ref[:, half:])]
    )


def merge_kernel(fences, shift, rows, width, pooled_rows, *refs):
    mine_ref, other_ref, out_ref = refs[fences:]
    out_ref[:pooled_rows, :] = mine_ref[:pooled_rows, :] + other_ref[:pooled_rows, :]
    if shift is None:
        out_ref[pooled_rows:, :] = mine_ref[pooled_rows:, :]
        return
    first = (lax.axis_index("slab") >> shift) % 2 == 0
    mine, other = [unpack_rows(ref, pooled_rows, width) for ref in (mine_ref, other_ref)]
    low, high = jnp.where(first, mine, other), jnp.where(first, other, mine)
    pieces = []
    for at in range(0, low.shape[0], rows):
        pieces += [low[at : at + rows], high[at : at + rows]]
    pack_rows(out_ref, pooled_rows, pieces)


def rotor_kernel(
    bits,
    planes,
    tile_ref,
    sub_ref,
    w_in_ref,
    w_out_ref,
    decay_ref,
    key_hot,
    place_hot,
    keep_ref,
    other_ref,
    *rest,
):
    field_refs, rest = rest[:planes], rest[planes:]
    out_ref, new_ref, by_slab, source_rows, wind, sems, new_sem = rest
    slabs, rows, width = by_slab.shape
    rotors = slabs * rows
    size_x, size_y, size_z = wind.shape
    parts = w_in_ref.shape[0] // TILE
    halves = size_z // TILE
    groups = tile_ref.shape[0]
    subs = w_out_ref.shape[1] // TILE
    depth = size_x // planes
    stores = []
    for k in range(planes):
        for c in range(1, parts):
            stores.append(
                pltpu.make_async_copy(
                    field_refs[k].at[c],
                    out_ref.at[c, pl.ds(k * depth, depth)],
                    sems.at[k * (parts - 1) + c - 1],
                )
            )
            stores[-1].start()
    split = parts * rotors // 2
    first = first_half(bits)
    keep, other = keep_ref[:split, :], other_ref[:split, :]
    pooled = jnp.concatenate(
        [jnp.where(first, keep, other), jnp.where(first, other, keep)], axis=0
    )
    pooled = (pooled * pool_scale).astype(BF16)
    pooled = jnp.concatenate([pooled[c * rotors : (c + 1) * rotors] for c in range(parts)], axis=1)
    keep, other = [unpack_rows(ref, split, width // 2) for ref in (keep_ref, other_ref)]
    old = jnp.concatenate(
        [jnp.where(first, keep, other), jnp.where(first, other, keep)], axis=1
    )
    drive = jnp.dot(pooled, w_in_ref[...], preferred_element_type=F32)
    new = old + state_step * (drive - decay_ref[...] * old)
    for j in range(slabs):
        by_slab[j] = new[j * rows : (j + 1) * rows, :]
    own = pltpu.make_async_copy(by_slab.at[lax.axis_index("slab")], new_ref, new_sem)
    own.start()
    stores.append(own)
    new_b = new.astype(BF16)

    half_rows = tile_ref[...] % halves
    sources = jnp.dot(new_b, w_out_ref[...], preferred_element_type=F32).astype(BF16)
    for pair in range(subs // 2):
        source_rows[pair * rotors : (pair + 1) * rotors, :] = sources[
            :, pair * 2 * TILE : (pair + 1) * 2 * TILE
        ]
    taken = jnp.dot(key_hot[...], source_rows[...], preferred_element_type=F32)
    second = jnp.concatenate(
        [as_column(sub_ref[g : g + 1, :] % 2) for g in range(groups)], axis=0
    )
    taken = jnp.where(second == 1, taken[:, TILE:], taken[:, :TILE])
    half = jnp.concatenate([as_column(half_rows[g : g + 1, :]) for g in range(groups)], axis=0)
    spread = jnp.concatenate(
        [jnp.where(half == h, taken, 0.0).astype(BF16) for h in range(halves)], axis=1
    )
    chunks = sems.shape[0] - planes * (parts - 1)
    step = size_x // chunks
    for k in range(chunks):
        forcing = jnp.dot(
            place_hot[pl.ds(k * step * size_y, step * size_y), :],
            spread,
            preferred_element_type=F32,
        )
        at = pl.ds(k * step, step)
        field = field_refs[k * step // depth][0, pl.ds(k * step % depth, step)]
        wind[at] = field - force_scale * forcing.reshape(step, size_y, size_z)
        stores.append(
            pltpu.make_async_copy(wind.at[at], out_ref.at[0, at], sems.at[planes * (parts - 1) + k])
        )
        stores[-1].start()
    for store in stores:
        store.wait()


def swap(value, axis, count, offset):
    return lax.ppermute(value, axis, [(i, i ^ offset) for i in range(count)])


def swap_pairs(value, axis, counts, first):
    slabs, crosses = counts
    if axis == "cross":
        pairs = [(i, (i + 1) % crosses) for i in range(first, crosses, 2)]
        return lax.ppermute(value, axis, pairs + [(j, i) for i, j in pairs])
    partner = {i: i + 1 for i in range(first, slabs - 1, 2)}
    partner.update({j: i for i, j in partner.items()})
    pairs = []
    for slab in range(slabs):
        for cross in range(crosses):
            to = (partner[slab], cross) if slab in partner else (slab, cross ^ 1)
            pairs.append((slab * crosses + cross, to[0] * crosses + to[1]))
    return lax.ppermute(value, BOTH, pairs)


def vmem(count):
    return [pl.BlockSpec(memory_space=pltpu.VMEM)] * count


def in_hbm(value):
    return pltpu.with_memory_space_constraint(value, pltpu.HBM)


SMEM = pl.BlockSpec(memory_space=pltpu.SMEM)
HBM = pl.BlockSpec(memory_space=pltpu.HBM)
ANY = pl.BlockSpec(memory_space=pl.ANY)


def load(tile, rotor, sub, slot_of_rotor, shape_weight, velocity):
    parts, size_x, size_y, size_z = velocity.shape
    columns = size_x * size_y
    groups = tile.shape[0]
    entries = groups * TILE
    rotors = slot_of_rotor.shape[0]
    return pl.pallas_call(
        load_kernel,
        out_shape=(
            jax.ShapeDtypeStruct((parts, size_y, size_z), BF16),
            jax.ShapeDtypeStruct(velocity.shape, F32),
            jax.ShapeDtypeStruct((entries, columns), BF16),
            jax.ShapeDtypeStruct((entries, parts * TILE), F32),
            jax.ShapeDtypeStruct((entries, TILE), jnp.int32),
            jax.ShapeDtypeStruct((rotors, entries), BF16),
        ),
        in_specs=[HBM] * 6,
        out_specs=tuple(vmem(6)),
        scratch_shapes=[
            pltpu.VMEM((groups, TILE), jnp.int32),
            pltpu.VMEM((groups, TILE), jnp.int32),
            pltpu.VMEM((groups, TILE), jnp.int32),
            pltpu.SMEM((rotors,), jnp.int32),
            pltpu.VMEM(shape_weight.shape, F32),
            pltpu.SemaphoreType.DMA((parts,)),
            pltpu.SemaphoreType.DMA((5,)),
        ],
        compiler_params=pltpu.CompilerParams(vmem_limit_bytes=8 << 20),
        cost_estimate=pl.CostEstimate(
            flops=2 * entries * columns * size_z,
            bytes_accessed=velocity.size * 4,
            transcendentals=0,
        ),
        name="load",
    )(*(in_hbm(value) for value in (tile, rotor, sub, slot_of_rotor, shape_weight, velocity)))


def pool(bits, cells, place_hot, gains, half_column, slot_hot):
    parts, size_x, size_y, size_z = cells.shape
    rows = parts * slot_hot.shape[0]
    part = jax.ShapeDtypeStruct((rows // 2, TILE), F32)
    return pl.pallas_call(
        functools.partial(pool_kernel, bits),
        out_shape=(
            part,
            part,
            jax.ShapeDtypeStruct((parts, size_x, size_z), BF16),
            jax.ShapeDtypeStruct((parts, size_x, size_z), BF16),
        ),
        in_specs=vmem(5),
        out_specs=tuple(vmem(4)),
        scratch_shapes=[pltpu.VMEM((rows, TILE), F32)],
        compiler_params=pltpu.CompilerParams(vmem_limit_bytes=12 << 20),
        cost_estimate=pl.CostEstimate(
            flops=2 * place_hot.size * parts * size_z, bytes_accessed=cells.size * 4, transcendentals=0
        ),
        name="pool",
    )(cells, place_hot, gains, half_column, slot_hot)


def stencil(begin, depth, fences, slabs, crosses, velocity, halos):
    parts, size_x, size_y, size_z = velocity.shape
    return pl.pallas_call(
        functools.partial(stencil_kernel, begin, depth, len(fences), slabs, crosses),
        out_shape=jax.ShapeDtypeStruct((parts, depth, size_y, size_z), F32),
        in_specs=[ANY] * len(fences) + vmem(5),
        out_specs=vmem(1)[0],
        compiler_params=pltpu.CompilerParams(vmem_limit_bytes=4 << 20),
        cost_estimate=pl.CostEstimate(
            flops=1000 * velocity.size * depth // size_x,
            bytes_accessed=8 * velocity.size * depth // size_x,
            transcendentals=0,
        ),
        name="stencil",
    )(*fences, velocity, *halos)


def key_matrix(fences, cells, slot_of_rotor, rotor, sub, keys):
    parts, _, size_y, size_z = cells.shape
    entries = rotor.shape[0] * TILE
    return pl.pallas_call(
        functools.partial(key_kernel, len(fences)),
        out_shape=(
            jax.ShapeDtypeStruct((entries, keys), BF16),
            jax.ShapeDtypeStruct((parts, size_y, size_z), BF16),
        ),
        in_specs=[ANY] * len(fences) + vmem(1) + [SMEM] + vmem(2),
        out_specs=tuple(vmem(2)),
        compiler_params=pltpu.CompilerParams(vmem_limit_bytes=4 << 20),
        cost_estimate=pl.CostEstimate(
            flops=1000 * entries * keys, bytes_accessed=2 * entries * keys, transcendentals=0
        ),
        name="keys",
    )(*fences, cells, slot_of_rotor, rotor, sub)


def place_matrix(fence, tile, columns, halves):
    entries = tile.shape[0] * TILE
    return pl.pallas_call(
        functools.partial(place_kernel, halves),
        out_shape=jax.ShapeDtypeStruct((columns, entries), BF16),
        in_specs=[ANY] + vmem(1),
        out_specs=vmem(1)[0],
        compiler_params=pltpu.CompilerParams(vmem_limit_bytes=4 << 20),
        cost_estimate=pl.CostEstimate(
            flops=1000 * entries * columns, bytes_accessed=2 * entries * columns, transcendentals=0
        ),
        name="places",
    )(fence, tile)


def join(bits, fences, keep, other, states):
    rows = keep.shape[0] + states.size // 2 // TILE
    return pl.pallas_call(
        functools.partial(join_kernel, bits, len(fences)),
        out_shape=jax.ShapeDtypeStruct((rows, TILE), F32),
        in_specs=[ANY] * len(fences) + vmem(3),
        out_specs=vmem(1)[0],
        compiler_params=pltpu.CompilerParams(vmem_limit_bytes=4 << 20),
        name="join",
    )(*fences, keep, other, states)


def merge(fences, shift, rows, width, pooled_rows, mine, other):
    total = mine.shape[0] + (other.shape[0] - pooled_rows if shift is not None else 0)
    return pl.pallas_call(
        functools.partial(merge_kernel, len(fences), shift, rows, width, pooled_rows),
        out_shape=jax.ShapeDtypeStruct((total, TILE), F32),
        in_specs=[ANY] * len(fences) + vmem(2),
        out_specs=vmem(1)[0],
        compiler_params=pltpu.CompilerParams(vmem_limit_bytes=4 << 20),
        name="merge",
    )(*fences, mine, other)


def rotors_step(
    slabs, bits, tile, sub, w_in, w_out, decay, key_hot, place_hot, keep, other, fields
):
    width = w_in.shape[1]
    planes = len(fields)
    parts, depth, size_y, size_z = fields[0].shape
    size_x = planes * depth
    keys = key_hot.shape[1]
    rows = keys // (w_out.shape[1] // (2 * TILE)) // slabs
    chunks = 4
    return pl.pallas_call(
        functools.partial(rotor_kernel, bits, planes),
        out_shape=(
            jax.ShapeDtypeStruct((parts, size_x, size_y, size_z), F32),
            jax.ShapeDtypeStruct((rows, width), F32),
        ),
        in_specs=vmem(9 + planes),
        out_specs=(HBM, HBM),
        scratch_shapes=[
            pltpu.VMEM((slabs, rows, width), F32),
            pltpu.VMEM((keys, 2 * TILE), BF16),
            pltpu.VMEM((size_x, size_y, size_z), F32),
            pltpu.SemaphoreType.DMA((planes * (parts - 1) + chunks,)),
            pltpu.SemaphoreType.DMA,
        ],
        compiler_params=pltpu.CompilerParams(vmem_limit_bytes=10 << 20),
        cost_estimate=pl.CostEstimate(
            flops=4 * place_hot.size * size_z, bytes_accessed=w_out.size * 2, transcendentals=0
        ),
        name="rotors",
    )(tile, sub, w_in, w_out, decay, key_hot, place_hot, keep, other, *fields)


def on_device(
    slabs,
    crosses,
    velocity,
    shape_weight,
    w_in,
    w_out,
    decay,
    rotor_states,
    slot_of_rotor,
    entry_rotor,
    entry_tile,
    entry_sub,
):
    size_x, size_y, size_z = velocity.shape[1:]
    entries = entry_tile.shape[0]
    width = w_in.shape[1]
    count = slabs * crosses
    tile = entry_tile.reshape(entries // TILE, TILE)
    rotor = entry_rotor.reshape(entries // TILE, TILE)
    sub = entry_sub.reshape(entries // TILE, TILE)

    bits = count.bit_length() - 1
    x_odd, cells, *loaded = load(tile, rotor, sub, slot_of_rotor, shape_weight, velocity)
    x_odd = swap_pairs(x_odd, "slab", (slabs, crosses), 1)
    keep, send, y_even, y_odd = pool(bits, cells, *loaded)
    y_even = swap_pairs(y_even, "cross", (slabs, crosses), 0)
    y_odd = swap_pairs(y_odd, "cross", (slabs, crosses), 1)
    pooled_rows = keep.shape[0]

    planes = 2
    depth = size_x // planes
    halos = [None, x_odd, y_even, y_odd]

    def make_keys(fence):
        made, face = key_matrix(
            (fence, x_odd),
            cells,
            slot_of_rotor,
            rotor,
            sub,
            w_out.shape[1] // (2 * TILE) * slot_of_rotor.shape[0],
        )
        halos[0] = swap_pairs(face, "slab", (slabs, crosses), 0)
        return made

    def make_places(fence):
        return place_matrix(fence, tile, size_x * size_y, size_z // TILE)

    def make_field(k, fence):
        return stencil(k * depth, depth, (fence,), slabs, crosses, cells, halos)

    work = [make_keys, make_places] + [functools.partial(make_field, k) for k in range(planes)]
    done = []
    packed = join(bits, (), keep, swap(send, BOTH, count, 1), rotor_states)
    steps = range(bits - 1, 0, -1)
    for bit in steps:
        beside = 1 if bit > steps[-1] else len(work) - len(done)
        made = [item(packed) for item in work[len(done) : len(done) + beside]]
        done += made
        if 1 << bit >= crosses:
            other, shift = packed, bit - (crosses.bit_length() - 1)
        else:
            other, shift = packed[:pooled_rows], None
        other = swap(other, BOTH, count, 1 << bit | 1)
        packed = merge(made, shift, rotor_states.shape[0], width // 2, pooled_rows, packed, other)
    other = swap(packed, BOTH, count, 1)
    key_hot, place_hot, *fields = done
    return rotors_step(
        slabs, bits, tile, sub, w_in, w_out, decay[None, :], key_hot, place_hot, packed, other, fields
    )


def solution(mesh):
    slabs, crosses = mesh.shape["slab"], mesh.shape["cross"]
    in_specs = (
        P(None, "slab", "cross", None),
        P(),
        P(),
        P(),
        P(),
        P("slab", None),
        P(),
        P(("slab", "cross"), None),
        P(("slab", "cross")),
        P(("slab", "cross")),
    )
    out_specs = (P(None, "slab", "cross", None), P("slab", None))
    return jax.shard_map(
        functools.partial(on_device, slabs, crosses),
        mesh=mesh,
        in_specs=in_specs,
        out_specs=out_specs,
        check_vma=False,
    )
```

```python
import functools

import jax
import jax.numpy as jnp
from jax import lax
from jax.experimental import pallas as pl
from jax.experimental.pallas import tpu as pltpu
from jax.sharding import PartitionSpec as P

TILE = 128

time_step = 0.1
viscosity = 0.3
pool_scale = 1.0 / 64.0
state_step = 0.5
force_scale = 0.5

BOTH = ("slab", "cross")
F32 = jnp.float32
BF16 = jnp.bfloat16


def lanes(rows):
    return lax.broadcasted_iota(jnp.int32, (rows, TILE), 1)


def sublanes(rows):
    return lax.broadcasted_iota(jnp.int32, (rows, TILE), 0)


def as_column(row):
    return jnp.transpose(jnp.broadcast_to(row, (TILE, TILE)))


def hot(mask):
    return jnp.where(mask, 1.0, 0.0).astype(BF16)


def slots_of(rotors, slot_ref):
    slots = jnp.zeros_like(rotors)
    for rotor in range(slot_ref.shape[0]):
        slots = jnp.where(rotors == rotor, slot_ref[rotor], slots)
    return slots


def load_kernel(
    tile_ref,
    rotor_ref,
    sub_ref,
    slot_ref,
    weight_ref,
    velocity_ref,
    x_odd_ref,
    cells,
    place_hot,
    gains,
    half_column,
    slot_hot,
    tiles,
    rotor_rows,
    sub_rows,
    slot_table,
    weights,
    sems,
    small_sems,
):
    parts, size_x, size_y, size_z = velocity_ref.shape
    columns = size_x * size_y
    halves = size_z // TILE
    groups = tile_ref.shape[0]
    rotors = slot_ref.shape[0]
    subs = weight_ref.shape[0]
    small = [
        pltpu.make_async_copy(source, target, small_sems.at[i])
        for i, (source, target) in enumerate(
            (
                (tile_ref, tiles),
                (sub_ref, sub_rows),
                (weight_ref, weights),
                (rotor_ref, rotor_rows),
                (slot_ref, slot_table),
            )
        )
    ]
    copies = [
        pltpu.make_async_copy(velocity_ref.at[c], cells.at[c], sems.at[c]) for c in range(parts)
    ]
    for copy in small + copies:
        copy.start()
    for copy in small:
        copy.wait()
    weight = weights[...]
    high = weight.astype(BF16)
    rest = weight - high.astype(F32)
    middle = rest.astype(BF16)
    low = (rest - middle.astype(F32)).astype(BF16)
    weight_parts = jnp.concatenate([high, middle, low], axis=0)
    sub_hot = []
    place_rows = tiles[...] // halves
    half_rows = tiles[...] % halves
    for group in range(groups):
        half_column[pl.ds(group * TILE, TILE), :] = as_column(half_rows[group : group + 1, :])
        place = as_column(place_rows[group : group + 1, :])
        for block in range(columns // TILE):
            place_hot[pl.ds(group * TILE, TILE), pl.ds(block * TILE, TILE)] = hot(
                place == lanes(TILE) + block * TILE
            )
        sub = as_column(sub_rows[group : group + 1, :])
        wide = jnp.concatenate([sub[:, :subs]] * 3, axis=1)
        index = lax.broadcasted_iota(jnp.int32, (TILE, subs), 1)
        sub_hot.append(hot(wide == jnp.concatenate([index] * 3, axis=1)))
    gains[...] = jnp.dot(
        jnp.concatenate(sub_hot, axis=0), weight_parts, preferred_element_type=F32
    )
    slots = slots_of(rotor_rows[...], slot_table)
    slot_hot[...] = jnp.concatenate(
        [hot(slots[g : g + 1, :] == sublanes(rotors)) for g in range(groups)], axis=1
    )
    even_x = lax.axis_index("slab") % 2 == 0
    for c in range(parts):
        copies[c].wait()
        first, last = cells[c, 0], cells[c, size_x - 1]
        x_odd_ref[c] = jnp.where(even_x, first, last).astype(BF16)


def first_half(bits):
    index = lax.axis_index("slab") * lax.axis_size("cross") + lax.axis_index("cross")
    parity = index
    for bit in range(1, bits):
        parity = parity ^ (index >> bit)
    return parity % 2 == 0


def pool_kernel(
    bits,
    cells,
    place_hot,
    gains,
    half_column,
    slot_hot,
    keep_ref,
    send_ref,
    y_even_ref,
    y_odd_ref,
    total,
):
    parts, size_x, size_y, size_z = cells.shape
    columns = size_x * size_y
    halves = size_z // TILE
    rotors = slot_hot.shape[0]
    half = half_column[...]
    even_y = lax.axis_index("cross") % 2 == 0
    flat = jnp.concatenate(
        [cells[c].reshape(columns, size_z).astype(BF16) for c in range(parts)], axis=1
    )
    found = jnp.dot(place_hot[...], flat, preferred_element_type=F32)
    for c in range(parts):
        sample = found[:, c * size_z : c * size_z + TILE]
        for h in range(1, halves):
            at = c * size_z + h * TILE
            sample = jnp.where(half == h, found[:, at : at + TILE], sample)
        weighted = sample * gains[:, c * TILE : (c + 1) * TILE]
        high = weighted.astype(BF16)
        low = (weighted - high.astype(F32)).astype(BF16)
        sums = jnp.dot(
            slot_hot[...], jnp.concatenate([high, low], axis=1), preferred_element_type=F32
        )
        total[c * rotors : (c + 1) * rotors, :] = sums[:, TILE:] + sums[:, :TILE]
        first, last = cells[c, :, 0, :], cells[c, :, size_y - 1, :]
        y_even_ref[c] = jnp.where(even_y, last, first).astype(BF16)
        y_odd_ref[c] = jnp.where(even_y, first, last).astype(BF16)
    rows = keep_ref.shape[0]
    first, second = total[:rows, :], total[rows:, :]
    keep_ref[...] = jnp.where(first_half(bits), first, second)
    send_ref[...] = jnp.where(first_half(bits), second, first)


def pack_rows(target_ref, start, blocks):
    rows, width = blocks[0].shape
    count = rows * len(blocks)
    for j in range(width // TILE):
        for k, block in enumerate(blocks):
            at = start + j * count + k * rows
            target_ref[at : at + rows, :] = block[:, j * TILE : (j + 1) * TILE]


def unpack_rows(source_ref, start, width):
    count = (source_ref.shape[0] - start) // (width // TILE)
    return jnp.concatenate(
        [source_ref[start + j * count : start + (j + 1) * count, :] for j in range(width // TILE)],
        axis=1,
    )


def stencil_kernel(planes, edges, fences, slabs, crosses, *refs):
    refs, out_ref = refs[fences:-1], refs[-1]
    velocity_ref, y_even_ref, y_odd_ref = refs[:3]
    if edges:
        x_even_ref, x_odd_ref = refs[3:]
    parts, size_x, size_y, size_z = velocity_ref.shape
    row = lax.broadcasted_iota(jnp.int32, (size_y, size_z), 0)
    lane = lax.broadcasted_iota(jnp.int32, (size_y, size_z), 1)
    slab, cross = lax.axis_index("slab"), lax.axis_index("cross")
    even_x, even_y = slab % 2 == 0, cross % 2 == 0
    inner_x = jnp.logical_and(slab > 0, slab < slabs - 1)
    inner_y = jnp.logical_and(cross > 0, cross < crosses - 1)
    souths, norths = [], []
    for c in range(parts):
        near = y_even_ref[c].astype(F32)
        far = jnp.where(inner_y, y_odd_ref[c].astype(F32), 0.0)
        souths.append(jnp.where(even_y, far, near))
        norths.append(jnp.where(even_y, near, far))
    spread = time_step * viscosity
    for at, x in enumerate(planes):
        drift = [(0.5 * time_step) * velocity_ref[d, x] for d in range(parts)]
        to_east, to_west = spread - drift[0], spread + drift[0]
        to_north, to_south = spread - drift[1], spread + drift[1]
        to_upper = jnp.where(lane == size_z - 1, 0.0, spread - drift[2])
        to_lower = jnp.where(lane == 0, 0.0, spread + drift[2])
        for c in range(parts):
            here = velocity_ref[c, x]
            if x > 0:
                west = velocity_ref[c, x - 1]
            else:
                far_x = jnp.where(inner_x, x_odd_ref[c].astype(F32), 0.0)
                west = jnp.where(even_x, far_x, x_even_ref[c].astype(F32))
            if x + 1 < size_x:
                east = velocity_ref[c, x + 1]
            else:
                far_x = jnp.where(inner_x, x_odd_ref[c].astype(F32), 0.0)
                east = jnp.where(even_x, x_even_ref[c].astype(F32), far_x)
            south = jnp.where(row == 0, souths[c][x : x + 1, :], pltpu.roll(here, 1, 0))
            north = jnp.where(
                row == size_y - 1, norths[c][x : x + 1, :], pltpu.roll(here, size_y - 1, 0)
            )
            out_ref[c, at] = (
                (1.0 - 6.0 * spread) * here
                + (to_east * east + to_west * west)
                + (to_north * north + to_south * south)
                + (to_upper * pltpu.roll(here, size_z - 1, 1) + to_lower * pltpu.roll(here, 1, 1))
            )


def key_kernel(fences, *refs):
    slot_ref, rotor_ref, sub_ref, key_ref = refs[fences:]
    rotors = slot_ref.shape[0]
    keys = sub_ref[...] // 2 * rotors + slots_of(rotor_ref[...], slot_ref)
    for group in range(keys.shape[0]):
        key = as_column(keys[group : group + 1, :])
        for block in range(key_ref.shape[1] // TILE):
            key_ref[pl.ds(group * TILE, TILE), pl.ds(block * TILE, TILE)] = hot(
                key == lanes(TILE) + block * TILE
            )


def place_kernel(halves, fence_ref, tile_ref, place_ref):
    del fence_ref
    places = tile_ref[...] // halves
    for group in range(places.shape[0]):
        for block in range(place_ref.shape[0] // TILE):
            place_ref[pl.ds(block * TILE, TILE), pl.ds(group * TILE, TILE)] = hot(
                places[group : group + 1, :] == sublanes(TILE) + block * TILE
            )


def join_kernel(bits, fences, *refs):
    keep_ref, other_ref, states_ref, cells, out_ref, x_even_ref = refs[fences:]
    even_x = lax.axis_index("slab") % 2 == 0
    for c in range(cells.shape[0]):
        face = jnp.where(even_x, cells[c, cells.shape[1] - 1], cells[c, 0])
        x_even_ref[c] = face.astype(BF16)
    rows = keep_ref.shape[0]
    out_ref[:rows, :] = keep_ref[...] + other_ref[...]
    half = states_ref.shape[1] // 2
    pack_rows(
        out_ref, rows, [jnp.where(first_half(bits), states_ref[:, :half], states_ref[:, half:])]
    )


def merge_kernel(fences, packs, shift, rows, width, pooled_rows, *refs):
    refs, out_ref = refs[fences:-1], refs[-1]
    total = refs[0][:pooled_rows, :]
    for other in refs[1:]:
        total = total + other[:pooled_rows, :]
    out_ref[:pooled_rows, :] = total
    mine = (lax.axis_index("slab") >> shift) % packs
    blocks = [unpack_rows(ref, pooled_rows, width) for ref in refs[:packs]]
    ordered = []
    for place in range(packs):
        block = blocks[0]
        for k in range(1, packs):
            block = jnp.where((mine ^ k) == place, blocks[k], block)
        ordered.append(block)
    pieces = []
    for at in range(0, blocks[0].shape[0], rows):
        pieces += [block[at : at + rows] for block in ordered]
    pack_rows(out_ref, pooled_rows, pieces)


def rotor_kernel(
    bits,
    runs,
    tile_ref,
    sub_ref,
    w_in_ref,
    w_out_ref,
    decay_ref,
    key_hot,
    place_hot,
    keep_ref,
    other_ref,
    *rest,
):
    count = 1 + max(run[2] for run in runs)
    field_refs, rest = rest[:count], rest[count:]
    out_ref, new_ref, by_slab, source_rows, wind, sems, new_sem = rest
    slabs, rows, width = by_slab.shape
    rotors = slabs * rows
    size_x, size_y, size_z = wind.shape
    parts = w_in_ref.shape[0] // TILE
    halves = size_z // TILE
    groups = tile_ref.shape[0]
    subs = w_out_ref.shape[1] // TILE
    stores = []
    for k, (first, number, which, at) in enumerate(runs):
        stores.append(
            pltpu.make_async_copy(
                field_refs[which].at[1:, pl.ds(at, number)],
                out_ref.at[1:, pl.ds(first, number)],
                sems.at[k],
            )
        )
        stores[-1].start()
    split = parts * rotors // 2
    first = first_half(bits)
    keep, other = keep_ref[:split, :], other_ref[:split, :]
    pooled = jnp.concatenate(
        [jnp.where(first, keep, other), jnp.where(first, other, keep)], axis=0
    )
    pooled = (pooled * pool_scale).astype(BF16)
    pooled = jnp.concatenate([pooled[c * rotors : (c + 1) * rotors] for c in range(parts)], axis=1)
    keep, other = [unpack_rows(ref, split, width // 2) for ref in (keep_ref, other_ref)]
    old = jnp.concatenate(
        [jnp.where(first, keep, other), jnp.where(first, other, keep)], axis=1
    )
    drive = jnp.dot(pooled, w_in_ref[...], preferred_element_type=F32)
    new = old + state_step * (drive - decay_ref[...] * old)
    for j in range(slabs):
        by_slab[j] = new[j * rows : (j + 1) * rows, :]
    own = pltpu.make_async_copy(by_slab.at[lax.axis_index("slab")], new_ref, new_sem)
    own.start()
    stores.append(own)
    new_b = new.astype(BF16)

    half_rows = tile_ref[...] % halves
    sources = jnp.dot(new_b, w_out_ref[...], preferred_element_type=F32).astype(BF16)
    for pair in range(subs // 2):
        source_rows[pair * rotors : (pair + 1) * rotors, :] = sources[
            :, pair * 2 * TILE : (pair + 1) * 2 * TILE
        ]
    taken = jnp.dot(key_hot[...], source_rows[...], preferred_element_type=F32)
    second = jnp.concatenate(
        [as_column(sub_ref[g : g + 1, :] % 2) for g in range(groups)], axis=0
    )
    taken = jnp.where(second == 1, taken[:, TILE:], taken[:, :TILE])
    half = jnp.concatenate([as_column(half_rows[g : g + 1, :]) for g in range(groups)], axis=0)
    spread = jnp.concatenate(
        [jnp.where(half == h, taken, 0.0).astype(BF16) for h in range(halves)], axis=1
    )
    chunks = sems.shape[0] - len(runs)
    step = size_x // chunks
    for k in range(chunks):
        forcing = jnp.dot(
            place_hot[pl.ds(k * step * size_y, step * size_y), :],
            spread,
            preferred_element_type=F32,
        ).reshape(step, size_y, size_z)
        for first, number, which, at in runs:
            begin, end = max(first, k * step), min(first + number, (k + 1) * step)
            if begin < end:
                field = field_refs[which][0, at + begin - first : at + end - first]
                wind[begin:end] = field - force_scale * forcing[begin - k * step : end - k * step]
        at = pl.ds(k * step, step)
        stores.append(
            pltpu.make_async_copy(wind.at[at], out_ref.at[0, at], sems.at[len(runs) + k])
        )
        stores[-1].start()
    for store in stores:
        store.wait()


def swap(value, axis, count, offset):
    return lax.ppermute(value, axis, [(i, i ^ offset) for i in range(count)])


def swap_pairs(value, axis, counts, first):
    slabs, crosses = counts
    if axis == "cross":
        pairs = [(i, (i + 1) % crosses) for i in range(first, crosses, 2)]
        return lax.ppermute(value, axis, pairs + [(j, i) for i, j in pairs])
    partner = {i: i + 1 for i in range(first, slabs - 1, 2)}
    partner.update({j: i for i, j in partner.items()})
    pairs = []
    for slab in range(slabs):
        for cross in range(crosses):
            to = (partner[slab], cross) if slab in partner else (slab, cross ^ 1)
            pairs.append((slab * crosses + cross, to[0] * crosses + to[1]))
    return lax.ppermute(value, BOTH, pairs)


def vmem(count):
    return [pl.BlockSpec(memory_space=pltpu.VMEM)] * count


def in_hbm(value):
    return pltpu.with_memory_space_constraint(value, pltpu.HBM)


SMEM = pl.BlockSpec(memory_space=pltpu.SMEM)
HBM = pl.BlockSpec(memory_space=pltpu.HBM)
ANY = pl.BlockSpec(memory_space=pl.ANY)


def load(tile, rotor, sub, slot_of_rotor, shape_weight, velocity):
    parts, size_x, size_y, size_z = velocity.shape
    columns = size_x * size_y
    groups = tile.shape[0]
    entries = groups * TILE
    rotors = slot_of_rotor.shape[0]
    return pl.pallas_call(
        load_kernel,
        out_shape=(
            jax.ShapeDtypeStruct((parts, size_y, size_z), BF16),
            jax.ShapeDtypeStruct(velocity.shape, F32),
            jax.ShapeDtypeStruct((entries, columns), BF16),
            jax.ShapeDtypeStruct((entries, parts * TILE), F32),
            jax.ShapeDtypeStruct((entries, TILE), jnp.int32),
            jax.ShapeDtypeStruct((rotors, entries), BF16),
        ),
        in_specs=[HBM] * 6,
        out_specs=tuple(vmem(6)),
        scratch_shapes=[
            pltpu.VMEM((groups, TILE), jnp.int32),
            pltpu.VMEM((groups, TILE), jnp.int32),
            pltpu.VMEM((groups, TILE), jnp.int32),
            pltpu.SMEM((rotors,), jnp.int32),
            pltpu.VMEM(shape_weight.shape, F32),
            pltpu.SemaphoreType.DMA((parts,)),
            pltpu.SemaphoreType.DMA((5,)),
        ],
        compiler_params=pltpu.CompilerParams(vmem_limit_bytes=8 << 20),
        cost_estimate=pl.CostEstimate(
            flops=2 * entries * columns * size_z,
            bytes_accessed=velocity.size * 4,
            transcendentals=0,
        ),
        name="load",
    )(*(in_hbm(value) for value in (tile, rotor, sub, slot_of_rotor, shape_weight, velocity)))


def pool(bits, cells, place_hot, gains, half_column, slot_hot):
    parts, size_x, size_y, size_z = cells.shape
    rows = parts * slot_hot.shape[0]
    part = jax.ShapeDtypeStruct((rows // 2, TILE), F32)
    return pl.pallas_call(
        functools.partial(pool_kernel, bits),
        out_shape=(
            part,
            part,
            jax.ShapeDtypeStruct((parts, size_x, size_z), BF16),
            jax.ShapeDtypeStruct((parts, size_x, size_z), BF16),
        ),
        in_specs=vmem(5),
        out_specs=tuple(vmem(4)),
        scratch_shapes=[pltpu.VMEM((rows, TILE), F32)],
        compiler_params=pltpu.CompilerParams(vmem_limit_bytes=12 << 20),
        cost_estimate=pl.CostEstimate(
            flops=2 * place_hot.size * parts * size_z, bytes_accessed=cells.size * 4, transcendentals=0
        ),
        name="pool",
    )(cells, place_hot, gains, half_column, slot_hot)


def stencil(planes, fences, slabs, crosses, velocity, halos):
    parts, size_x, size_y, size_z = velocity.shape
    edges = len(halos) > 2
    return pl.pallas_call(
        functools.partial(stencil_kernel, planes, edges, len(fences), slabs, crosses),
        out_shape=jax.ShapeDtypeStruct((parts, len(planes), size_y, size_z), F32),
        in_specs=[ANY] * len(fences) + vmem(1 + len(halos)),
        out_specs=vmem(1)[0],
        compiler_params=pltpu.CompilerParams(vmem_limit_bytes=4 << 20),
        cost_estimate=pl.CostEstimate(
            flops=1000 * velocity.size * len(planes) // size_x,
            bytes_accessed=8 * velocity.size * len(planes) // size_x,
            transcendentals=0,
        ),
        name="stencil",
    )(*fences, velocity, *halos)


def key_matrix(fences, slot_of_rotor, rotor, sub, keys):
    entries = rotor.shape[0] * TILE
    return pl.pallas_call(
        functools.partial(key_kernel, len(fences)),
        out_shape=jax.ShapeDtypeStruct((entries, keys), BF16),
        in_specs=[ANY] * len(fences) + [SMEM] + vmem(2),
        out_specs=vmem(1)[0],
        compiler_params=pltpu.CompilerParams(vmem_limit_bytes=4 << 20),
        cost_estimate=pl.CostEstimate(
            flops=1000 * entries * keys, bytes_accessed=2 * entries * keys, transcendentals=0
        ),
        name="keys",
    )(*fences, slot_of_rotor, rotor, sub)


def place_matrix(fence, tile, columns, halves):
    entries = tile.shape[0] * TILE
    return pl.pallas_call(
        functools.partial(place_kernel, halves),
        out_shape=jax.ShapeDtypeStruct((columns, entries), BF16),
        in_specs=[ANY] + vmem(1),
        out_specs=vmem(1)[0],
        compiler_params=pltpu.CompilerParams(vmem_limit_bytes=4 << 20),
        cost_estimate=pl.CostEstimate(
            flops=1000 * entries * columns, bytes_accessed=2 * entries * columns, transcendentals=0
        ),
        name="places",
    )(fence, tile)


def join(bits, fences, keep, other, states, cells):
    parts, _, size_y, size_z = cells.shape
    rows = keep.shape[0] + states.size // 2 // TILE
    return pl.pallas_call(
        functools.partial(join_kernel, bits, len(fences)),
        out_shape=(
            jax.ShapeDtypeStruct((rows, TILE), F32),
            jax.ShapeDtypeStruct((parts, size_y, size_z), BF16),
        ),
        in_specs=[ANY] * len(fences) + vmem(4),
        out_specs=tuple(vmem(2)),
        compiler_params=pltpu.CompilerParams(vmem_limit_bytes=4 << 20),
        name="join",
    )(*fences, keep, other, states, cells)


def merge(fences, shift, rows, width, pooled_rows, packed, pooled):
    total = pooled_rows + len(packed) * (packed[0].shape[0] - pooled_rows)
    return pl.pallas_call(
        functools.partial(
            merge_kernel, len(fences), len(packed), shift, rows, width, pooled_rows
        ),
        out_shape=jax.ShapeDtypeStruct((total, TILE), F32),
        in_specs=[ANY] * len(fences) + vmem(len(packed) + len(pooled)),
        out_specs=vmem(1)[0],
        compiler_params=pltpu.CompilerParams(vmem_limit_bytes=4 << 20),
        name="merge",
    )(*fences, *packed, *pooled)


def rotors_step(
    slabs, bits, runs, tile, sub, w_in, w_out, decay, key_hot, place_hot, keep, other, fields
):
    width = w_in.shape[1]
    parts, _, size_y, size_z = fields[0].shape
    size_x = sum(field.shape[1] for field in fields)
    keys = key_hot.shape[1]
    rows = keys // (w_out.shape[1] // (2 * TILE)) // slabs
    chunks = 2
    return pl.pallas_call(
        functools.partial(rotor_kernel, bits, runs),
        out_shape=(
            jax.ShapeDtypeStruct((parts, size_x, size_y, size_z), F32),
            jax.ShapeDtypeStruct((rows, width), F32),
        ),
        in_specs=vmem(9 + len(fields)),
        out_specs=(HBM, HBM),
        scratch_shapes=[
            pltpu.VMEM((slabs, rows, width), F32),
            pltpu.VMEM((keys, 2 * TILE), BF16),
            pltpu.VMEM((size_x, size_y, size_z), F32),
            pltpu.SemaphoreType.DMA((len(runs) + chunks,)),
            pltpu.SemaphoreType.DMA,
        ],
        compiler_params=pltpu.CompilerParams(vmem_limit_bytes=10 << 20),
        cost_estimate=pl.CostEstimate(
            flops=4 * place_hot.size * size_z, bytes_accessed=w_out.size * 2, transcendentals=0
        ),
        name="rotors",
    )(tile, sub, w_in, w_out, decay, key_hot, place_hot, keep, other, *fields)


def on_device(
    slabs,
    crosses,
    velocity,
    shape_weight,
    w_in,
    w_out,
    decay,
    rotor_states,
    slot_of_rotor,
    entry_rotor,
    entry_tile,
    entry_sub,
):
    size_x, size_y, size_z = velocity.shape[1:]
    entries = entry_tile.shape[0]
    width = w_in.shape[1]
    count = slabs * crosses
    tile = entry_tile.reshape(entries // TILE, TILE)
    rotor = entry_rotor.reshape(entries // TILE, TILE)
    sub = entry_sub.reshape(entries // TILE, TILE)

    bits = count.bit_length() - 1
    x_odd, cells, *loaded = load(tile, rotor, sub, slot_of_rotor, shape_weight, velocity)
    x_odd = swap_pairs(x_odd, "slab", (slabs, crosses), 1)
    keep, send, y_even, y_odd = pool(bits, cells, *loaded)
    y_even = swap_pairs(y_even, "cross", (slabs, crosses), 0)
    y_odd = swap_pairs(y_odd, "cross", (slabs, crosses), 1)
    pooled_rows = keep.shape[0]

    middle = size_x // 2
    inner, outer = tuple(range(1, middle)), (0,) + tuple(range(middle, size_x))
    runs = ((1, middle - 1, 0, 0), (0, 1, 1, 0), (middle, size_x - middle, 1, 1))
    packed, x_even = join(bits, (), keep, swap(send, BOTH, count, 1), rotor_states, cells)
    x_even = swap_pairs(x_even, "slab", (slabs, crosses), 0)
    slab_bit = crosses.bit_length() - 1
    steps = [tuple(range(b, min(b + 2, bits))) for b in range(1, bits, 2)][::-1]
    fields = []
    for step in steps:
        made = []
        if step == steps[0]:
            keys = w_out.shape[1] // (2 * TILE) * slot_of_rotor.shape[0]
            key_hot = key_matrix((packed, x_odd), slot_of_rotor, rotor, sub, keys)
            fields.append(stencil(inner, (packed,), slabs, crosses, cells, (y_even, y_odd)))
            made += [key_hot, fields[-1]]
        if step == steps[-1]:
            place_hot = place_matrix(packed, tile, size_x * size_y, size_z // TILE)
            halos = (y_even, y_odd, x_even, x_odd)
            fields.append(stencil(outer, (packed,), slabs, crosses, cells, halos))
            made += [place_hot, fields[-1]]
        slab_bits = [b for b in step if b >= slab_bit]
        across = [1 << b | 1 for b in slab_bits]
        if len(slab_bits) == 2:
            across.append(sum(1 << b for b in step))
            within = []
        else:
            within = [1 << b | 1 for b in step if b < slab_bit]
            within += [sum(1 << b for b in step)] if len(step) == 2 else []
        sums = packed[:pooled_rows]
        packed = merge(
            made,
            slab_bits[0] - slab_bit,
            rotor_states.shape[0],
            width // 2,
            pooled_rows,
            [packed] + [swap(packed, BOTH, count, offset) for offset in across],
            [swap(sums, BOTH, count, offset) for offset in within],
        )
    other = swap(packed, BOTH, count, 1)
    return rotors_step(
        slabs,
        bits,
        runs,
        tile,
        sub,
        w_in,
        w_out,
        decay[None, :],
        key_hot,
        place_hot,
        packed,
        other,
        fields,
    )


def solution(mesh):
    slabs, crosses = mesh.shape["slab"], mesh.shape["cross"]
    in_specs = (
        P(None, "slab", "cross", None),
        P(),
        P(),
        P(),
        P(),
        P("slab", None),
        P(),
        P(("slab", "cross"), None),
        P(("slab", "cross")),
        P(("slab", "cross")),
    )
    out_specs = (P(None, "slab", "cross", None), P("slab", None))
    return jax.shard_map(
        functools.partial(on_device, slabs, crosses),
        mesh=mesh,
        in_specs=in_specs,
        out_specs=out_specs,
        check_vma=False,
    )
```

```python
import functools

import jax
import jax.numpy as jnp
from jax import lax
from jax.experimental import pallas as pl
from jax.experimental.pallas import tpu as pltpu
from jax.sharding import PartitionSpec as P

TILE = 128

time_step = 0.1
viscosity = 0.3
pool_scale = 1.0 / 64.0
state_step = 0.5
force_scale = 0.5

BOTH = ("slab", "cross")
F32 = jnp.float32
BF16 = jnp.bfloat16


def lanes(rows):
    return lax.broadcasted_iota(jnp.int32, (rows, TILE), 1)


def sublanes(rows):
    return lax.broadcasted_iota(jnp.int32, (rows, TILE), 0)


def as_column(row):
    return jnp.transpose(jnp.broadcast_to(row, (TILE, TILE)))


def hot(mask):
    return jnp.where(mask, 1.0, 0.0).astype(BF16)


def slots_of(rotors, slot_ref):
    slots = jnp.zeros_like(rotors)
    for rotor in range(slot_ref.shape[0]):
        slots = jnp.where(rotors == rotor, slot_ref[rotor], slots)
    return slots


def load_kernel(
    tile_ref,
    rotor_ref,
    sub_ref,
    slot_ref,
    weight_ref,
    velocity_ref,
    x_odd_ref,
    cells,
    place_hot,
    gains,
    half_column,
    slot_hot,
    tiles,
    rotor_rows,
    sub_rows,
    slot_table,
    weights,
    sems,
    small_sems,
):
    parts, size_x, size_y, size_z = velocity_ref.shape
    columns = size_x * size_y
    halves = size_z // TILE
    groups = tile_ref.shape[0]
    rotors = slot_ref.shape[0]
    subs = weight_ref.shape[0]
    small = [
        pltpu.make_async_copy(source, target, small_sems.at[i])
        for i, (source, target) in enumerate(
            (
                (tile_ref, tiles),
                (sub_ref, sub_rows),
                (weight_ref, weights),
                (rotor_ref, rotor_rows),
                (slot_ref, slot_table),
            )
        )
    ]
    copies = [
        pltpu.make_async_copy(velocity_ref.at[c], cells.at[c], sems.at[c]) for c in range(parts)
    ]
    for copy in small + copies:
        copy.start()
    for copy in small:
        copy.wait()
    weight = weights[...]
    high = weight.astype(BF16)
    rest = weight - high.astype(F32)
    middle = rest.astype(BF16)
    low = (rest - middle.astype(F32)).astype(BF16)
    weight_parts = jnp.concatenate([high, middle, low], axis=0)
    sub_hot = []
    place_rows = tiles[...] // halves
    half_rows = tiles[...] % halves
    for group in range(groups):
        half_column[pl.ds(group * TILE, TILE), :] = as_column(half_rows[group : group + 1, :])
        place = as_column(place_rows[group : group + 1, :])
        for block in range(columns // TILE):
            place_hot[pl.ds(group * TILE, TILE), pl.ds(block * TILE, TILE)] = hot(
                place == lanes(TILE) + block * TILE
            )
        sub = as_column(sub_rows[group : group + 1, :])
        wide = jnp.concatenate([sub[:, :subs]] * 3, axis=1)
        index = lax.broadcasted_iota(jnp.int32, (TILE, subs), 1)
        sub_hot.append(hot(wide == jnp.concatenate([index] * 3, axis=1)))
    gains[...] = jnp.dot(
        jnp.concatenate(sub_hot, axis=0), weight_parts, preferred_element_type=F32
    )
    slots = slots_of(rotor_rows[...], slot_table)
    slot_hot[...] = jnp.concatenate(
        [hot(slots[g : g + 1, :] == sublanes(rotors)) for g in range(groups)], axis=1
    )
    even_x = lax.axis_index("slab") % 2 == 0
    for c in range(parts):
        copies[c].wait()
        first, last = cells[c, 0], cells[c, size_x - 1]
        x_odd_ref[c] = jnp.where(even_x, first, last).astype(BF16)


def first_half(bits):
    index = lax.axis_index("slab") * lax.axis_size("cross") + lax.axis_index("cross")
    parity = index
    for bit in range(1, bits):
        parity = parity ^ (index >> bit)
    return parity % 2 == 0


def pool_kernel(
    bits,
    cells,
    place_hot,
    gains,
    half_column,
    slot_hot,
    keep_ref,
    send_ref,
    y_even_ref,
    y_odd_ref,
    total,
):
    parts, size_x, size_y, size_z = cells.shape
    columns = size_x * size_y
    halves = size_z // TILE
    rotors = slot_hot.shape[0]
    half = half_column[...]
    even_y = lax.axis_index("cross") % 2 == 0
    flat = jnp.concatenate(
        [cells[c].reshape(columns, size_z).astype(BF16) for c in range(parts)], axis=1
    )
    found = jnp.dot(place_hot[...], flat, preferred_element_type=F32)
    for c in range(parts):
        sample = found[:, c * size_z : c * size_z + TILE]
        for h in range(1, halves):
            at = c * size_z + h * TILE
            sample = jnp.where(half == h, found[:, at : at + TILE], sample)
        weighted = sample * gains[:, c * TILE : (c + 1) * TILE]
        high = weighted.astype(BF16)
        low = (weighted - high.astype(F32)).astype(BF16)
        sums = jnp.dot(
            slot_hot[...], jnp.concatenate([high, low], axis=1), preferred_element_type=F32
        )
        total[c * rotors : (c + 1) * rotors, :] = sums[:, TILE:] + sums[:, :TILE]
        first, last = cells[c, :, 0, :], cells[c, :, size_y - 1, :]
        y_even_ref[c] = jnp.where(even_y, last, first).astype(BF16)
        y_odd_ref[c] = jnp.where(even_y, first, last).astype(BF16)
    rows = keep_ref.shape[0]
    first, second = total[:rows, :], total[rows:, :]
    keep_ref[...] = jnp.where(first_half(bits), first, second)
    send_ref[...] = jnp.where(first_half(bits), second, first)


def pack_rows(target_ref, start, blocks):
    rows, width = blocks[0].shape
    count = rows * len(blocks)
    for j in range(width // TILE):
        for k, block in enumerate(blocks):
            at = start + j * count + k * rows
            target_ref[at : at + rows, :] = block[:, j * TILE : (j + 1) * TILE]


def unpack_rows(source_ref, start, width):
    count = (source_ref.shape[0] - start) // (width // TILE)
    return jnp.concatenate(
        [source_ref[start + j * count : start + (j + 1) * count, :] for j in range(width // TILE)],
        axis=1,
    )


def stencil_kernel(planes, edges, fences, slabs, crosses, *refs):
    refs, out_ref = refs[fences:-1], refs[-1]
    velocity_ref, y_even_ref, y_odd_ref = refs[:3]
    if edges:
        x_even_ref, x_odd_ref = refs[3:]
    parts, size_x, size_y, size_z = velocity_ref.shape
    row = lax.broadcasted_iota(jnp.int32, (size_y, size_z), 0)
    lane = lax.broadcasted_iota(jnp.int32, (size_y, size_z), 1)
    slab, cross = lax.axis_index("slab"), lax.axis_index("cross")
    even_x, even_y = slab % 2 == 0, cross % 2 == 0
    inner_x = jnp.logical_and(slab > 0, slab < slabs - 1)
    inner_y = jnp.logical_and(cross > 0, cross < crosses - 1)
    souths, norths = [], []
    for c in range(parts):
        near = y_even_ref[c].astype(F32)
        far = jnp.where(inner_y, y_odd_ref[c].astype(F32), 0.0)
        souths.append(jnp.where(even_y, far, near))
        norths.append(jnp.where(even_y, near, far))
    spread = time_step * viscosity
    for at, x in enumerate(planes):
        drift = [(0.5 * time_step) * velocity_ref[d, x] for d in range(parts)]
        to_east, to_west = spread - drift[0], spread + drift[0]
        to_north, to_south = spread - drift[1], spread + drift[1]
        to_upper = jnp.where(lane == size_z - 1, 0.0, spread - drift[2])
        to_lower = jnp.where(lane == 0, 0.0, spread + drift[2])
        for c in range(parts):
            here = velocity_ref[c, x]
            if x > 0:
                west = velocity_ref[c, x - 1]
            else:
                far_x = jnp.where(inner_x, x_odd_ref[c].astype(F32), 0.0)
                west = jnp.where(even_x, far_x, x_even_ref[c].astype(F32))
            if x + 1 < size_x:
                east = velocity_ref[c, x + 1]
            else:
                far_x = jnp.where(inner_x, x_odd_ref[c].astype(F32), 0.0)
                east = jnp.where(even_x, x_even_ref[c].astype(F32), far_x)
            south = jnp.where(row == 0, souths[c][x : x + 1, :], pltpu.roll(here, 1, 0))
            north = jnp.where(
                row == size_y - 1, norths[c][x : x + 1, :], pltpu.roll(here, size_y - 1, 0)
            )
            out_ref[c, at] = (
                (1.0 - 6.0 * spread) * here
                + (to_east * east + to_west * west)
                + (to_north * north + to_south * south)
                + (to_upper * pltpu.roll(here, size_z - 1, 1) + to_lower * pltpu.roll(here, 1, 1))
            )


def key_kernel(fences, *refs):
    slot_ref, rotor_ref, sub_ref, key_ref = refs[fences:]
    rotors = slot_ref.shape[0]
    keys = sub_ref[...] // 2 * rotors + slots_of(rotor_ref[...], slot_ref)
    for group in range(keys.shape[0]):
        key = as_column(keys[group : group + 1, :])
        for block in range(key_ref.shape[1] // TILE):
            key_ref[pl.ds(group * TILE, TILE), pl.ds(block * TILE, TILE)] = hot(
                key == lanes(TILE) + block * TILE
            )


def place_kernel(halves, fence_ref, tile_ref, place_ref):
    del fence_ref
    places = tile_ref[...] // halves
    for group in range(places.shape[0]):
        for block in range(place_ref.shape[0] // TILE):
            place_ref[pl.ds(block * TILE, TILE), pl.ds(group * TILE, TILE)] = hot(
                places[group : group + 1, :] == sublanes(TILE) + block * TILE
            )


def join_kernel(bits, fences, *refs):
    keep_ref, other_ref, states_ref, cells, out_ref, x_even_ref = refs[fences:]
    even_x = lax.axis_index("slab") % 2 == 0
    for c in range(cells.shape[0]):
        face = jnp.where(even_x, cells[c, cells.shape[1] - 1], cells[c, 0])
        x_even_ref[c] = face.astype(BF16)
    rows = keep_ref.shape[0]
    out_ref[:rows, :] = keep_ref[...] + other_ref[...]
    half = states_ref.shape[1] // 2
    pack_rows(
        out_ref, rows, [jnp.where(first_half(bits), states_ref[:, :half], states_ref[:, half:])]
    )


def merge_kernel(fences, packs, shift, rows, width, pooled_rows, *refs):
    refs, out_ref = refs[fences:-1], refs[-1]
    total = refs[0][:pooled_rows, :]
    for other in refs[1:]:
        total = total + other[:pooled_rows, :]
    out_ref[:pooled_rows, :] = total
    mine = (lax.axis_index("slab") >> shift) % packs
    blocks = [unpack_rows(ref, pooled_rows, width) for ref in refs[:packs]]
    ordered = []
    for place in range(packs):
        block = blocks[0]
        for k in range(1, packs):
            block = jnp.where((mine ^ k) == place, blocks[k], block)
        ordered.append(block)
    pieces = []
    for at in range(0, blocks[0].shape[0], rows):
        pieces += [block[at : at + rows] for block in ordered]
    pack_rows(out_ref, pooled_rows, pieces)


def rotor_kernel(
    bits,
    runs,
    tile_ref,
    sub_ref,
    w_in_ref,
    w_out_ref,
    decay_ref,
    key_hot,
    place_hot,
    keep_ref,
    other_ref,
    *rest,
):
    count = 1 + max(run[2] for run in runs)
    field_refs, rest = rest[:count], rest[count:]
    out_ref, new_ref, by_slab, source_rows, wind, sems, new_sem = rest
    slabs, rows, width = by_slab.shape
    rotors = slabs * rows
    size_x, size_y, size_z = wind.shape
    parts = w_in_ref.shape[0] // TILE
    halves = size_z // TILE
    groups = tile_ref.shape[0]
    subs = w_out_ref.shape[1] // TILE
    stores = []
    for k, (first, number, which, at) in enumerate(runs):
        stores.append(
            pltpu.make_async_copy(
                field_refs[which].at[1:, pl.ds(at, number)],
                out_ref.at[1:, pl.ds(first, number)],
                sems.at[k],
            )
        )
        stores[-1].start()
    split = parts * rotors // 2
    first = first_half(bits)
    keep, other = keep_ref[:split, :], other_ref[:split, :]
    pooled = jnp.concatenate(
        [jnp.where(first, keep, other), jnp.where(first, other, keep)], axis=0
    )
    pooled = (pooled * pool_scale).astype(BF16)
    pooled = jnp.concatenate([pooled[c * rotors : (c + 1) * rotors] for c in range(parts)], axis=1)
    keep, other = [unpack_rows(ref, split, width // 2) for ref in (keep_ref, other_ref)]
    old = jnp.concatenate(
        [jnp.where(first, keep, other), jnp.where(first, other, keep)], axis=1
    )
    drive = jnp.dot(pooled, w_in_ref[...], preferred_element_type=F32)
    new = old + state_step * (drive - decay_ref[...] * old)
    for j in range(slabs):
        by_slab[j] = new[j * rows : (j + 1) * rows, :]
    own = pltpu.make_async_copy(by_slab.at[lax.axis_index("slab")], new_ref, new_sem)
    own.start()
    stores.append(own)
    new_b = new.astype(BF16)

    half_rows = tile_ref[...] % halves
    new_b = jnp.concatenate([new_b, jnp.zeros((max(TILE - rotors, 0), width), BF16)], axis=0)
    sources = jnp.dot(new_b, w_out_ref[...], preferred_element_type=F32)[:rotors].astype(BF16)
    for pair in range(subs // 2):
        source_rows[pair * rotors : (pair + 1) * rotors, :] = sources[
            :, pair * 2 * TILE : (pair + 1) * 2 * TILE
        ]
    taken = jnp.dot(key_hot[...], source_rows[...], preferred_element_type=F32)
    second = jnp.concatenate(
        [as_column(sub_ref[g : g + 1, :] % 2) for g in range(groups)], axis=0
    )
    taken = jnp.where(second == 1, taken[:, TILE:], taken[:, :TILE])
    half = jnp.concatenate([as_column(half_rows[g : g + 1, :]) for g in range(groups)], axis=0)
    spread = jnp.concatenate(
        [jnp.where(half == h, taken, 0.0).astype(BF16) for h in range(halves)], axis=1
    )
    chunks = sems.shape[0] - len(runs)
    step = size_x // chunks
    for k in range(chunks):
        forcing = jnp.dot(
            place_hot[pl.ds(k * step * size_y, step * size_y), :],
            spread,
            preferred_element_type=F32,
        ).reshape(step, size_y, size_z)
        for first, number, which, at in runs:
            begin, end = max(first, k * step), min(first + number, (k + 1) * step)
            if begin < end:
                field = field_refs[which][0, at + begin - first : at + end - first]
                wind[begin:end] = field - force_scale * forcing[begin - k * step : end - k * step]
        at = pl.ds(k * step, step)
        stores.append(
            pltpu.make_async_copy(wind.at[at], out_ref.at[0, at], sems.at[len(runs) + k])
        )
        stores[-1].start()
    for store in stores:
        store.wait()


def swap(value, axis, count, offset):
    return lax.ppermute(value, axis, [(i, i ^ offset) for i in range(count)])


def swap_pairs(value, axis, counts, first):
    slabs, crosses = counts
    if axis == "cross":
        pairs = [(i, (i + 1) % crosses) for i in range(first, crosses, 2)]
        return lax.ppermute(value, axis, pairs + [(j, i) for i, j in pairs])
    partner = {i: i + 1 for i in range(first, slabs - 1, 2)}
    partner.update({j: i for i, j in partner.items()})
    pairs = []
    for slab in range(slabs):
        for cross in range(crosses):
            to = (partner[slab], cross) if slab in partner else (slab, cross ^ 1)
            pairs.append((slab * crosses + cross, to[0] * crosses + to[1]))
    return lax.ppermute(value, BOTH, pairs)


def vmem(count):
    return [pl.BlockSpec(memory_space=pltpu.VMEM)] * count


def in_hbm(value):
    return pltpu.with_memory_space_constraint(value, pltpu.HBM)


SMEM = pl.BlockSpec(memory_space=pltpu.SMEM)
HBM = pl.BlockSpec(memory_space=pltpu.HBM)
ANY = pl.BlockSpec(memory_space=pl.ANY)


def load(tile, rotor, sub, slot_of_rotor, shape_weight, velocity):
    parts, size_x, size_y, size_z = velocity.shape
    columns = size_x * size_y
    groups = tile.shape[0]
    entries = groups * TILE
    rotors = slot_of_rotor.shape[0]
    return pl.pallas_call(
        load_kernel,
        out_shape=(
            jax.ShapeDtypeStruct((parts, size_y, size_z), BF16),
            jax.ShapeDtypeStruct(velocity.shape, F32),
            jax.ShapeDtypeStruct((entries, columns), BF16),
            jax.ShapeDtypeStruct((entries, parts * TILE), F32),
            jax.ShapeDtypeStruct((entries, TILE), jnp.int32),
            jax.ShapeDtypeStruct((rotors, entries), BF16),
        ),
        in_specs=[HBM] * 6,
        out_specs=tuple(vmem(6)),
        scratch_shapes=[
            pltpu.VMEM((groups, TILE), jnp.int32),
            pltpu.VMEM((groups, TILE), jnp.int32),
            pltpu.VMEM((groups, TILE), jnp.int32),
            pltpu.SMEM((rotors,), jnp.int32),
            pltpu.VMEM(shape_weight.shape, F32),
            pltpu.SemaphoreType.DMA((parts,)),
            pltpu.SemaphoreType.DMA((5,)),
        ],
        compiler_params=pltpu.CompilerParams(vmem_limit_bytes=8 << 20),
        cost_estimate=pl.CostEstimate(
            flops=2 * entries * columns * size_z,
            bytes_accessed=velocity.size * 4,
            transcendentals=0,
        ),
        name="load",
    )(*(in_hbm(value) for value in (tile, rotor, sub, slot_of_rotor, shape_weight, velocity)))


def pool(bits, cells, place_hot, gains, half_column, slot_hot):
    parts, size_x, size_y, size_z = cells.shape
    rows = parts * slot_hot.shape[0]
    part = jax.ShapeDtypeStruct((rows // 2, TILE), F32)
    return pl.pallas_call(
        functools.partial(pool_kernel, bits),
        out_shape=(
            part,
            part,
            jax.ShapeDtypeStruct((parts, size_x, size_z), BF16),
            jax.ShapeDtypeStruct((parts, size_x, size_z), BF16),
        ),
        in_specs=vmem(5),
        out_specs=tuple(vmem(4)),
        scratch_shapes=[pltpu.VMEM((rows, TILE), F32)],
        compiler_params=pltpu.CompilerParams(vmem_limit_bytes=12 << 20),
        cost_estimate=pl.CostEstimate(
            flops=2 * place_hot.size * parts * size_z, bytes_accessed=cells.size * 4, transcendentals=0
        ),
        name="pool",
    )(cells, place_hot, gains, half_column, slot_hot)


def stencil(planes, fences, slabs, crosses, velocity, halos):
    parts, size_x, size_y, size_z = velocity.shape
    edges = len(halos) > 2
    return pl.pallas_call(
        functools.partial(stencil_kernel, planes, edges, len(fences), slabs, crosses),
        out_shape=jax.ShapeDtypeStruct((parts, len(planes), size_y, size_z), F32),
        in_specs=[ANY] * len(fences) + vmem(1 + len(halos)),
        out_specs=vmem(1)[0],
        compiler_params=pltpu.CompilerParams(vmem_limit_bytes=4 << 20),
        cost_estimate=pl.CostEstimate(
            flops=1000 * velocity.size * len(planes) // size_x,
            bytes_accessed=8 * velocity.size * len(planes) // size_x,
            transcendentals=0,
        ),
        name="stencil",
    )(*fences, velocity, *halos)


def key_matrix(fences, slot_of_rotor, rotor, sub, keys):
    entries = rotor.shape[0] * TILE
    return pl.pallas_call(
        functools.partial(key_kernel, len(fences)),
        out_shape=jax.ShapeDtypeStruct((entries, keys), BF16),
        in_specs=[ANY] * len(fences) + [SMEM] + vmem(2),
        out_specs=vmem(1)[0],
        compiler_params=pltpu.CompilerParams(vmem_limit_bytes=4 << 20),
        cost_estimate=pl.CostEstimate(
            flops=1000 * entries * keys, bytes_accessed=2 * entries * keys, transcendentals=0
        ),
        name="keys",
    )(*fences, slot_of_rotor, rotor, sub)


def place_matrix(fence, tile, columns, halves):
    entries = tile.shape[0] * TILE
    return pl.pallas_call(
        functools.partial(place_kernel, halves),
        out_shape=jax.ShapeDtypeStruct((columns, entries), BF16),
        in_specs=[ANY] + vmem(1),
        out_specs=vmem(1)[0],
        compiler_params=pltpu.CompilerParams(vmem_limit_bytes=4 << 20),
        cost_estimate=pl.CostEstimate(
            flops=1000 * entries * columns, bytes_accessed=2 * entries * columns, transcendentals=0
        ),
        name="places",
    )(fence, tile)


def join(bits, fences, keep, other, states, cells):
    parts, _, size_y, size_z = cells.shape
    rows = keep.shape[0] + states.size // 2 // TILE
    return pl.pallas_call(
        functools.partial(join_kernel, bits, len(fences)),
        out_shape=(
            jax.ShapeDtypeStruct((rows, TILE), F32),
            jax.ShapeDtypeStruct((parts, size_y, size_z), BF16),
        ),
        in_specs=[ANY] * len(fences) + vmem(4),
        out_specs=tuple(vmem(2)),
        compiler_params=pltpu.CompilerParams(vmem_limit_bytes=4 << 20),
        name="join",
    )(*fences, keep, other, states, cells)


def merge(fences, shift, rows, width, pooled_rows, packed, pooled):
    total = pooled_rows + len(packed) * (packed[0].shape[0] - pooled_rows)
    return pl.pallas_call(
        functools.partial(
            merge_kernel, len(fences), len(packed), shift, rows, width, pooled_rows
        ),
        out_shape=jax.ShapeDtypeStruct((total, TILE), F32),
        in_specs=[ANY] * len(fences) + vmem(len(packed) + len(pooled)),
        out_specs=vmem(1)[0],
        compiler_params=pltpu.CompilerParams(vmem_limit_bytes=4 << 20),
        name="merge",
    )(*fences, *packed, *pooled)


def rotors_step(
    slabs, bits, runs, tile, sub, w_in, w_out, decay, key_hot, place_hot, keep, other, fields
):
    width = w_in.shape[1]
    parts, _, size_y, size_z = fields[0].shape
    size_x = sum(field.shape[1] for field in fields)
    keys = key_hot.shape[1]
    rows = keys // (w_out.shape[1] // (2 * TILE)) // slabs
    chunks = 2
    return pl.pallas_call(
        functools.partial(rotor_kernel, bits, runs),
        out_shape=(
            jax.ShapeDtypeStruct((parts, size_x, size_y, size_z), F32),
            jax.ShapeDtypeStruct((rows, width), F32),
        ),
        in_specs=vmem(9 + len(fields)),
        out_specs=(HBM, HBM),
        scratch_shapes=[
            pltpu.VMEM((slabs, rows, width), F32),
            pltpu.VMEM((keys, 2 * TILE), BF16),
            pltpu.VMEM((size_x, size_y, size_z), F32),
            pltpu.SemaphoreType.DMA((len(runs) + chunks,)),
            pltpu.SemaphoreType.DMA,
        ],
        compiler_params=pltpu.CompilerParams(vmem_limit_bytes=10 << 20),
        cost_estimate=pl.CostEstimate(
            flops=4 * place_hot.size * size_z, bytes_accessed=w_out.size * 2, transcendentals=0
        ),
        name="rotors",
    )(tile, sub, w_in, w_out, decay, key_hot, place_hot, keep, other, *fields)


def on_device(
    slabs,
    crosses,
    velocity,
    shape_weight,
    w_in,
    w_out,
    decay,
    rotor_states,
    slot_of_rotor,
    entry_rotor,
    entry_tile,
    entry_sub,
):
    size_x, size_y, size_z = velocity.shape[1:]
    entries = entry_tile.shape[0]
    width = w_in.shape[1]
    count = slabs * crosses
    tile = entry_tile.reshape(entries // TILE, TILE)
    rotor = entry_rotor.reshape(entries // TILE, TILE)
    sub = entry_sub.reshape(entries // TILE, TILE)

    bits = count.bit_length() - 1
    x_odd, cells, *loaded = load(tile, rotor, sub, slot_of_rotor, shape_weight, velocity)
    x_odd = swap_pairs(x_odd, "slab", (slabs, crosses), 1)
    keep, send, y_even, y_odd = pool(bits, cells, *loaded)
    y_even = swap_pairs(y_even, "cross", (slabs, crosses), 0)
    y_odd = swap_pairs(y_odd, "cross", (slabs, crosses), 1)
    pooled_rows = keep.shape[0]

    middle = size_x // 2
    inner, outer = tuple(range(1, middle)), (0,) + tuple(range(middle, size_x))
    runs = ((1, middle - 1, 0, 0), (0, 1, 1, 0), (middle, size_x - middle, 1, 1))
    packed, x_even = join(bits, (), keep, swap(send, BOTH, count, 1), rotor_states, cells)
    x_even = swap_pairs(x_even, "slab", (slabs, crosses), 0)
    slab_bit = crosses.bit_length() - 1
    steps = [tuple(range(b, min(b + 2, bits))) for b in range(1, bits, 2)][::-1]
    fields = []
    for step in steps:
        made = []
        if step == steps[0]:
            keys = w_out.shape[1] // (2 * TILE) * slot_of_rotor.shape[0]
            key_hot = key_matrix((packed, x_odd), slot_of_rotor, rotor, sub, keys)
            fields.append(stencil(inner, (packed,), slabs, crosses, cells, (y_even, y_odd)))
            made += [key_hot, fields[-1]]
        if step == steps[-1]:
            place_hot = place_matrix(packed, tile, size_x * size_y, size_z // TILE)
            halos = (y_even, y_odd, x_even, x_odd)
            fields.append(stencil(outer, (packed,), slabs, crosses, cells, halos))
            made += [place_hot, fields[-1]]
        slab_bits = [b for b in step if b >= slab_bit]
        across = [1 << b | 1 for b in slab_bits]
        if len(slab_bits) == 2:
            across.append(sum(1 << b for b in step))
            within = []
        else:
            within = [1 << b | 1 for b in step if b < slab_bit]
            within += [sum(1 << b for b in step)] if len(step) == 2 else []
        sums = packed[:pooled_rows]
        packed = merge(
            made,
            slab_bits[0] - slab_bit,
            rotor_states.shape[0],
            width // 2,
            pooled_rows,
            [packed] + [swap(packed, BOTH, count, offset) for offset in across],
            [swap(sums, BOTH, count, offset) for offset in within],
        )
    other = swap(packed, BOTH, count, 1)
    return rotors_step(
        slabs,
        bits,
        runs,
        tile,
        sub,
        w_in,
        w_out,
        decay[None, :],
        key_hot,
        place_hot,
        packed,
        other,
        fields,
    )


def solution(mesh):
    slabs, crosses = mesh.shape["slab"], mesh.shape["cross"]
    in_specs = (
        P(None, "slab", "cross", None),
        P(),
        P(),
        P(),
        P(),
        P("slab", None),
        P(),
        P(("slab", "cross"), None),
        P(("slab", "cross")),
        P(("slab", "cross")),
    )
    out_specs = (P(None, "slab", "cross", None), P("slab", None))
    return jax.shard_map(
        functools.partial(on_device, slabs, crosses),
        mesh=mesh,
        in_specs=in_specs,
        out_specs=out_specs,
        check_vma=False,
    )
```

```python
import functools

import jax
import jax.numpy as jnp
from jax import lax
from jax.experimental import pallas as pl
from jax.experimental.pallas import tpu as pltpu
from jax.sharding import PartitionSpec as P

TILE = 128

time_step = 0.1
viscosity = 0.3
pool_scale = 1.0 / 64.0
state_step = 0.5
force_scale = 0.5

BOTH = ("slab", "cross")
F32 = jnp.float32
BF16 = jnp.bfloat16


def lanes(rows):
    return lax.broadcasted_iota(jnp.int32, (rows, TILE), 1)


def sublanes(rows):
    return lax.broadcasted_iota(jnp.int32, (rows, TILE), 0)


def as_column(row):
    return jnp.transpose(jnp.broadcast_to(row, (TILE, TILE)))


def hot(mask):
    return jnp.where(mask, 1.0, 0.0).astype(BF16)


def slots_of(rotors, slot_ref):
    slots = jnp.zeros_like(rotors)
    for rotor in range(slot_ref.shape[0]):
        slots = jnp.where(rotors == rotor, slot_ref[rotor], slots)
    return slots


def load_kernel(
    tile_ref,
    rotor_ref,
    sub_ref,
    slot_ref,
    weight_ref,
    velocity_ref,
    x_odd_ref,
    slots_ref,
    cells,
    place_hot,
    gains,
    half_column,
    slot_hot,
    tiles,
    rotor_rows,
    sub_rows,
    slot_table,
    weights,
    sems,
    small_sems,
):
    parts, size_x, size_y, size_z = velocity_ref.shape
    columns = size_x * size_y
    halves = size_z // TILE
    groups = tile_ref.shape[0]
    rotors = slot_ref.shape[0]
    subs = weight_ref.shape[0]
    small = [
        pltpu.make_async_copy(source, target, small_sems.at[i])
        for i, (source, target) in enumerate(
            (
                (tile_ref, tiles),
                (sub_ref, sub_rows),
                (weight_ref, weights),
                (rotor_ref, rotor_rows),
                (slot_ref, slot_table),
            )
        )
    ]
    copies = [
        pltpu.make_async_copy(velocity_ref.at[c], cells.at[c], sems.at[c]) for c in range(parts)
    ]
    for copy in small + copies:
        copy.start()
    for copy in small:
        copy.wait()
    weight = weights[...]
    high = weight.astype(BF16)
    rest = weight - high.astype(F32)
    middle = rest.astype(BF16)
    low = (rest - middle.astype(F32)).astype(BF16)
    weight_parts = jnp.concatenate([high, middle, low], axis=0)
    sub_hot = []
    place_rows = tiles[...] // halves
    half_rows = tiles[...] % halves
    for group in range(groups):
        half_column[pl.ds(group * TILE, TILE), :] = as_column(half_rows[group : group + 1, :])
        place = as_column(place_rows[group : group + 1, :])
        for block in range(columns // TILE):
            place_hot[pl.ds(group * TILE, TILE), pl.ds(block * TILE, TILE)] = hot(
                place == lanes(TILE) + block * TILE
            )
        sub = as_column(sub_rows[group : group + 1, :])
        wide = jnp.concatenate([sub[:, :subs]] * 3, axis=1)
        index = lax.broadcasted_iota(jnp.int32, (TILE, subs), 1)
        sub_hot.append(hot(wide == jnp.concatenate([index] * 3, axis=1)))
    gains[...] = jnp.dot(
        jnp.concatenate(sub_hot, axis=0), weight_parts, preferred_element_type=F32
    )
    slots = slots_of(rotor_rows[...], slot_table)
    slots_ref[...] = slots
    slot_hot[...] = jnp.concatenate(
        [hot(slots[g : g + 1, :] == sublanes(rotors)) for g in range(groups)], axis=1
    )
    even_x = lax.axis_index("slab") % 2 == 0
    for c in range(parts):
        copies[c].wait()
        first, last = cells[c, 0], cells[c, size_x - 1]
        x_odd_ref[c] = jnp.where(even_x, first, last).astype(BF16)


def first_half(bits):
    index = lax.axis_index("slab") * lax.axis_size("cross") + lax.axis_index("cross")
    parity = index
    for bit in range(1, bits):
        parity = parity ^ (index >> bit)
    return parity % 2 == 0


def pool_kernel(
    bits,
    cells,
    place_hot,
    gains,
    half_column,
    slot_hot,
    keep_ref,
    send_ref,
    y_even_ref,
    y_odd_ref,
    total,
):
    parts, size_x, size_y, size_z = cells.shape
    columns = size_x * size_y
    halves = size_z // TILE
    rotors = slot_hot.shape[0]
    half = half_column[...]
    even_y = lax.axis_index("cross") % 2 == 0
    flat = jnp.concatenate(
        [cells[c].reshape(columns, size_z).astype(BF16) for c in range(parts)], axis=1
    )
    found = jnp.dot(place_hot[...], flat, preferred_element_type=F32)
    for c in range(parts):
        sample = found[:, c * size_z : c * size_z + TILE]
        for h in range(1, halves):
            at = c * size_z + h * TILE
            sample = jnp.where(half == h, found[:, at : at + TILE], sample)
        weighted = sample * gains[:, c * TILE : (c + 1) * TILE]
        high = weighted.astype(BF16)
        low = (weighted - high.astype(F32)).astype(BF16)
        sums = jnp.dot(
            slot_hot[...], jnp.concatenate([high, low], axis=1), preferred_element_type=F32
        )
        total[c * rotors : (c + 1) * rotors, :] = sums[:, TILE:] + sums[:, :TILE]
        first, last = cells[c, :, 0, :], cells[c, :, size_y - 1, :]
        y_even_ref[c] = jnp.where(even_y, last, first).astype(BF16)
        y_odd_ref[c] = jnp.where(even_y, first, last).astype(BF16)
    rows = keep_ref.shape[0]
    first, second = total[:rows, :], total[rows:, :]
    keep_ref[...] = jnp.where(first_half(bits), first, second)
    send_ref[...] = jnp.where(first_half(bits), second, first)


def pack_rows(target_ref, start, blocks):
    rows, width = blocks[0].shape
    count = rows * len(blocks)
    for j in range(width // TILE):
        for k, block in enumerate(blocks):
            at = start + j * count + k * rows
            target_ref[at : at + rows, :] = block[:, j * TILE : (j + 1) * TILE]


def unpack_rows(source_ref, start, width):
    count = (source_ref.shape[0] - start) // (width // TILE)
    return jnp.concatenate(
        [source_ref[start + j * count : start + (j + 1) * count, :] for j in range(width // TILE)],
        axis=1,
    )


def stencil_kernel(planes, edges, fences, slabs, crosses, *refs):
    refs, out_ref = refs[fences:-1], refs[-1]
    velocity_ref, y_even_ref, y_odd_ref = refs[:3]
    if edges:
        x_even_ref, x_odd_ref = refs[3:]
    parts, size_x, size_y, size_z = velocity_ref.shape
    row = lax.broadcasted_iota(jnp.int32, (size_y, size_z), 0)
    lane = lax.broadcasted_iota(jnp.int32, (size_y, size_z), 1)
    slab, cross = lax.axis_index("slab"), lax.axis_index("cross")
    even_x, even_y = slab % 2 == 0, cross % 2 == 0
    inner_x = jnp.logical_and(slab > 0, slab < slabs - 1)
    inner_y = jnp.logical_and(cross > 0, cross < crosses - 1)
    souths, norths = [], []
    for c in range(parts):
        near = y_even_ref[c].astype(F32)
        far = jnp.where(inner_y, y_odd_ref[c].astype(F32), 0.0)
        souths.append(jnp.where(even_y, far, near))
        norths.append(jnp.where(even_y, near, far))
    spread = time_step * viscosity
    for at, x in enumerate(planes):
        drift = [(0.5 * time_step) * velocity_ref[d, x] for d in range(parts)]
        to_east, to_west = spread - drift[0], spread + drift[0]
        to_north, to_south = spread - drift[1], spread + drift[1]
        to_upper = jnp.where(lane == size_z - 1, 0.0, spread - drift[2])
        to_lower = jnp.where(lane == 0, 0.0, spread + drift[2])
        for c in range(parts):
            here = velocity_ref[c, x]
            if x > 0:
                west = velocity_ref[c, x - 1]
            else:
                far_x = jnp.where(inner_x, x_odd_ref[c].astype(F32), 0.0)
                west = jnp.where(even_x, far_x, x_even_ref[c].astype(F32))
            if x + 1 < size_x:
                east = velocity_ref[c, x + 1]
            else:
                far_x = jnp.where(inner_x, x_odd_ref[c].astype(F32), 0.0)
                east = jnp.where(even_x, x_even_ref[c].astype(F32), far_x)
            south = jnp.where(row == 0, souths[c][x : x + 1, :], pltpu.roll(here, 1, 0))
            north = jnp.where(
                row == size_y - 1, norths[c][x : x + 1, :], pltpu.roll(here, size_y - 1, 0)
            )
            out_ref[c, at] = (
                (1.0 - 6.0 * spread) * here
                + (to_east * east + to_west * west)
                + (to_north * north + to_south * south)
                + (to_upper * pltpu.roll(here, size_z - 1, 1) + to_lower * pltpu.roll(here, 1, 1))
            )


def key_kernel(rotors, fences, *refs):
    slots_ref, sub_ref, key_ref = refs[fences:]
    keys = sub_ref[...] // 2 * rotors + slots_ref[...]
    for group in range(keys.shape[0]):
        key = as_column(keys[group : group + 1, :])
        for block in range(key_ref.shape[1] // TILE):
            key_ref[pl.ds(group * TILE, TILE), pl.ds(block * TILE, TILE)] = hot(
                key == lanes(TILE) + block * TILE
            )


def place_kernel(halves, fence_ref, tile_ref, place_ref):
    del fence_ref
    places = tile_ref[...] // halves
    for group in range(places.shape[0]):
        for block in range(place_ref.shape[0] // TILE):
            place_ref[pl.ds(block * TILE, TILE), pl.ds(group * TILE, TILE)] = hot(
                places[group : group + 1, :] == sublanes(TILE) + block * TILE
            )


def join_kernel(bits, fences, *refs):
    keep_ref, other_ref, states_ref, cells, out_ref, x_even_ref = refs[fences:]
    even_x = lax.axis_index("slab") % 2 == 0
    for c in range(cells.shape[0]):
        face = jnp.where(even_x, cells[c, cells.shape[1] - 1], cells[c, 0])
        x_even_ref[c] = face.astype(BF16)
    rows = keep_ref.shape[0]
    out_ref[:rows, :] = keep_ref[...] + other_ref[...]
    half = states_ref.shape[1] // 2
    pack_rows(
        out_ref, rows, [jnp.where(first_half(bits), states_ref[:, :half], states_ref[:, half:])]
    )


def merge_kernel(fences, packs, shift, rows, width, pooled_rows, *refs):
    refs, out_ref = refs[fences:-1], refs[-1]
    total = refs[0][:pooled_rows, :]
    for other in refs[1:]:
        total = total + other[:pooled_rows, :]
    out_ref[:pooled_rows, :] = total
    mine = (lax.axis_index("slab") >> shift) % packs
    blocks = [unpack_rows(ref, pooled_rows, width) for ref in refs[:packs]]
    ordered = []
    for place in range(packs):
        block = blocks[0]
        for k in range(1, packs):
            block = jnp.where((mine ^ k) == place, blocks[k], block)
        ordered.append(block)
    pieces = []
    for at in range(0, blocks[0].shape[0], rows):
        pieces += [block[at : at + rows] for block in ordered]
    pack_rows(out_ref, pooled_rows, pieces)


def rotor_kernel(
    bits,
    runs,
    tile_ref,
    sub_ref,
    w_in_ref,
    w_out_ref,
    decay_ref,
    key_hot,
    place_hot,
    keep_ref,
    other_ref,
    *rest,
):
    count = 1 + max(run[2] for run in runs)
    field_refs, rest = rest[:count], rest[count:]
    out_ref, new_ref, by_slab, source_rows, wind, sems, new_sem = rest
    slabs, rows, width = by_slab.shape
    rotors = slabs * rows
    size_x, size_y, size_z = wind.shape
    parts = w_in_ref.shape[0] // TILE
    halves = size_z // TILE
    groups = tile_ref.shape[0]
    subs = w_out_ref.shape[1] // TILE
    stores = []
    for k, (first, number, which, at) in enumerate(runs):
        stores.append(
            pltpu.make_async_copy(
                field_refs[which].at[1:, pl.ds(at, number)],
                out_ref.at[1:, pl.ds(first, number)],
                sems.at[k],
            )
        )
        stores[-1].start()
    split = parts * rotors // 2
    first = first_half(bits)
    keep, other = keep_ref[:split, :], other_ref[:split, :]
    pooled = jnp.concatenate(
        [jnp.where(first, keep, other), jnp.where(first, other, keep)], axis=0
    )
    pooled = (pooled * pool_scale).astype(BF16)
    pooled = jnp.concatenate([pooled[c * rotors : (c + 1) * rotors] for c in range(parts)], axis=1)
    keep, other = [unpack_rows(ref, split, width // 2) for ref in (keep_ref, other_ref)]
    old = jnp.concatenate(
        [jnp.where(first, keep, other), jnp.where(first, other, keep)], axis=1
    )
    drive = jnp.dot(pooled, w_in_ref[...], preferred_element_type=F32)
    new = old + state_step * (drive - decay_ref[...] * old)
    for j in range(slabs):
        by_slab[j] = new[j * rows : (j + 1) * rows, :]
    own = pltpu.make_async_copy(by_slab.at[lax.axis_index("slab")], new_ref, new_sem)
    own.start()
    stores.append(own)
    new_b = new.astype(BF16)

    half_rows = tile_ref[...] % halves
    new_b = jnp.concatenate([new_b, jnp.zeros((max(TILE - rotors, 0), width), BF16)], axis=0)
    sources = jnp.dot(new_b, w_out_ref[...], preferred_element_type=F32)[:rotors].astype(BF16)
    for pair in range(subs // 2):
        source_rows[pair * rotors : (pair + 1) * rotors, :] = sources[
            :, pair * 2 * TILE : (pair + 1) * 2 * TILE
        ]
    taken = jnp.dot(key_hot[...], source_rows[...], preferred_element_type=F32)
    second = jnp.concatenate(
        [as_column(sub_ref[g : g + 1, :] % 2) for g in range(groups)], axis=0
    )
    taken = jnp.where(second == 1, taken[:, TILE:], taken[:, :TILE])
    half = jnp.concatenate([as_column(half_rows[g : g + 1, :]) for g in range(groups)], axis=0)
    spread = jnp.concatenate(
        [jnp.where(half == h, taken, 0.0).astype(BF16) for h in range(halves)], axis=1
    )
    chunks = sems.shape[0] - len(runs)
    step = size_x // chunks
    for k in range(chunks):
        forcing = jnp.dot(
            place_hot[pl.ds(k * step * size_y, step * size_y), :],
            spread,
            preferred_element_type=F32,
        ).reshape(step, size_y, size_z)
        for first, number, which, at in runs:
            begin, end = max(first, k * step), min(first + number, (k + 1) * step)
            if begin < end:
                field = field_refs[which][0, at + begin - first : at + end - first]
                wind[begin:end] = field - force_scale * forcing[begin - k * step : end - k * step]
        at = pl.ds(k * step, step)
        stores.append(
            pltpu.make_async_copy(wind.at[at], out_ref.at[0, at], sems.at[len(runs) + k])
        )
        stores[-1].start()
    for store in stores:
        store.wait()


def swap(value, axis, count, offset):
    return lax.ppermute(value, axis, [(i, i ^ offset) for i in range(count)])


def swap_pairs(value, axis, counts, first):
    slabs, crosses = counts
    if axis == "cross":
        pairs = [(i, (i + 1) % crosses) for i in range(first, crosses, 2)]
        return lax.ppermute(value, axis, pairs + [(j, i) for i, j in pairs])
    partner = {i: i + 1 for i in range(first, slabs - 1, 2)}
    partner.update({j: i for i, j in partner.items()})
    pairs = []
    for slab in range(slabs):
        for cross in range(crosses):
            to = (partner[slab], cross) if slab in partner else (slab, cross ^ 1)
            pairs.append((slab * crosses + cross, to[0] * crosses + to[1]))
    return lax.ppermute(value, BOTH, pairs)


def vmem(count):
    return [pl.BlockSpec(memory_space=pltpu.VMEM)] * count


def in_hbm(value):
    return pltpu.with_memory_space_constraint(value, pltpu.HBM)


SMEM = pl.BlockSpec(memory_space=pltpu.SMEM)
HBM = pl.BlockSpec(memory_space=pltpu.HBM)
ANY = pl.BlockSpec(memory_space=pl.ANY)


def load(tile, rotor, sub, slot_of_rotor, shape_weight, velocity):
    parts, size_x, size_y, size_z = velocity.shape
    columns = size_x * size_y
    groups = tile.shape[0]
    entries = groups * TILE
    rotors = slot_of_rotor.shape[0]
    return pl.pallas_call(
        load_kernel,
        out_shape=(
            jax.ShapeDtypeStruct((parts, size_y, size_z), BF16),
            jax.ShapeDtypeStruct((groups, TILE), jnp.int32),
            jax.ShapeDtypeStruct(velocity.shape, F32),
            jax.ShapeDtypeStruct((entries, columns), BF16),
            jax.ShapeDtypeStruct((entries, parts * TILE), F32),
            jax.ShapeDtypeStruct((entries, TILE), jnp.int32),
            jax.ShapeDtypeStruct((rotors, entries), BF16),
        ),
        in_specs=[HBM] * 6,
        out_specs=tuple(vmem(7)),
        scratch_shapes=[
            pltpu.VMEM((groups, TILE), jnp.int32),
            pltpu.VMEM((groups, TILE), jnp.int32),
            pltpu.VMEM((groups, TILE), jnp.int32),
            pltpu.SMEM((rotors,), jnp.int32),
            pltpu.VMEM(shape_weight.shape, F32),
            pltpu.SemaphoreType.DMA((parts,)),
            pltpu.SemaphoreType.DMA((5,)),
        ],
        compiler_params=pltpu.CompilerParams(vmem_limit_bytes=8 << 20),
        cost_estimate=pl.CostEstimate(
            flops=2 * entries * columns * size_z,
            bytes_accessed=velocity.size * 4,
            transcendentals=0,
        ),
        name="load",
    )(*(in_hbm(value) for value in (tile, rotor, sub, slot_of_rotor, shape_weight, velocity)))


def pool(bits, cells, place_hot, gains, half_column, slot_hot):
    parts, size_x, size_y, size_z = cells.shape
    rows = parts * slot_hot.shape[0]
    part = jax.ShapeDtypeStruct((rows // 2, TILE), F32)
    return pl.pallas_call(
        functools.partial(pool_kernel, bits),
        out_shape=(
            part,
            part,
            jax.ShapeDtypeStruct((parts, size_x, size_z), BF16),
            jax.ShapeDtypeStruct((parts, size_x, size_z), BF16),
        ),
        in_specs=vmem(5),
        out_specs=tuple(vmem(4)),
        scratch_shapes=[pltpu.VMEM((rows, TILE), F32)],
        compiler_params=pltpu.CompilerParams(vmem_limit_bytes=12 << 20),
        cost_estimate=pl.CostEstimate(
            flops=2 * place_hot.size * parts * size_z, bytes_accessed=cells.size * 4, transcendentals=0
        ),
        name="pool",
    )(cells, place_hot, gains, half_column, slot_hot)


def stencil(planes, fences, slabs, crosses, velocity, halos):
    parts, size_x, size_y, size_z = velocity.shape
    edges = len(halos) > 2
    return pl.pallas_call(
        functools.partial(stencil_kernel, planes, edges, len(fences), slabs, crosses),
        out_shape=jax.ShapeDtypeStruct((parts, len(planes), size_y, size_z), F32),
        in_specs=[ANY] * len(fences) + vmem(1 + len(halos)),
        out_specs=vmem(1)[0],
        compiler_params=pltpu.CompilerParams(vmem_limit_bytes=4 << 20),
        cost_estimate=pl.CostEstimate(
            flops=1000 * velocity.size * len(planes) // size_x,
            bytes_accessed=8 * velocity.size * len(planes) // size_x,
            transcendentals=0,
        ),
        name="stencil",
    )(*fences, velocity, *halos)


def key_matrix(rotors, fences, slots, sub, keys):
    entries = slots.shape[0] * TILE
    return pl.pallas_call(
        functools.partial(key_kernel, rotors, len(fences)),
        out_shape=jax.ShapeDtypeStruct((entries, keys), BF16),
        in_specs=[ANY] * len(fences) + vmem(2),
        out_specs=vmem(1)[0],
        compiler_params=pltpu.CompilerParams(vmem_limit_bytes=4 << 20),
        cost_estimate=pl.CostEstimate(
            flops=1000 * entries * keys, bytes_accessed=2 * entries * keys, transcendentals=0
        ),
        name="keys",
    )(*fences, slots, sub)


def place_matrix(fence, tile, columns, halves):
    entries = tile.shape[0] * TILE
    return pl.pallas_call(
        functools.partial(place_kernel, halves),
        out_shape=jax.ShapeDtypeStruct((columns, entries), BF16),
        in_specs=[ANY] + vmem(1),
        out_specs=vmem(1)[0],
        compiler_params=pltpu.CompilerParams(vmem_limit_bytes=4 << 20),
        cost_estimate=pl.CostEstimate(
            flops=1000 * entries * columns, bytes_accessed=2 * entries * columns, transcendentals=0
        ),
        name="places",
    )(fence, tile)


def join(bits, fences, keep, other, states, cells):
    parts, _, size_y, size_z = cells.shape
    rows = keep.shape[0] + states.size // 2 // TILE
    return pl.pallas_call(
        functools.partial(join_kernel, bits, len(fences)),
        out_shape=(
            jax.ShapeDtypeStruct((rows, TILE), F32),
            jax.ShapeDtypeStruct((parts, size_y, size_z), BF16),
        ),
        in_specs=[ANY] * len(fences) + vmem(4),
        out_specs=tuple(vmem(2)),
        compiler_params=pltpu.CompilerParams(vmem_limit_bytes=4 << 20),
        name="join",
    )(*fences, keep, other, states, cells)


def merge(fences, shift, rows, width, pooled_rows, packed, pooled):
    total = pooled_rows + len(packed) * (packed[0].shape[0] - pooled_rows)
    return pl.pallas_call(
        functools.partial(
            merge_kernel, len(fences), len(packed), shift, rows, width, pooled_rows
        ),
        out_shape=jax.ShapeDtypeStruct((total, TILE), F32),
        in_specs=[ANY] * len(fences) + vmem(len(packed) + len(pooled)),
        out_specs=vmem(1)[0],
        compiler_params=pltpu.CompilerParams(vmem_limit_bytes=4 << 20),
        name="merge",
    )(*fences, *packed, *pooled)


def rotors_step(
    slabs, bits, runs, tile, sub, w_in, w_out, decay, key_hot, place_hot, keep, other, fields
):
    width = w_in.shape[1]
    parts, _, size_y, size_z = fields[0].shape
    size_x = sum(field.shape[1] for field in fields)
    keys = key_hot.shape[1]
    rows = keys // (w_out.shape[1] // (2 * TILE)) // slabs
    chunks = 2
    return pl.pallas_call(
        functools.partial(rotor_kernel, bits, runs),
        out_shape=(
            jax.ShapeDtypeStruct((parts, size_x, size_y, size_z), F32),
            jax.ShapeDtypeStruct((rows, width), F32),
        ),
        in_specs=vmem(9 + len(fields)),
        out_specs=(HBM, HBM),
        scratch_shapes=[
            pltpu.VMEM((slabs, rows, width), F32),
            pltpu.VMEM((keys, 2 * TILE), BF16),
            pltpu.VMEM((size_x, size_y, size_z), F32),
            pltpu.SemaphoreType.DMA((len(runs) + chunks,)),
            pltpu.SemaphoreType.DMA,
        ],
        compiler_params=pltpu.CompilerParams(vmem_limit_bytes=10 << 20),
        cost_estimate=pl.CostEstimate(
            flops=4 * place_hot.size * size_z, bytes_accessed=w_out.size * 2, transcendentals=0
        ),
        name="rotors",
    )(tile, sub, w_in, w_out, decay, key_hot, place_hot, keep, other, *fields)


def on_device(
    slabs,
    crosses,
    velocity,
    shape_weight,
    w_in,
    w_out,
    decay,
    rotor_states,
    slot_of_rotor,
    entry_rotor,
    entry_tile,
    entry_sub,
):
    size_x, size_y, size_z = velocity.shape[1:]
    entries = entry_tile.shape[0]
    width = w_in.shape[1]
    count = slabs * crosses
    tile = entry_tile.reshape(entries // TILE, TILE)
    rotor = entry_rotor.reshape(entries // TILE, TILE)
    sub = entry_sub.reshape(entries // TILE, TILE)

    bits = count.bit_length() - 1
    x_odd, slots, cells, *loaded = load(tile, rotor, sub, slot_of_rotor, shape_weight, velocity)
    x_odd = swap_pairs(x_odd, "slab", (slabs, crosses), 1)
    keep, send, y_even, y_odd = pool(bits, cells, *loaded)
    y_even = swap_pairs(y_even, "cross", (slabs, crosses), 0)
    y_odd = swap_pairs(y_odd, "cross", (slabs, crosses), 1)
    pooled_rows = keep.shape[0]

    middle = size_x // 2
    inner, outer = tuple(range(1, middle)), (0,) + tuple(range(middle, size_x))
    runs = ((1, middle - 1, 0, 0), (0, 1, 1, 0), (middle, size_x - middle, 1, 1))
    packed, x_even = join(bits, (), keep, swap(send, BOTH, count, 1), rotor_states, cells)
    x_even = swap_pairs(x_even, "slab", (slabs, crosses), 0)
    slab_bit = crosses.bit_length() - 1
    steps = [tuple(range(b, min(b + 2, bits))) for b in range(1, bits, 2)][::-1]
    fields = []
    for step in steps:
        made = []
        if step == steps[0]:
            rotors = slot_of_rotor.shape[0]
            keys = w_out.shape[1] // (2 * TILE) * rotors
            key_hot = key_matrix(rotors, (packed, x_odd), slots, sub, keys)
            fields.append(stencil(inner, (packed,), slabs, crosses, cells, (y_even, y_odd)))
            made += [key_hot, fields[-1]]
        if step == steps[-1]:
            place_hot = place_matrix(packed, tile, size_x * size_y, size_z // TILE)
            halos = (y_even, y_odd, x_even, x_odd)
            fields.append(stencil(outer, (packed,), slabs, crosses, cells, halos))
            made += [place_hot, fields[-1]]
        slab_bits = [b for b in step if b >= slab_bit]
        across = [1 << b | 1 for b in slab_bits]
        if len(slab_bits) == 2:
            across.append(sum(1 << b for b in step))
            within = []
        else:
            within = [1 << b | 1 for b in step if b < slab_bit]
            within += [sum(1 << b for b in step)] if len(step) == 2 else []
        sums = packed[:pooled_rows]
        packed = merge(
            made,
            slab_bits[0] - slab_bit,
            rotor_states.shape[0],
            width // 2,
            pooled_rows,
            [packed] + [swap(packed, BOTH, count, offset) for offset in across],
            [swap(sums, BOTH, count, offset) for offset in within],
        )
    other = swap(packed, BOTH, count, 1)
    return rotors_step(
        slabs,
        bits,
        runs,
        tile,
        sub,
        w_in,
        w_out,
        decay[None, :],
        key_hot,
        place_hot,
        packed,
        other,
        fields,
    )


def solution(mesh):
    slabs, crosses = mesh.shape["slab"], mesh.shape["cross"]
    in_specs = (
        P(None, "slab", "cross", None),
        P(),
        P(),
        P(),
        P(),
        P("slab", None),
        P(),
        P(("slab", "cross"), None),
        P(("slab", "cross")),
        P(("slab", "cross")),
    )
    out_specs = (P(None, "slab", "cross", None), P("slab", None))
    return jax.shard_map(
        functools.partial(on_device, slabs, crosses),
        mesh=mesh,
        in_specs=in_specs,
        out_specs=out_specs,
        check_vma=False,
    )
```

```python
import functools

import jax
import jax.numpy as jnp
from jax import lax
from jax.experimental import pallas as pl
from jax.experimental.pallas import tpu as pltpu
from jax.sharding import PartitionSpec as P

TILE = 128

time_step = 0.1
viscosity = 0.3
pool_scale = 1.0 / 64.0
state_step = 0.5
force_scale = 0.5

BOTH = ("slab", "cross")
F32 = jnp.float32
BF16 = jnp.bfloat16


def lanes(rows):
    return lax.broadcasted_iota(jnp.int32, (rows, TILE), 1)


def sublanes(rows):
    return lax.broadcasted_iota(jnp.int32, (rows, TILE), 0)


def as_column(row):
    return jnp.transpose(jnp.broadcast_to(row, (TILE, TILE)))


def hot(mask):
    return jnp.where(mask, 1.0, 0.0).astype(BF16)


def slots_of(rotors, slot_ref):
    slots = jnp.zeros_like(rotors)
    for rotor in range(slot_ref.shape[0]):
        slots = jnp.where(rotors == rotor, slot_ref[rotor], slots)
    return slots


def load_kernel(
    tile_ref,
    rotor_ref,
    sub_ref,
    slot_ref,
    weight_ref,
    velocity_ref,
    slots_ref,
    cells,
    place_hot,
    gains,
    half_column,
    slot_hot,
    tiles,
    rotor_rows,
    sub_rows,
    slot_table,
    weights,
    sems,
    small_sems,
):
    parts, size_x, size_y, size_z = velocity_ref.shape
    columns = size_x * size_y
    halves = size_z // TILE
    groups = tile_ref.shape[0]
    rotors = slot_ref.shape[0]
    subs = weight_ref.shape[0]
    small = [
        pltpu.make_async_copy(source, target, small_sems.at[i])
        for i, (source, target) in enumerate(
            (
                (tile_ref, tiles),
                (sub_ref, sub_rows),
                (weight_ref, weights),
                (rotor_ref, rotor_rows),
                (slot_ref, slot_table),
            )
        )
    ]
    copies = [
        pltpu.make_async_copy(velocity_ref.at[c], cells.at[c], sems.at[c]) for c in range(parts)
    ]
    for copy in small + copies:
        copy.start()
    for copy in small:
        copy.wait()
    weight = weights[...]
    high = weight.astype(BF16)
    rest = weight - high.astype(F32)
    middle = rest.astype(BF16)
    low = (rest - middle.astype(F32)).astype(BF16)
    weight_parts = jnp.concatenate([high, middle, low], axis=0)
    sub_hot = []
    place_rows = tiles[...] // halves
    half_rows = tiles[...] % halves
    for group in range(groups):
        half_column[pl.ds(group * TILE, TILE), :] = as_column(half_rows[group : group + 1, :])
        place = as_column(place_rows[group : group + 1, :])
        for block in range(columns // TILE):
            place_hot[pl.ds(group * TILE, TILE), pl.ds(block * TILE, TILE)] = hot(
                place == lanes(TILE) + block * TILE
            )
        sub = as_column(sub_rows[group : group + 1, :])
        wide = jnp.concatenate([sub[:, :subs]] * 3, axis=1)
        index = lax.broadcasted_iota(jnp.int32, (TILE, subs), 1)
        sub_hot.append(hot(wide == jnp.concatenate([index] * 3, axis=1)))
    gains[...] = jnp.dot(
        jnp.concatenate(sub_hot, axis=0), weight_parts, preferred_element_type=F32
    )
    slots = slots_of(rotor_rows[...], slot_table)
    slots_ref[...] = slots
    slot_hot[...] = jnp.concatenate(
        [hot(slots[g : g + 1, :] == sublanes(rotors)) for g in range(groups)], axis=1
    )
    for copy in copies:
        copy.wait()


def first_half(bits):
    index = lax.axis_index("slab") * lax.axis_size("cross") + lax.axis_index("cross")
    parity = index
    for bit in range(1, bits):
        parity = parity ^ (index >> bit)
    return parity % 2 == 0


def pool_kernel(
    bits,
    cells,
    place_hot,
    gains,
    half_column,
    slot_hot,
    keep_ref,
    send_ref,
    y_even_ref,
    y_odd_ref,
    total,
):
    parts, size_x, size_y, size_z = cells.shape
    columns = size_x * size_y
    halves = size_z // TILE
    rotors = slot_hot.shape[0]
    half = half_column[...]
    even_y = lax.axis_index("cross") % 2 == 0
    flat = jnp.concatenate(
        [cells[c].reshape(columns, size_z).astype(BF16) for c in range(parts)], axis=1
    )
    found = jnp.dot(place_hot[...], flat, preferred_element_type=F32)
    for c in range(parts):
        sample = found[:, c * size_z : c * size_z + TILE]
        for h in range(1, halves):
            at = c * size_z + h * TILE
            sample = jnp.where(half == h, found[:, at : at + TILE], sample)
        weighted = sample * gains[:, c * TILE : (c + 1) * TILE]
        high = weighted.astype(BF16)
        low = (weighted - high.astype(F32)).astype(BF16)
        sums = jnp.dot(
            slot_hot[...], jnp.concatenate([high, low], axis=1), preferred_element_type=F32
        )
        total[c * rotors : (c + 1) * rotors, :] = sums[:, TILE:] + sums[:, :TILE]
        first, last = cells[c, :, 0, :], cells[c, :, size_y - 1, :]
        y_even_ref[c] = jnp.where(even_y, last, first).astype(BF16)
        y_odd_ref[c] = jnp.where(even_y, first, last).astype(BF16)
    rows = keep_ref.shape[0]
    first, second = total[:rows, :], total[rows:, :]
    keep_ref[...] = jnp.where(first_half(bits), first, second)
    send_ref[...] = jnp.where(first_half(bits), second, first)


def pack_rows(target_ref, start, blocks):
    rows, width = blocks[0].shape
    count = rows * len(blocks)
    for j in range(width // TILE):
        for k, block in enumerate(blocks):
            at = start + j * count + k * rows
            target_ref[at : at + rows, :] = block[:, j * TILE : (j + 1) * TILE]


def unpack_rows(source_ref, start, width):
    count = (source_ref.shape[0] - start) // (width // TILE)
    return jnp.concatenate(
        [source_ref[start + j * count : start + (j + 1) * count, :] for j in range(width // TILE)],
        axis=1,
    )


def stencil_kernel(planes, edges, fences, slabs, crosses, *refs):
    refs, out_ref = refs[fences:-1], refs[-1]
    velocity_ref, y_even_ref, y_odd_ref = refs[:3]
    if edges:
        x_even_ref, x_odd_ref = refs[3:]
    parts, size_x, size_y, size_z = velocity_ref.shape
    row = lax.broadcasted_iota(jnp.int32, (size_y, size_z), 0)
    lane = lax.broadcasted_iota(jnp.int32, (size_y, size_z), 1)
    slab, cross = lax.axis_index("slab"), lax.axis_index("cross")
    even_x, even_y = slab % 2 == 0, cross % 2 == 0
    inner_x = jnp.logical_and(slab > 0, slab < slabs - 1)
    inner_y = jnp.logical_and(cross > 0, cross < crosses - 1)
    souths, norths = [], []
    for c in range(parts):
        near = y_even_ref[c].astype(F32)
        far = jnp.where(inner_y, y_odd_ref[c].astype(F32), 0.0)
        souths.append(jnp.where(even_y, far, near))
        norths.append(jnp.where(even_y, near, far))
    spread = time_step * viscosity
    for at, x in enumerate(planes):
        drift = [(0.5 * time_step) * velocity_ref[d, x] for d in range(parts)]
        to_east, to_west = spread - drift[0], spread + drift[0]
        to_north, to_south = spread - drift[1], spread + drift[1]
        to_upper = jnp.where(lane == size_z - 1, 0.0, spread - drift[2])
        to_lower = jnp.where(lane == 0, 0.0, spread + drift[2])
        for c in range(parts):
            here = velocity_ref[c, x]
            if x > 0:
                west = velocity_ref[c, x - 1]
            else:
                far_x = jnp.where(inner_x, x_odd_ref[c].astype(F32), 0.0)
                west = jnp.where(even_x, far_x, x_even_ref[c].astype(F32))
            if x + 1 < size_x:
                east = velocity_ref[c, x + 1]
            else:
                far_x = jnp.where(inner_x, x_odd_ref[c].astype(F32), 0.0)
                east = jnp.where(even_x, x_even_ref[c].astype(F32), far_x)
            south = jnp.where(row == 0, souths[c][x : x + 1, :], pltpu.roll(here, 1, 0))
            north = jnp.where(
                row == size_y - 1, norths[c][x : x + 1, :], pltpu.roll(here, size_y - 1, 0)
            )
            out_ref[c, at] = (
                (1.0 - 6.0 * spread) * here
                + (to_east * east + to_west * west)
                + (to_north * north + to_south * south)
                + (to_upper * pltpu.roll(here, size_z - 1, 1) + to_lower * pltpu.roll(here, 1, 1))
            )


def key_kernel(rotors, fences, *refs):
    slots_ref, sub_ref, key_ref = refs[fences:]
    keys = sub_ref[...] // 2 * rotors + slots_ref[...]
    for group in range(keys.shape[0]):
        key = as_column(keys[group : group + 1, :])
        for block in range(key_ref.shape[1] // TILE):
            key_ref[pl.ds(group * TILE, TILE), pl.ds(block * TILE, TILE)] = hot(
                key == lanes(TILE) + block * TILE
            )


def place_kernel(halves, fence_ref, tile_ref, place_ref):
    del fence_ref
    places = tile_ref[...] // halves
    for group in range(places.shape[0]):
        for block in range(place_ref.shape[0] // TILE):
            place_ref[pl.ds(block * TILE, TILE), pl.ds(group * TILE, TILE)] = hot(
                places[group : group + 1, :] == sublanes(TILE) + block * TILE
            )


def join_kernel(bits, fences, *refs):
    keep_ref, other_ref, states_ref, cells, out_ref, x_even_ref, x_odd_ref = refs[fences:]
    even_x = lax.axis_index("slab") % 2 == 0
    for c in range(cells.shape[0]):
        first, last = cells[c, 0], cells[c, cells.shape[1] - 1]
        x_even_ref[c] = jnp.where(even_x, last, first).astype(BF16)
        x_odd_ref[c] = jnp.where(even_x, first, last).astype(BF16)
    rows = keep_ref.shape[0]
    out_ref[:rows, :] = keep_ref[...] + other_ref[...]
    half = states_ref.shape[1] // 2
    pack_rows(
        out_ref, rows, [jnp.where(first_half(bits), states_ref[:, :half], states_ref[:, half:])]
    )


def merge_kernel(fences, packs, shift, rows, width, pooled_rows, *refs):
    refs, out_ref = refs[fences:-1], refs[-1]
    total = refs[0][:pooled_rows, :]
    for other in refs[1:]:
        total = total + other[:pooled_rows, :]
    out_ref[:pooled_rows, :] = total
    mine = (lax.axis_index("slab") >> shift) % packs
    blocks = [unpack_rows(ref, pooled_rows, width) for ref in refs[:packs]]
    ordered = []
    for place in range(packs):
        block = blocks[0]
        for k in range(1, packs):
            block = jnp.where((mine ^ k) == place, blocks[k], block)
        ordered.append(block)
    pieces = []
    for at in range(0, blocks[0].shape[0], rows):
        pieces += [block[at : at + rows] for block in ordered]
    pack_rows(out_ref, pooled_rows, pieces)


def rotor_kernel(
    bits,
    runs,
    tile_ref,
    sub_ref,
    w_in_ref,
    w_out_ref,
    decay_ref,
    key_hot,
    place_hot,
    keep_ref,
    other_ref,
    *rest,
):
    count = 1 + max(run[2] for run in runs)
    field_refs, rest = rest[:count], rest[count:]
    out_ref, new_ref, by_slab, source_rows, wind, sems, new_sem = rest
    slabs, rows, width = by_slab.shape
    rotors = slabs * rows
    size_x, size_y, size_z = wind.shape
    parts = w_in_ref.shape[0] // TILE
    halves = size_z // TILE
    groups = tile_ref.shape[0]
    subs = w_out_ref.shape[1] // TILE
    stores = []
    for k, (first, number, which, at) in enumerate(runs):
        stores.append(
            pltpu.make_async_copy(
                field_refs[which].at[1:, pl.ds(at, number)],
                out_ref.at[1:, pl.ds(first, number)],
                sems.at[k],
            )
        )
        stores[-1].start()
    split = parts * rotors // 2
    first = first_half(bits)
    keep, other = keep_ref[:split, :], other_ref[:split, :]
    pooled = jnp.concatenate(
        [jnp.where(first, keep, other), jnp.where(first, other, keep)], axis=0
    )
    pooled = (pooled * pool_scale).astype(BF16)
    pooled = jnp.concatenate([pooled[c * rotors : (c + 1) * rotors] for c in range(parts)], axis=1)
    keep, other = [unpack_rows(ref, split, width // 2) for ref in (keep_ref, other_ref)]
    old = jnp.concatenate(
        [jnp.where(first, keep, other), jnp.where(first, other, keep)], axis=1
    )
    drive = jnp.dot(pooled, w_in_ref[...], preferred_element_type=F32)
    new = old + state_step * (drive - decay_ref[...] * old)
    for j in range(slabs):
        by_slab[j] = new[j * rows : (j + 1) * rows, :]
    own = pltpu.make_async_copy(by_slab.at[lax.axis_index("slab")], new_ref, new_sem)
    own.start()
    stores.append(own)
    new_b = new.astype(BF16)

    half_rows = tile_ref[...] % halves
    new_b = jnp.concatenate([new_b, jnp.zeros((max(TILE - rotors, 0), width), BF16)], axis=0)
    sources = jnp.dot(new_b, w_out_ref[...], preferred_element_type=F32)[:rotors].astype(BF16)
    for pair in range(subs // 2):
        source_rows[pair * rotors : (pair + 1) * rotors, :] = sources[
            :, pair * 2 * TILE : (pair + 1) * 2 * TILE
        ]
    taken = jnp.dot(key_hot[...], source_rows[...], preferred_element_type=F32)
    second = jnp.concatenate(
        [as_column(sub_ref[g : g + 1, :] % 2) for g in range(groups)], axis=0
    )
    taken = jnp.where(second == 1, taken[:, TILE:], taken[:, :TILE])
    half = jnp.concatenate([as_column(half_rows[g : g + 1, :]) for g in range(groups)], axis=0)
    spread = jnp.concatenate(
        [jnp.where(half == h, taken, 0.0).astype(BF16) for h in range(halves)], axis=1
    )
    chunks = sems.shape[0] - len(runs)
    step = size_x // chunks
    for k in range(chunks):
        forcing = jnp.dot(
            place_hot[pl.ds(k * step * size_y, step * size_y), :],
            spread,
            preferred_element_type=F32,
        ).reshape(step, size_y, size_z)
        for first, number, which, at in runs:
            begin, end = max(first, k * step), min(first + number, (k + 1) * step)
            if begin < end:
                field = field_refs[which][0, at + begin - first : at + end - first]
                wind[begin:end] = field - force_scale * forcing[begin - k * step : end - k * step]
        at = pl.ds(k * step, step)
        stores.append(
            pltpu.make_async_copy(wind.at[at], out_ref.at[0, at], sems.at[len(runs) + k])
        )
        stores[-1].start()
    for store in stores:
        store.wait()


def swap(value, axis, count, offset):
    return lax.ppermute(value, axis, [(i, i ^ offset) for i in range(count)])


def swap_pairs(value, axis, counts, first):
    slabs, crosses = counts
    if axis == "cross":
        pairs = [(i, (i + 1) % crosses) for i in range(first, crosses, 2)]
        return lax.ppermute(value, axis, pairs + [(j, i) for i, j in pairs])
    partner = {i: i + 1 for i in range(first, slabs - 1, 2)}
    partner.update({j: i for i, j in partner.items()})
    pairs = []
    for slab in range(slabs):
        for cross in range(crosses):
            to = (partner[slab], cross) if slab in partner else (slab, cross ^ 1)
            pairs.append((slab * crosses + cross, to[0] * crosses + to[1]))
    return lax.ppermute(value, BOTH, pairs)


def vmem(count):
    return [pl.BlockSpec(memory_space=pltpu.VMEM)] * count


def in_hbm(value):
    return pltpu.with_memory_space_constraint(value, pltpu.HBM)


SMEM = pl.BlockSpec(memory_space=pltpu.SMEM)
HBM = pl.BlockSpec(memory_space=pltpu.HBM)
ANY = pl.BlockSpec(memory_space=pl.ANY)


def load(tile, rotor, sub, slot_of_rotor, shape_weight, velocity):
    parts, size_x, size_y, size_z = velocity.shape
    columns = size_x * size_y
    groups = tile.shape[0]
    entries = groups * TILE
    rotors = slot_of_rotor.shape[0]
    return pl.pallas_call(
        load_kernel,
        out_shape=(
            jax.ShapeDtypeStruct((groups, TILE), jnp.int32),
            jax.ShapeDtypeStruct(velocity.shape, F32),
            jax.ShapeDtypeStruct((entries, columns), BF16),
            jax.ShapeDtypeStruct((entries, parts * TILE), F32),
            jax.ShapeDtypeStruct((entries, TILE), jnp.int32),
            jax.ShapeDtypeStruct((rotors, entries), BF16),
        ),
        in_specs=[HBM] * 6,
        out_specs=tuple(vmem(6)),
        scratch_shapes=[
            pltpu.VMEM((groups, TILE), jnp.int32),
            pltpu.VMEM((groups, TILE), jnp.int32),
            pltpu.VMEM((groups, TILE), jnp.int32),
            pltpu.SMEM((rotors,), jnp.int32),
            pltpu.VMEM(shape_weight.shape, F32),
            pltpu.SemaphoreType.DMA((parts,)),
            pltpu.SemaphoreType.DMA((5,)),
        ],
        compiler_params=pltpu.CompilerParams(vmem_limit_bytes=8 << 20),
        cost_estimate=pl.CostEstimate(
            flops=2 * entries * columns * size_z,
            bytes_accessed=velocity.size * 4,
            transcendentals=0,
        ),
        name="load",
    )(*(in_hbm(value) for value in (tile, rotor, sub, slot_of_rotor, shape_weight, velocity)))


def pool(bits, cells, place_hot, gains, half_column, slot_hot):
    parts, size_x, size_y, size_z = cells.shape
    rows = parts * slot_hot.shape[0]
    part = jax.ShapeDtypeStruct((rows // 2, TILE), F32)
    return pl.pallas_call(
        functools.partial(pool_kernel, bits),
        out_shape=(
            part,
            part,
            jax.ShapeDtypeStruct((parts, size_x, size_z), BF16),
            jax.ShapeDtypeStruct((parts, size_x, size_z), BF16),
        ),
        in_specs=vmem(5),
        out_specs=tuple(vmem(4)),
        scratch_shapes=[pltpu.VMEM((rows, TILE), F32)],
        compiler_params=pltpu.CompilerParams(vmem_limit_bytes=12 << 20),
        cost_estimate=pl.CostEstimate(
            flops=2 * place_hot.size * parts * size_z, bytes_accessed=cells.size * 4, transcendentals=0
        ),
        name="pool",
    )(cells, place_hot, gains, half_column, slot_hot)


def stencil(planes, fences, slabs, crosses, velocity, halos):
    parts, size_x, size_y, size_z = velocity.shape
    edges = len(halos) > 2
    return pl.pallas_call(
        functools.partial(stencil_kernel, planes, edges, len(fences), slabs, crosses),
        out_shape=jax.ShapeDtypeStruct((parts, len(planes), size_y, size_z), F32),
        in_specs=[ANY] * len(fences) + vmem(1 + len(halos)),
        out_specs=vmem(1)[0],
        compiler_params=pltpu.CompilerParams(vmem_limit_bytes=4 << 20),
        cost_estimate=pl.CostEstimate(
            flops=1000 * velocity.size * len(planes) // size_x,
            bytes_accessed=8 * velocity.size * len(planes) // size_x,
            transcendentals=0,
        ),
        name="stencil",
    )(*fences, velocity, *halos)


def key_matrix(rotors, fences, slots, sub, keys):
    entries = slots.shape[0] * TILE
    return pl.pallas_call(
        functools.partial(key_kernel, rotors, len(fences)),
        out_shape=jax.ShapeDtypeStruct((entries, keys), BF16),
        in_specs=[ANY] * len(fences) + vmem(2),
        out_specs=vmem(1)[0],
        compiler_params=pltpu.CompilerParams(vmem_limit_bytes=4 << 20),
        cost_estimate=pl.CostEstimate(
            flops=1000 * entries * keys, bytes_accessed=2 * entries * keys, transcendentals=0
        ),
        name="keys",
    )(*fences, slots, sub)


def place_matrix(fence, tile, columns, halves):
    entries = tile.shape[0] * TILE
    return pl.pallas_call(
        functools.partial(place_kernel, halves),
        out_shape=jax.ShapeDtypeStruct((columns, entries), BF16),
        in_specs=[ANY] + vmem(1),
        out_specs=vmem(1)[0],
        compiler_params=pltpu.CompilerParams(vmem_limit_bytes=4 << 20),
        cost_estimate=pl.CostEstimate(
            flops=1000 * entries * columns, bytes_accessed=2 * entries * columns, transcendentals=0
        ),
        name="places",
    )(fence, tile)


def join(bits, fences, keep, other, states, cells):
    parts, _, size_y, size_z = cells.shape
    rows = keep.shape[0] + states.size // 2 // TILE
    return pl.pallas_call(
        functools.partial(join_kernel, bits, len(fences)),
        out_shape=(
            jax.ShapeDtypeStruct((rows, TILE), F32),
            jax.ShapeDtypeStruct((parts, size_y, size_z), BF16),
            jax.ShapeDtypeStruct((parts, size_y, size_z), BF16),
        ),
        in_specs=[ANY] * len(fences) + vmem(4),
        out_specs=tuple(vmem(3)),
        compiler_params=pltpu.CompilerParams(vmem_limit_bytes=4 << 20),
        name="join",
    )(*fences, keep, other, states, cells)


def merge(fences, shift, rows, width, pooled_rows, packed, pooled):
    total = pooled_rows + len(packed) * (packed[0].shape[0] - pooled_rows)
    return pl.pallas_call(
        functools.partial(
            merge_kernel, len(fences), len(packed), shift, rows, width, pooled_rows
        ),
        out_shape=jax.ShapeDtypeStruct((total, TILE), F32),
        in_specs=[ANY] * len(fences) + vmem(len(packed) + len(pooled)),
        out_specs=vmem(1)[0],
        compiler_params=pltpu.CompilerParams(vmem_limit_bytes=4 << 20),
        name="merge",
    )(*fences, *packed, *pooled)


def rotors_step(
    slabs, bits, runs, tile, sub, w_in, w_out, decay, key_hot, place_hot, keep, other, fields
):
    width = w_in.shape[1]
    parts, _, size_y, size_z = fields[0].shape
    size_x = sum(field.shape[1] for field in fields)
    keys = key_hot.shape[1]
    rows = keys // (w_out.shape[1] // (2 * TILE)) // slabs
    chunks = 2
    return pl.pallas_call(
        functools.partial(rotor_kernel, bits, runs),
        out_shape=(
            jax.ShapeDtypeStruct((parts, size_x, size_y, size_z), F32),
            jax.ShapeDtypeStruct((rows, width), F32),
        ),
        in_specs=vmem(9 + len(fields)),
        out_specs=(HBM, HBM),
        scratch_shapes=[
            pltpu.VMEM((slabs, rows, width), F32),
            pltpu.VMEM((keys, 2 * TILE), BF16),
            pltpu.VMEM((size_x, size_y, size_z), F32),
            pltpu.SemaphoreType.DMA((len(runs) + chunks,)),
            pltpu.SemaphoreType.DMA,
        ],
        compiler_params=pltpu.CompilerParams(vmem_limit_bytes=10 << 20),
        cost_estimate=pl.CostEstimate(
            flops=4 * place_hot.size * size_z, bytes_accessed=w_out.size * 2, transcendentals=0
        ),
        name="rotors",
    )(tile, sub, w_in, w_out, decay, key_hot, place_hot, keep, other, *fields)


def on_device(
    slabs,
    crosses,
    velocity,
    shape_weight,
    w_in,
    w_out,
    decay,
    rotor_states,
    slot_of_rotor,
    entry_rotor,
    entry_tile,
    entry_sub,
):
    size_x, size_y, size_z = velocity.shape[1:]
    entries = entry_tile.shape[0]
    width = w_in.shape[1]
    count = slabs * crosses
    tile = entry_tile.reshape(entries // TILE, TILE)
    rotor = entry_rotor.reshape(entries // TILE, TILE)
    sub = entry_sub.reshape(entries // TILE, TILE)

    bits = count.bit_length() - 1
    slots, cells, *loaded = load(tile, rotor, sub, slot_of_rotor, shape_weight, velocity)
    keep, send, y_even, y_odd = pool(bits, cells, *loaded)
    y_even = swap_pairs(y_even, "cross", (slabs, crosses), 0)
    y_odd = swap_pairs(y_odd, "cross", (slabs, crosses), 1)
    pooled_rows = keep.shape[0]

    middle = size_x // 2
    inner, outer = tuple(range(1, middle)), (0,) + tuple(range(middle, size_x))
    runs = ((1, middle - 1, 0, 0), (0, 1, 1, 0), (middle, size_x - middle, 1, 1))
    packed, x_even, x_odd = join(
        bits, (), keep, swap(send, BOTH, count, 1), rotor_states, cells
    )
    x_even = swap_pairs(x_even, "slab", (slabs, crosses), 0)
    x_odd = swap_pairs(x_odd, "slab", (slabs, crosses), 1)
    slab_bit = crosses.bit_length() - 1
    steps = [tuple(range(b, min(b + 2, bits))) for b in range(1, bits, 2)][::-1]
    fields = []
    for step in steps:
        made = []
        if step == steps[0]:
            rotors = slot_of_rotor.shape[0]
            keys = w_out.shape[1] // (2 * TILE) * rotors
            key_hot = key_matrix(rotors, (packed,), slots, sub, keys)
            fields.append(stencil(inner, (packed,), slabs, crosses, cells, (y_even, y_odd)))
            made += [key_hot, fields[-1]]
        if step == steps[-1]:
            place_hot = place_matrix(packed, tile, size_x * size_y, size_z // TILE)
            halos = (y_even, y_odd, x_even, x_odd)
            fields.append(stencil(outer, (packed,), slabs, crosses, cells, halos))
            made += [place_hot, fields[-1]]
        slab_bits = [b for b in step if b >= slab_bit]
        across = [1 << b | 1 for b in slab_bits]
        if len(slab_bits) == 2:
            across.append(sum(1 << b for b in step))
            within = []
        else:
            within = [1 << b | 1 for b in step if b < slab_bit]
            within += [sum(1 << b for b in step)] if len(step) == 2 else []
        sums = packed[:pooled_rows]
        packed = merge(
            made,
            slab_bits[0] - slab_bit,
            rotor_states.shape[0],
            width // 2,
            pooled_rows,
            [packed] + [swap(packed, BOTH, count, offset) for offset in across],
            [swap(sums, BOTH, count, offset) for offset in within],
        )
    other = swap(packed, BOTH, count, 1)
    return rotors_step(
        slabs,
        bits,
        runs,
        tile,
        sub,
        w_in,
        w_out,
        decay[None, :],
        key_hot,
        place_hot,
        packed,
        other,
        fields,
    )


def solution(mesh):
    slabs, crosses = mesh.shape["slab"], mesh.shape["cross"]
    in_specs = (
        P(None, "slab", "cross", None),
        P(),
        P(),
        P(),
        P(),
        P("slab", None),
        P(),
        P(("slab", "cross"), None),
        P(("slab", "cross")),
        P(("slab", "cross")),
    )
    out_specs = (P(None, "slab", "cross", None), P("slab", None))
    return jax.shard_map(
        functools.partial(on_device, slabs, crosses),
        mesh=mesh,
        in_specs=in_specs,
        out_specs=out_specs,
        check_vma=False,
    )
```

```python
import functools

import jax
import jax.numpy as jnp
from jax import lax
from jax.experimental import pallas as pl
from jax.experimental.pallas import tpu as pltpu
from jax.sharding import PartitionSpec as P

TILE = 128

time_step = 0.1
viscosity = 0.3
pool_scale = 1.0 / 64.0
state_step = 0.5
force_scale = 0.5

BOTH = ("slab", "cross")
F32 = jnp.float32
BF16 = jnp.bfloat16


def lanes(rows):
    return lax.broadcasted_iota(jnp.int32, (rows, TILE), 1)


def sublanes(rows):
    return lax.broadcasted_iota(jnp.int32, (rows, TILE), 0)


def as_column(row):
    return jnp.transpose(jnp.broadcast_to(row, (TILE, TILE)))


def hot(mask):
    return jnp.where(mask, 1.0, 0.0).astype(BF16)


def slots_of(rotors, slot_ref):
    slots = jnp.zeros_like(rotors)
    for rotor in range(slot_ref.shape[0]):
        slots = jnp.where(rotors == rotor, slot_ref[rotor], slots)
    return slots


def load_kernel(
    tile_ref,
    rotor_ref,
    sub_ref,
    slot_ref,
    weight_ref,
    velocity_ref,
    slots_ref,
    cells,
    place_hot,
    gains,
    half_column,
    slot_hot,
    tiles,
    rotor_rows,
    sub_rows,
    slot_table,
    weights,
    sems,
    small_sems,
):
    parts, size_x, size_y, size_z = velocity_ref.shape
    columns = size_x * size_y
    halves = size_z // TILE
    groups = tile_ref.shape[0]
    rotors = slot_ref.shape[0]
    subs = weight_ref.shape[0]
    small = [
        pltpu.make_async_copy(source, target, small_sems.at[i])
        for i, (source, target) in enumerate(
            (
                (tile_ref, tiles),
                (sub_ref, sub_rows),
                (weight_ref, weights),
                (rotor_ref, rotor_rows),
                (slot_ref, slot_table),
            )
        )
    ]
    copies = [
        pltpu.make_async_copy(velocity_ref.at[c], cells.at[c], sems.at[c]) for c in range(parts)
    ]
    for copy in small + copies:
        copy.start()
    for copy in small:
        copy.wait()
    weight = weights[...]
    high = weight.astype(BF16)
    rest = weight - high.astype(F32)
    middle = rest.astype(BF16)
    low = (rest - middle.astype(F32)).astype(BF16)
    weight_parts = jnp.concatenate([high, middle, low], axis=0)
    sub_hot = []
    place_rows = tiles[...] // halves
    half_rows = tiles[...] % halves
    for group in range(groups):
        half_column[pl.ds(group * TILE, TILE), :] = as_column(half_rows[group : group + 1, :])
        place = as_column(place_rows[group : group + 1, :])
        for block in range(columns // TILE):
            place_hot[pl.ds(group * TILE, TILE), pl.ds(block * TILE, TILE)] = hot(
                place == lanes(TILE) + block * TILE
            )
        sub = as_column(sub_rows[group : group + 1, :])
        wide = jnp.concatenate([sub[:, :subs]] * 3, axis=1)
        index = lax.broadcasted_iota(jnp.int32, (TILE, subs), 1)
        sub_hot.append(hot(wide == jnp.concatenate([index] * 3, axis=1)))
    gains[...] = jnp.dot(
        jnp.concatenate(sub_hot, axis=0), weight_parts, preferred_element_type=F32
    )
    slots = slots_of(rotor_rows[...], slot_table)
    slots_ref[...] = slots
    slot_hot[...] = jnp.concatenate(
        [hot(slots[g : g + 1, :] == sublanes(rotors)) for g in range(groups)], axis=1
    )
    for copy in copies:
        copy.wait()


def first_half(bits):
    index = lax.axis_index("slab") * lax.axis_size("cross") + lax.axis_index("cross")
    parity = index
    for bit in range(1, bits):
        parity = parity ^ (index >> bit)
    return parity % 2 == 0


def pool_kernel(
    bits,
    cells,
    place_hot,
    gains,
    half_column,
    slot_hot,
    keep_ref,
    send_ref,
    y_even_ref,
    y_odd_ref,
    total,
):
    parts, size_x, size_y, size_z = cells.shape
    columns = size_x * size_y
    halves = size_z // TILE
    rotors = slot_hot.shape[0]
    half = half_column[...]
    even_y = lax.axis_index("cross") % 2 == 0
    flat = jnp.concatenate(
        [cells[c].reshape(columns, size_z).astype(BF16) for c in range(parts)], axis=1
    )
    found = jnp.dot(place_hot[...], flat, preferred_element_type=F32)
    for c in range(parts):
        sample = found[:, c * size_z : c * size_z + TILE]
        for h in range(1, halves):
            at = c * size_z + h * TILE
            sample = jnp.where(half == h, found[:, at : at + TILE], sample)
        weighted = sample * gains[:, c * TILE : (c + 1) * TILE]
        high = weighted.astype(BF16)
        low = (weighted - high.astype(F32)).astype(BF16)
        sums = jnp.dot(
            slot_hot[...], jnp.concatenate([high, low], axis=1), preferred_element_type=F32
        )
        total[c * rotors : (c + 1) * rotors, :] = sums[:, TILE:] + sums[:, :TILE]
        first, last = cells[c, :, 0, :], cells[c, :, size_y - 1, :]
        y_even_ref[c] = jnp.where(even_y, last, first).astype(BF16)
        y_odd_ref[c] = jnp.where(even_y, first, last).astype(BF16)
    rows = keep_ref.shape[0]
    first, second = total[:rows, :], total[rows:, :]
    keep_ref[...] = jnp.where(first_half(bits), first, second)
    send_ref[...] = jnp.where(first_half(bits), second, first)


def pack_rows(target_ref, start, blocks):
    rows, width = blocks[0].shape
    count = rows * len(blocks)
    for j in range(width // TILE):
        for k, block in enumerate(blocks):
            at = start + j * count + k * rows
            target_ref[at : at + rows, :] = block[:, j * TILE : (j + 1) * TILE]


def unpack_rows(source_ref, start, width):
    count = (source_ref.shape[0] - start) // (width // TILE)
    return jnp.concatenate(
        [source_ref[start + j * count : start + (j + 1) * count, :] for j in range(width // TILE)],
        axis=1,
    )


def stencil_kernel(planes, edges, fences, slabs, crosses, *refs):
    refs, out_ref = refs[fences:-1], refs[-1]
    velocity_ref, y_even_ref, y_odd_ref = refs[:3]
    if edges:
        x_even_ref, x_odd_ref = refs[3:]
    parts, size_x, size_y, size_z = velocity_ref.shape
    row = lax.broadcasted_iota(jnp.int32, (size_y, size_z), 0)
    lane = lax.broadcasted_iota(jnp.int32, (size_y, size_z), 1)
    slab, cross = lax.axis_index("slab"), lax.axis_index("cross")
    even_x, even_y = slab % 2 == 0, cross % 2 == 0
    inner_x = jnp.logical_and(slab > 0, slab < slabs - 1)
    inner_y = jnp.logical_and(cross > 0, cross < crosses - 1)
    souths, norths = [], []
    for c in range(parts):
        near = y_even_ref[c].astype(F32)
        far = jnp.where(inner_y, y_odd_ref[c].astype(F32), 0.0)
        souths.append(jnp.where(even_y, far, near))
        norths.append(jnp.where(even_y, near, far))
    spread = time_step * viscosity
    for at, x in enumerate(planes):
        drift = [(0.5 * time_step) * velocity_ref[d, x] for d in range(parts)]
        to_east, to_west = spread - drift[0], spread + drift[0]
        to_north, to_south = spread - drift[1], spread + drift[1]
        to_upper = jnp.where(lane == size_z - 1, 0.0, spread - drift[2])
        to_lower = jnp.where(lane == 0, 0.0, spread + drift[2])
        for c in range(parts):
            here = velocity_ref[c, x]
            if x > 0:
                west = velocity_ref[c, x - 1]
            else:
                far_x = jnp.where(inner_x, x_odd_ref[c].astype(F32), 0.0)
                west = jnp.where(even_x, far_x, x_even_ref[c].astype(F32))
            if x + 1 < size_x:
                east = velocity_ref[c, x + 1]
            else:
                far_x = jnp.where(inner_x, x_odd_ref[c].astype(F32), 0.0)
                east = jnp.where(even_x, x_even_ref[c].astype(F32), far_x)
            south = jnp.where(row == 0, souths[c][x : x + 1, :], pltpu.roll(here, 1, 0))
            north = jnp.where(
                row == size_y - 1, norths[c][x : x + 1, :], pltpu.roll(here, size_y - 1, 0)
            )
            out_ref[c, at] = (
                (1.0 - 6.0 * spread) * here
                + (to_east * east + to_west * west)
                + (to_north * north + to_south * south)
                + (to_upper * pltpu.roll(here, size_z - 1, 1) + to_lower * pltpu.roll(here, 1, 1))
            )


def key_kernel(rotors, fences, *refs):
    slots_ref, sub_ref, key_ref = refs[fences:]
    keys = sub_ref[...] // 2 * rotors + slots_ref[...]
    for group in range(keys.shape[0]):
        key = as_column(keys[group : group + 1, :])
        for block in range(key_ref.shape[1] // TILE):
            key_ref[pl.ds(group * TILE, TILE), pl.ds(block * TILE, TILE)] = hot(
                key == lanes(TILE) + block * TILE
            )


def place_kernel(halves, fence_ref, tile_ref, place_ref):
    del fence_ref
    places = tile_ref[...] // halves
    for group in range(places.shape[0]):
        for block in range(place_ref.shape[0] // TILE):
            place_ref[pl.ds(block * TILE, TILE), pl.ds(group * TILE, TILE)] = hot(
                places[group : group + 1, :] == sublanes(TILE) + block * TILE
            )


def join_kernel(bits, fences, *refs):
    keep_ref, other_ref, states_ref, cells, out_ref, x_even_ref, x_odd_ref = refs[fences:]
    even_x = lax.axis_index("slab") % 2 == 0
    for c in range(cells.shape[0]):
        first, last = cells[c, 0], cells[c, cells.shape[1] - 1]
        x_even_ref[c] = jnp.where(even_x, last, first).astype(BF16)
        x_odd_ref[c] = jnp.where(even_x, first, last).astype(BF16)
    rows = keep_ref.shape[0]
    out_ref[:rows, :] = keep_ref[...] + other_ref[...]
    half = states_ref.shape[1] // 2
    pack_rows(
        out_ref, rows, [jnp.where(first_half(bits), states_ref[:, :half], states_ref[:, half:])]
    )


def merge_kernel(fences, packs, shift, rows, width, pooled_rows, *refs):
    refs, out_ref = refs[fences:-1], refs[-1]
    total = refs[0][:pooled_rows, :]
    for other in refs[1:]:
        total = total + other[:pooled_rows, :]
    out_ref[:pooled_rows, :] = total
    mine = (lax.axis_index("slab") >> shift) % packs
    blocks = [unpack_rows(ref, pooled_rows, width) for ref in refs[:packs]]
    ordered = []
    for place in range(packs):
        block = blocks[0]
        for k in range(1, packs):
            block = jnp.where((mine ^ k) == place, blocks[k], block)
        ordered.append(block)
    pieces = []
    for at in range(0, blocks[0].shape[0], rows):
        pieces += [block[at : at + rows] for block in ordered]
    pack_rows(out_ref, pooled_rows, pieces)


def rotor_kernel(
    bits,
    runs,
    tile_ref,
    sub_ref,
    w_in_ref,
    w_out_ref,
    decay_ref,
    key_hot,
    place_hot,
    keep_ref,
    other_ref,
    *rest,
):
    count = 1 + max(run[2] for run in runs)
    field_refs, rest = rest[:count], rest[count:]
    out_ref, new_ref, by_slab, source_rows, wind, sems, new_sem = rest
    slabs, rows, width = by_slab.shape
    rotors = slabs * rows
    size_x, size_y, size_z = wind.shape
    parts = w_in_ref.shape[0] // TILE
    halves = size_z // TILE
    groups = tile_ref.shape[0]
    subs = w_out_ref.shape[1] // TILE
    stores = []
    for k, (first, number, which, at) in enumerate(runs):
        stores.append(
            pltpu.make_async_copy(
                field_refs[which].at[1:, pl.ds(at, number)],
                out_ref.at[1:, pl.ds(first, number)],
                sems.at[k],
            )
        )
        stores[-1].start()
    split = parts * rotors // 2
    first = first_half(bits)
    keep, other = keep_ref[:split, :], other_ref[:split, :]
    pooled = jnp.concatenate(
        [jnp.where(first, keep, other), jnp.where(first, other, keep)], axis=0
    )
    pooled = (pooled * pool_scale).astype(BF16)
    pooled = jnp.concatenate([pooled[c * rotors : (c + 1) * rotors] for c in range(parts)], axis=1)
    keep, other = [unpack_rows(ref, split, width // 2) for ref in (keep_ref, other_ref)]
    old = jnp.concatenate(
        [jnp.where(first, keep, other), jnp.where(first, other, keep)], axis=1
    )
    drive = jnp.dot(pooled, w_in_ref[...], preferred_element_type=F32)
    new = old + state_step * (drive - decay_ref[...] * old)
    for j in range(slabs):
        by_slab[j] = new[j * rows : (j + 1) * rows, :]
    own = pltpu.make_async_copy(by_slab.at[lax.axis_index("slab")], new_ref, new_sem)
    own.start()
    stores.append(own)
    new_b = new.astype(BF16)

    half_rows = tile_ref[...] % halves
    new_b = jnp.concatenate([new_b, jnp.zeros((max(TILE - rotors, 0), width), BF16)], axis=0)
    sources = jnp.dot(new_b, w_out_ref[...], preferred_element_type=F32)[:rotors].astype(BF16)
    for pair in range(subs // 2):
        source_rows[pair * rotors : (pair + 1) * rotors, :] = sources[
            :, pair * 2 * TILE : (pair + 1) * 2 * TILE
        ]
    taken = jnp.dot(key_hot[...], source_rows[...], preferred_element_type=F32)
    second = jnp.concatenate(
        [as_column(sub_ref[g : g + 1, :] % 2) for g in range(groups)], axis=0
    )
    taken = jnp.where(second == 1, taken[:, TILE:], taken[:, :TILE])
    half = jnp.concatenate([as_column(half_rows[g : g + 1, :]) for g in range(groups)], axis=0)
    spread = jnp.concatenate(
        [jnp.where(half == h, taken, 0.0).astype(BF16) for h in range(halves)], axis=1
    )
    chunks = sems.shape[0] - len(runs)
    step = size_x // chunks
    for k in range(chunks):
        forcing = jnp.dot(
            place_hot[pl.ds(k * step * size_y, step * size_y), :],
            spread,
            preferred_element_type=F32,
        ).reshape(step, size_y, size_z)
        for first, number, which, at in runs:
            begin, end = max(first, k * step), min(first + number, (k + 1) * step)
            if begin < end:
                field = field_refs[which][0, at + begin - first : at + end - first]
                wind[begin:end] = field - force_scale * forcing[begin - k * step : end - k * step]
        at = pl.ds(k * step, step)
        stores.append(
            pltpu.make_async_copy(wind.at[at], out_ref.at[0, at], sems.at[len(runs) + k])
        )
        stores[-1].start()
    for store in stores:
        store.wait()


def swap(value, axis, count, offset):
    return lax.ppermute(value, axis, [(i, i ^ offset) for i in range(count)])


def swap_pairs(value, axis, counts, first):
    slabs, crosses = counts
    if axis == "cross":
        pairs = [(i, (i + 1) % crosses) for i in range(first, crosses, 2)]
        return lax.ppermute(value, axis, pairs + [(j, i) for i, j in pairs])
    partner = {i: i + 1 for i in range(first, slabs - 1, 2)}
    partner.update({j: i for i, j in partner.items()})
    pairs = []
    for slab in range(slabs):
        for cross in range(crosses):
            to = (partner[slab], cross) if slab in partner else (slab, cross ^ 1)
            pairs.append((slab * crosses + cross, to[0] * crosses + to[1]))
    return lax.ppermute(value, BOTH, pairs)


def vmem(count):
    return [pl.BlockSpec(memory_space=pltpu.VMEM)] * count


def in_hbm(value):
    return pltpu.with_memory_space_constraint(value, pltpu.HBM)


SMEM = pl.BlockSpec(memory_space=pltpu.SMEM)
HBM = pl.BlockSpec(memory_space=pltpu.HBM)
ANY = pl.BlockSpec(memory_space=pl.ANY)


def load(tile, rotor, sub, slot_of_rotor, shape_weight, velocity):
    parts, size_x, size_y, size_z = velocity.shape
    columns = size_x * size_y
    groups = tile.shape[0]
    entries = groups * TILE
    rotors = slot_of_rotor.shape[0]
    return pl.pallas_call(
        load_kernel,
        out_shape=(
            jax.ShapeDtypeStruct((groups, TILE), jnp.int32),
            jax.ShapeDtypeStruct(velocity.shape, F32),
            jax.ShapeDtypeStruct((entries, columns), BF16),
            jax.ShapeDtypeStruct((entries, parts * TILE), F32),
            jax.ShapeDtypeStruct((entries, TILE), jnp.int32),
            jax.ShapeDtypeStruct((rotors, entries), BF16),
        ),
        in_specs=[HBM] * 6,
        out_specs=tuple(vmem(6)),
        scratch_shapes=[
            pltpu.VMEM((groups, TILE), jnp.int32),
            pltpu.VMEM((groups, TILE), jnp.int32),
            pltpu.VMEM((groups, TILE), jnp.int32),
            pltpu.SMEM((rotors,), jnp.int32),
            pltpu.VMEM(shape_weight.shape, F32),
            pltpu.SemaphoreType.DMA((parts,)),
            pltpu.SemaphoreType.DMA((5,)),
        ],
        compiler_params=pltpu.CompilerParams(vmem_limit_bytes=8 << 20),
        cost_estimate=pl.CostEstimate(
            flops=2 * entries * columns * size_z,
            bytes_accessed=velocity.size * 4,
            transcendentals=0,
        ),
        name="load",
    )(*(in_hbm(value) for value in (tile, rotor, sub, slot_of_rotor, shape_weight, velocity)))


def pool(bits, cells, place_hot, gains, half_column, slot_hot):
    parts, size_x, size_y, size_z = cells.shape
    rows = parts * slot_hot.shape[0]
    part = jax.ShapeDtypeStruct((rows // 2, TILE), F32)
    return pl.pallas_call(
        functools.partial(pool_kernel, bits),
        out_shape=(
            part,
            part,
            jax.ShapeDtypeStruct((parts, size_x, size_z), BF16),
            jax.ShapeDtypeStruct((parts, size_x, size_z), BF16),
        ),
        in_specs=vmem(5),
        out_specs=tuple(vmem(4)),
        scratch_shapes=[pltpu.VMEM((rows, TILE), F32)],
        compiler_params=pltpu.CompilerParams(vmem_limit_bytes=12 << 20),
        cost_estimate=pl.CostEstimate(
            flops=2 * place_hot.size * parts * size_z, bytes_accessed=cells.size * 4, transcendentals=0
        ),
        name="pool",
    )(cells, place_hot, gains, half_column, slot_hot)


def stencil(planes, fences, slabs, crosses, velocity, halos):
    parts, size_x, size_y, size_z = velocity.shape
    edges = len(halos) > 2
    return pl.pallas_call(
        functools.partial(stencil_kernel, planes, edges, len(fences), slabs, crosses),
        out_shape=jax.ShapeDtypeStruct((parts, len(planes), size_y, size_z), F32),
        in_specs=[ANY] * len(fences) + vmem(1 + len(halos)),
        out_specs=vmem(1)[0],
        compiler_params=pltpu.CompilerParams(vmem_limit_bytes=4 << 20),
        cost_estimate=pl.CostEstimate(
            flops=1000 * velocity.size * len(planes) // size_x,
            bytes_accessed=8 * velocity.size * len(planes) // size_x,
            transcendentals=0,
        ),
        name="stencil",
    )(*fences, velocity, *halos)


def key_matrix(rotors, fences, slots, sub, keys):
    entries = slots.shape[0] * TILE
    return pl.pallas_call(
        functools.partial(key_kernel, rotors, len(fences)),
        out_shape=jax.ShapeDtypeStruct((entries, keys), BF16),
        in_specs=[ANY] * len(fences) + vmem(2),
        out_specs=vmem(1)[0],
        compiler_params=pltpu.CompilerParams(vmem_limit_bytes=4 << 20),
        cost_estimate=pl.CostEstimate(
            flops=1000 * entries * keys, bytes_accessed=2 * entries * keys, transcendentals=0
        ),
        name="keys",
    )(*fences, slots, sub)


def place_matrix(fence, tile, columns, halves):
    entries = tile.shape[0] * TILE
    return pl.pallas_call(
        functools.partial(place_kernel, halves),
        out_shape=jax.ShapeDtypeStruct((columns, entries), BF16),
        in_specs=[ANY] + vmem(1),
        out_specs=vmem(1)[0],
        compiler_params=pltpu.CompilerParams(vmem_limit_bytes=4 << 20),
        cost_estimate=pl.CostEstimate(
            flops=1000 * entries * columns, bytes_accessed=2 * entries * columns, transcendentals=0
        ),
        name="places",
    )(fence, tile)


def join(bits, fences, keep, other, states, cells):
    parts, _, size_y, size_z = cells.shape
    rows = keep.shape[0] + states.size // 2 // TILE
    return pl.pallas_call(
        functools.partial(join_kernel, bits, len(fences)),
        out_shape=(
            jax.ShapeDtypeStruct((rows, TILE), F32),
            jax.ShapeDtypeStruct((parts, size_y, size_z), BF16),
            jax.ShapeDtypeStruct((parts, size_y, size_z), BF16),
        ),
        in_specs=[ANY] * len(fences) + vmem(4),
        out_specs=tuple(vmem(3)),
        compiler_params=pltpu.CompilerParams(vmem_limit_bytes=4 << 20),
        name="join",
    )(*fences, keep, other, states, cells)


def merge(fences, shift, rows, width, pooled_rows, packed, pooled):
    total = pooled_rows + len(packed) * (packed[0].shape[0] - pooled_rows)
    return pl.pallas_call(
        functools.partial(
            merge_kernel, len(fences), len(packed), shift, rows, width, pooled_rows
        ),
        out_shape=jax.ShapeDtypeStruct((total, TILE), F32),
        in_specs=[ANY] * len(fences) + vmem(len(packed) + len(pooled)),
        out_specs=vmem(1)[0],
        compiler_params=pltpu.CompilerParams(vmem_limit_bytes=4 << 20),
        name="merge",
    )(*fences, *packed, *pooled)


def rotors_step(
    slabs, bits, runs, tile, sub, w_in, w_out, decay, key_hot, place_hot, keep, other, fields
):
    width = w_in.shape[1]
    parts, _, size_y, size_z = fields[0].shape
    size_x = sum(field.shape[1] for field in fields)
    keys = key_hot.shape[1]
    rows = keys // (w_out.shape[1] // (2 * TILE)) // slabs
    chunks = 2
    return pl.pallas_call(
        functools.partial(rotor_kernel, bits, runs),
        out_shape=(
            jax.ShapeDtypeStruct((parts, size_x, size_y, size_z), F32),
            jax.ShapeDtypeStruct((rows, width), F32),
        ),
        in_specs=vmem(9 + len(fields)),
        out_specs=(HBM, HBM),
        scratch_shapes=[
            pltpu.VMEM((slabs, rows, width), F32),
            pltpu.VMEM((keys, 2 * TILE), BF16),
            pltpu.VMEM((size_x, size_y, size_z), F32),
            pltpu.SemaphoreType.DMA((len(runs) + chunks,)),
            pltpu.SemaphoreType.DMA,
        ],
        compiler_params=pltpu.CompilerParams(vmem_limit_bytes=10 << 20),
        cost_estimate=pl.CostEstimate(
            flops=4 * place_hot.size * size_z, bytes_accessed=w_out.size * 2, transcendentals=0
        ),
        name="rotors",
    )(tile, sub, w_in, w_out, decay, key_hot, place_hot, keep, other, *fields)


def on_device(
    slabs,
    crosses,
    velocity,
    shape_weight,
    w_in,
    w_out,
    decay,
    rotor_states,
    slot_of_rotor,
    entry_rotor,
    entry_tile,
    entry_sub,
):
    size_x, size_y, size_z = velocity.shape[1:]
    entries = entry_tile.shape[0]
    width = w_in.shape[1]
    count = slabs * crosses
    tile = entry_tile.reshape(entries // TILE, TILE)
    rotor = entry_rotor.reshape(entries // TILE, TILE)
    sub = entry_sub.reshape(entries // TILE, TILE)

    bits = count.bit_length() - 1
    slots, cells, *loaded = load(tile, rotor, sub, slot_of_rotor, shape_weight, velocity)
    keep, send, y_even, y_odd = pool(bits, cells, *loaded)
    y_even = swap_pairs(y_even, "cross", (slabs, crosses), 0)
    y_odd = swap_pairs(y_odd, "cross", (slabs, crosses), 1)
    pooled_rows = keep.shape[0]

    middle = size_x * 3 // 16
    inner, outer = tuple(range(1, middle)), (0,) + tuple(range(middle, size_x))
    runs = ((1, middle - 1, 0, 0), (0, 1, 1, 0), (middle, size_x - middle, 1, 1))
    packed, x_even, x_odd = join(
        bits, (), keep, swap(send, BOTH, count, 1), rotor_states, cells
    )
    x_even = swap_pairs(x_even, "slab", (slabs, crosses), 0)
    x_odd = swap_pairs(x_odd, "slab", (slabs, crosses), 1)
    slab_bit = crosses.bit_length() - 1
    steps = [tuple(range(b, min(b + 2, bits))) for b in range(1, bits, 2)][::-1]
    fields = []
    for step in steps:
        made = []
        if step == steps[0]:
            rotors = slot_of_rotor.shape[0]
            keys = w_out.shape[1] // (2 * TILE) * rotors
            key_hot = key_matrix(rotors, (packed,), slots, sub, keys)
            fields.append(stencil(inner, (packed,), slabs, crosses, cells, (y_even, y_odd)))
            made += [key_hot, fields[-1]]
        if step == steps[-1]:
            place_hot = place_matrix(packed, tile, size_x * size_y, size_z // TILE)
            halos = (y_even, y_odd, x_even, x_odd)
            fields.append(stencil(outer, (packed,), slabs, crosses, cells, halos))
            made += [place_hot, fields[-1]]
        slab_bits = [b for b in step if b >= slab_bit]
        across = [1 << b | 1 for b in slab_bits]
        if len(slab_bits) == 2:
            across.append(sum(1 << b for b in step))
            within = []
        else:
            within = [1 << b | 1 for b in step if b < slab_bit]
            within += [sum(1 << b for b in step)] if len(step) == 2 else []
        sums = packed[:pooled_rows]
        packed = merge(
            made,
            slab_bits[0] - slab_bit,
            rotor_states.shape[0],
            width // 2,
            pooled_rows,
            [packed] + [swap(packed, BOTH, count, offset) for offset in across],
            [swap(sums, BOTH, count, offset) for offset in within],
        )
    other = swap(packed, BOTH, count, 1)
    return rotors_step(
        slabs,
        bits,
        runs,
        tile,
        sub,
        w_in,
        w_out,
        decay[None, :],
        key_hot,
        place_hot,
        packed,
        other,
        fields,
    )


def solution(mesh):
    slabs, crosses = mesh.shape["slab"], mesh.shape["cross"]
    in_specs = (
        P(None, "slab", "cross", None),
        P(),
        P(),
        P(),
        P(),
        P("slab", None),
        P(),
        P(("slab", "cross"), None),
        P(("slab", "cross")),
        P(("slab", "cross")),
    )
    out_specs = (P(None, "slab", "cross", None), P("slab", None))
    return jax.shard_map(
        functools.partial(on_device, slabs, crosses),
        mesh=mesh,
        in_specs=in_specs,
        out_specs=out_specs,
        check_vma=False,
    )
```

```python
import functools

import jax
import jax.numpy as jnp
from jax import lax
from jax.experimental import pallas as pl
from jax.experimental.pallas import tpu as pltpu
from jax.sharding import PartitionSpec as P

TILE = 128

time_step = 0.1
viscosity = 0.3
pool_scale = 1.0 / 64.0
state_step = 0.5
force_scale = 0.5

BOTH = ("slab", "cross")
F32 = jnp.float32
BF16 = jnp.bfloat16


def lanes(rows):
    return lax.broadcasted_iota(jnp.int32, (rows, TILE), 1)


def sublanes(rows):
    return lax.broadcasted_iota(jnp.int32, (rows, TILE), 0)


def as_column(row):
    return jnp.transpose(jnp.broadcast_to(row, (TILE, TILE)))


def hot(mask):
    return jnp.where(mask, 1.0, 0.0).astype(BF16)


def slots_of(rotors, slot_ref):
    slots = jnp.zeros_like(rotors)
    for rotor in range(slot_ref.shape[0]):
        slots = jnp.where(rotors == rotor, slot_ref[rotor], slots)
    return slots


def load_kernel(
    tile_ref,
    rotor_ref,
    sub_ref,
    slot_ref,
    weight_ref,
    velocity_ref,
    slots_ref,
    cells,
    place_hot,
    gains,
    half_column,
    slot_hot,
    tiles,
    rotor_rows,
    sub_rows,
    slot_table,
    weights,
    sems,
    small_sems,
):
    parts, size_x, size_y, size_z = velocity_ref.shape
    columns = size_x * size_y
    halves = size_z // TILE
    groups = tile_ref.shape[0]
    rotors = slot_ref.shape[0]
    subs = weight_ref.shape[0]
    small = [
        pltpu.make_async_copy(source, target, small_sems.at[i])
        for i, (source, target) in enumerate(
            (
                (tile_ref, tiles),
                (sub_ref, sub_rows),
                (weight_ref, weights),
                (rotor_ref, rotor_rows),
                (slot_ref, slot_table),
            )
        )
    ]
    copies = [
        pltpu.make_async_copy(velocity_ref.at[c], cells.at[c], sems.at[c]) for c in range(parts)
    ]
    for copy in small + copies:
        copy.start()
    for copy in small:
        copy.wait()
    weight = weights[...]
    high = weight.astype(BF16)
    rest = weight - high.astype(F32)
    middle = rest.astype(BF16)
    low = (rest - middle.astype(F32)).astype(BF16)
    weight_parts = jnp.concatenate([high, middle, low], axis=0)
    sub_hot = []
    place_rows = tiles[...] // halves
    half_rows = tiles[...] % halves
    for group in range(groups):
        half_column[pl.ds(group * TILE, TILE), :] = as_column(half_rows[group : group + 1, :])
        place = as_column(place_rows[group : group + 1, :])
        for block in range(columns // TILE):
            place_hot[pl.ds(group * TILE, TILE), pl.ds(block * TILE, TILE)] = hot(
                place == lanes(TILE) + block * TILE
            )
        sub = as_column(sub_rows[group : group + 1, :])
        wide = jnp.concatenate([sub[:, :subs]] * 3, axis=1)
        index = lax.broadcasted_iota(jnp.int32, (TILE, subs), 1)
        sub_hot.append(hot(wide == jnp.concatenate([index] * 3, axis=1)))
    gains[...] = jnp.dot(
        jnp.concatenate(sub_hot, axis=0), weight_parts, preferred_element_type=F32
    )
    slots = slots_of(rotor_rows[...], slot_table)
    slots_ref[...] = slots
    slot_hot[...] = jnp.concatenate(
        [hot(slots[g : g + 1, :] == sublanes(rotors)) for g in range(groups)], axis=1
    )
    for copy in copies:
        copy.wait()


def first_half(bits):
    index = lax.axis_index("slab") * lax.axis_size("cross") + lax.axis_index("cross")
    parity = index
    for bit in range(1, bits):
        parity = parity ^ (index >> bit)
    return parity % 2 == 0


def pool_kernel(
    bits,
    cells,
    place_hot,
    gains,
    half_column,
    slot_hot,
    keep_ref,
    send_ref,
    y_even_ref,
    y_odd_ref,
    total,
):
    parts, size_x, size_y, size_z = cells.shape
    columns = size_x * size_y
    halves = size_z // TILE
    rotors = slot_hot.shape[0]
    half = half_column[...]
    even_y = lax.axis_index("cross") % 2 == 0
    flat = jnp.concatenate(
        [cells[c].reshape(columns, size_z).astype(BF16) for c in range(parts)], axis=1
    )
    found = jnp.dot(place_hot[...], flat, preferred_element_type=F32)
    for c in range(parts):
        sample = found[:, c * size_z : c * size_z + TILE]
        for h in range(1, halves):
            at = c * size_z + h * TILE
            sample = jnp.where(half == h, found[:, at : at + TILE], sample)
        weighted = sample * gains[:, c * TILE : (c + 1) * TILE]
        high = weighted.astype(BF16)
        low = (weighted - high.astype(F32)).astype(BF16)
        sums = jnp.dot(
            slot_hot[...], jnp.concatenate([high, low], axis=1), preferred_element_type=F32
        )
        total[c * rotors : (c + 1) * rotors, :] = sums[:, TILE:] + sums[:, :TILE]
        first, last = cells[c, :, 0, :], cells[c, :, size_y - 1, :]
        y_even_ref[c] = jnp.where(even_y, last, first).astype(BF16)
        y_odd_ref[c] = jnp.where(even_y, first, last).astype(BF16)
    rows = keep_ref.shape[0]
    first, second = total[:rows, :], total[rows:, :]
    keep_ref[...] = jnp.where(first_half(bits), first, second)
    send_ref[...] = jnp.where(first_half(bits), second, first)


def pack_rows(target_ref, start, blocks):
    rows, width = blocks[0].shape
    count = rows * len(blocks)
    for j in range(width // TILE):
        for k, block in enumerate(blocks):
            at = start + j * count + k * rows
            target_ref[at : at + rows, :] = block[:, j * TILE : (j + 1) * TILE]


def unpack_rows(source_ref, start, width):
    count = (source_ref.shape[0] - start) // (width // TILE)
    return jnp.concatenate(
        [source_ref[start + j * count : start + (j + 1) * count, :] for j in range(width // TILE)],
        axis=1,
    )


def stencil_kernel(planes, edges, fences, slabs, crosses, *refs):
    refs, out_ref = refs[fences:-1], refs[-1]
    velocity_ref, y_even_ref, y_odd_ref = refs[:3]
    if edges:
        x_even_ref, x_odd_ref = refs[3:]
    parts, size_x, size_y, size_z = velocity_ref.shape
    row = lax.broadcasted_iota(jnp.int32, (size_y, size_z), 0)
    lane = lax.broadcasted_iota(jnp.int32, (size_y, size_z), 1)
    slab, cross = lax.axis_index("slab"), lax.axis_index("cross")
    even_x, even_y = slab % 2 == 0, cross % 2 == 0
    inner_x = jnp.logical_and(slab > 0, slab < slabs - 1)
    inner_y = jnp.logical_and(cross > 0, cross < crosses - 1)
    souths, norths = [], []
    for c in range(parts):
        near = y_even_ref[c].astype(F32)
        far = jnp.where(inner_y, y_odd_ref[c].astype(F32), 0.0)
        souths.append(jnp.where(even_y, far, near))
        norths.append(jnp.where(even_y, near, far))
    spread = time_step * viscosity
    for at, x in enumerate(planes):
        drift = [(0.5 * time_step) * velocity_ref[d, x] for d in range(parts)]
        to_east, to_west = spread - drift[0], spread + drift[0]
        to_north, to_south = spread - drift[1], spread + drift[1]
        to_upper = jnp.where(lane == size_z - 1, 0.0, spread - drift[2])
        to_lower = jnp.where(lane == 0, 0.0, spread + drift[2])
        for c in range(parts):
            here = velocity_ref[c, x]
            if x > 0:
                west = velocity_ref[c, x - 1]
            else:
                far_x = jnp.where(inner_x, x_odd_ref[c].astype(F32), 0.0)
                west = jnp.where(even_x, far_x, x_even_ref[c].astype(F32))
            if x + 1 < size_x:
                east = velocity_ref[c, x + 1]
            else:
                far_x = jnp.where(inner_x, x_odd_ref[c].astype(F32), 0.0)
                east = jnp.where(even_x, x_even_ref[c].astype(F32), far_x)
            south = jnp.where(row == 0, souths[c][x : x + 1, :], pltpu.roll(here, 1, 0))
            north = jnp.where(
                row == size_y - 1, norths[c][x : x + 1, :], pltpu.roll(here, size_y - 1, 0)
            )
            out_ref[c, at] = (
                (1.0 - 6.0 * spread) * here
                + (to_east * east + to_west * west)
                + (to_north * north + to_south * south)
                + (to_upper * pltpu.roll(here, size_z - 1, 1) + to_lower * pltpu.roll(here, 1, 1))
            )


def key_kernel(rotors, fences, *refs):
    slots_ref, sub_ref, key_ref = refs[fences:]
    keys = sub_ref[...] // 2 * rotors + slots_ref[...]
    for group in range(keys.shape[0]):
        key = as_column(keys[group : group + 1, :])
        for block in range(key_ref.shape[1] // TILE):
            key_ref[pl.ds(group * TILE, TILE), pl.ds(block * TILE, TILE)] = hot(
                key == lanes(TILE) + block * TILE
            )


def place_kernel(halves, fence_ref, tile_ref, place_ref):
    del fence_ref
    places = tile_ref[...] // halves
    low, high = (places % TILE).astype(F32), (places // TILE).astype(F32)
    rows = sublanes(TILE).astype(F32).astype(BF16)
    zeros = jnp.zeros((TILE, TILE), BF16)
    for group in range(places.shape[0]):
        row = jnp.broadcast_to(low[group : group + 1, :], (TILE, TILE)).astype(BF16)
        part = jnp.broadcast_to(high[group : group + 1, :], (TILE, TILE)).astype(BF16)
        found = jnp.where(row == rows, jnp.ones((TILE, TILE), BF16), zeros)
        for block in range(place_ref.shape[0] // TILE):
            place_ref[pl.ds(block * TILE, TILE), pl.ds(group * TILE, TILE)] = jnp.where(
                part == jnp.asarray(block, BF16), found, zeros
            )


def join_kernel(bits, fences, *refs):
    keep_ref, other_ref, states_ref, cells, out_ref, x_even_ref, x_odd_ref = refs[fences:]
    even_x = lax.axis_index("slab") % 2 == 0
    for c in range(cells.shape[0]):
        first, last = cells[c, 0], cells[c, cells.shape[1] - 1]
        x_even_ref[c] = jnp.where(even_x, last, first).astype(BF16)
        x_odd_ref[c] = jnp.where(even_x, first, last).astype(BF16)
    rows = keep_ref.shape[0]
    out_ref[:rows, :] = keep_ref[...] + other_ref[...]
    half = states_ref.shape[1] // 2
    pack_rows(
        out_ref, rows, [jnp.where(first_half(bits), states_ref[:, :half], states_ref[:, half:])]
    )


def merge_kernel(fences, packs, shift, rows, width, pooled_rows, *refs):
    refs, out_ref = refs[fences:-1], refs[-1]
    total = refs[0][:pooled_rows, :]
    for other in refs[1:]:
        total = total + other[:pooled_rows, :]
    out_ref[:pooled_rows, :] = total
    mine = (lax.axis_index("slab") >> shift) % packs
    blocks = [unpack_rows(ref, pooled_rows, width) for ref in refs[:packs]]
    ordered = []
    for place in range(packs):
        block = blocks[0]
        for k in range(1, packs):
            block = jnp.where((mine ^ k) == place, blocks[k], block)
        ordered.append(block)
    pieces = []
    for at in range(0, blocks[0].shape[0], rows):
        pieces += [block[at : at + rows] for block in ordered]
    pack_rows(out_ref, pooled_rows, pieces)


def rotor_kernel(
    bits,
    runs,
    tile_ref,
    sub_ref,
    w_in_ref,
    w_out_ref,
    decay_ref,
    key_hot,
    place_hot,
    keep_ref,
    other_ref,
    *rest,
):
    count = 1 + max(run[2] for run in runs)
    field_refs, rest = rest[:count], rest[count:]
    out_ref, new_ref, by_slab, source_rows, wind, sems, new_sem = rest
    slabs, rows, width = by_slab.shape
    rotors = slabs * rows
    size_x, size_y, size_z = wind.shape
    parts = w_in_ref.shape[0] // TILE
    halves = size_z // TILE
    groups = tile_ref.shape[0]
    subs = w_out_ref.shape[1] // TILE
    stores = []
    for k, (first, number, which, at) in enumerate(runs):
        stores.append(
            pltpu.make_async_copy(
                field_refs[which].at[1:, pl.ds(at, number)],
                out_ref.at[1:, pl.ds(first, number)],
                sems.at[k],
            )
        )
        stores[-1].start()
    split = parts * rotors // 2
    first = first_half(bits)
    keep, other = keep_ref[:split, :], other_ref[:split, :]
    pooled = jnp.concatenate(
        [jnp.where(first, keep, other), jnp.where(first, other, keep)], axis=0
    )
    pooled = (pooled * pool_scale).astype(BF16)
    pooled = jnp.concatenate([pooled[c * rotors : (c + 1) * rotors] for c in range(parts)], axis=1)
    keep, other = [unpack_rows(ref, split, width // 2) for ref in (keep_ref, other_ref)]
    old = jnp.concatenate(
        [jnp.where(first, keep, other), jnp.where(first, other, keep)], axis=1
    )
    drive = jnp.dot(pooled, w_in_ref[...], preferred_element_type=F32)
    new = old + state_step * (drive - decay_ref[...] * old)
    for j in range(slabs):
        by_slab[j] = new[j * rows : (j + 1) * rows, :]
    own = pltpu.make_async_copy(by_slab.at[lax.axis_index("slab")], new_ref, new_sem)
    own.start()
    stores.append(own)
    new_b = new.astype(BF16)

    half_rows = tile_ref[...] % halves
    new_b = jnp.concatenate([new_b, jnp.zeros((max(TILE - rotors, 0), width), BF16)], axis=0)
    sources = jnp.dot(new_b, w_out_ref[...], preferred_element_type=F32)[:rotors].astype(BF16)
    for pair in range(subs // 2):
        source_rows[pair * rotors : (pair + 1) * rotors, :] = sources[
            :, pair * 2 * TILE : (pair + 1) * 2 * TILE
        ]
    taken = jnp.dot(key_hot[...], source_rows[...], preferred_element_type=F32)
    second = jnp.concatenate(
        [as_column(sub_ref[g : g + 1, :] % 2) for g in range(groups)], axis=0
    )
    taken = jnp.where(second == 1, taken[:, TILE:], taken[:, :TILE])
    half = jnp.concatenate([as_column(half_rows[g : g + 1, :]) for g in range(groups)], axis=0)
    spread = jnp.concatenate(
        [jnp.where(half == h, taken, 0.0).astype(BF16) for h in range(halves)], axis=1
    )
    chunks = sems.shape[0] - len(runs)
    step = size_x // chunks
    for k in range(chunks):
        forcing = jnp.dot(
            place_hot[pl.ds(k * step * size_y, step * size_y), :],
            spread,
            preferred_element_type=F32,
        ).reshape(step, size_y, size_z)
        for first, number, which, at in runs:
            begin, end = max(first, k * step), min(first + number, (k + 1) * step)
            if begin < end:
                field = field_refs[which][0, at + begin - first : at + end - first]
                wind[begin:end] = field - force_scale * forcing[begin - k * step : end - k * step]
        at = pl.ds(k * step, step)
        stores.append(
            pltpu.make_async_copy(wind.at[at], out_ref.at[0, at], sems.at[len(runs) + k])
        )
        stores[-1].start()
    for store in stores:
        store.wait()


def swap(value, axis, count, offset):
    return lax.ppermute(value, axis, [(i, i ^ offset) for i in range(count)])


def swap_pairs(value, axis, counts, first):
    slabs, crosses = counts
    if axis == "cross":
        pairs = [(i, (i + 1) % crosses) for i in range(first, crosses, 2)]
        return lax.ppermute(value, axis, pairs + [(j, i) for i, j in pairs])
    partner = {i: i + 1 for i in range(first, slabs - 1, 2)}
    partner.update({j: i for i, j in partner.items()})
    pairs = []
    for slab in range(slabs):
        for cross in range(crosses):
            to = (partner[slab], cross) if slab in partner else (slab, cross ^ 1)
            pairs.append((slab * crosses + cross, to[0] * crosses + to[1]))
    return lax.ppermute(value, BOTH, pairs)


def vmem(count):
    return [pl.BlockSpec(memory_space=pltpu.VMEM)] * count


def in_hbm(value):
    return pltpu.with_memory_space_constraint(value, pltpu.HBM)


SMEM = pl.BlockSpec(memory_space=pltpu.SMEM)
HBM = pl.BlockSpec(memory_space=pltpu.HBM)
ANY = pl.BlockSpec(memory_space=pl.ANY)


def load(tile, rotor, sub, slot_of_rotor, shape_weight, velocity):
    parts, size_x, size_y, size_z = velocity.shape
    columns = size_x * size_y
    groups = tile.shape[0]
    entries = groups * TILE
    rotors = slot_of_rotor.shape[0]
    return pl.pallas_call(
        load_kernel,
        out_shape=(
            jax.ShapeDtypeStruct((groups, TILE), jnp.int32),
            jax.ShapeDtypeStruct(velocity.shape, F32),
            jax.ShapeDtypeStruct((entries, columns), BF16),
            jax.ShapeDtypeStruct((entries, parts * TILE), F32),
            jax.ShapeDtypeStruct((entries, TILE), jnp.int32),
            jax.ShapeDtypeStruct((rotors, entries), BF16),
        ),
        in_specs=[HBM] * 6,
        out_specs=tuple(vmem(6)),
        scratch_shapes=[
            pltpu.VMEM((groups, TILE), jnp.int32),
            pltpu.VMEM((groups, TILE), jnp.int32),
            pltpu.VMEM((groups, TILE), jnp.int32),
            pltpu.SMEM((rotors,), jnp.int32),
            pltpu.VMEM(shape_weight.shape, F32),
            pltpu.SemaphoreType.DMA((parts,)),
            pltpu.SemaphoreType.DMA((5,)),
        ],
        compiler_params=pltpu.CompilerParams(vmem_limit_bytes=8 << 20),
        cost_estimate=pl.CostEstimate(
            flops=2 * entries * columns * size_z,
            bytes_accessed=velocity.size * 4,
            transcendentals=0,
        ),
        name="load",
    )(*(in_hbm(value) for value in (tile, rotor, sub, slot_of_rotor, shape_weight, velocity)))


def pool(bits, cells, place_hot, gains, half_column, slot_hot):
    parts, size_x, size_y, size_z = cells.shape
    rows = parts * slot_hot.shape[0]
    part = jax.ShapeDtypeStruct((rows // 2, TILE), F32)
    return pl.pallas_call(
        functools.partial(pool_kernel, bits),
        out_shape=(
            part,
            part,
            jax.ShapeDtypeStruct((parts, size_x, size_z), BF16),
            jax.ShapeDtypeStruct((parts, size_x, size_z), BF16),
        ),
        in_specs=vmem(5),
        out_specs=tuple(vmem(4)),
        scratch_shapes=[pltpu.VMEM((rows, TILE), F32)],
        compiler_params=pltpu.CompilerParams(vmem_limit_bytes=12 << 20),
        cost_estimate=pl.CostEstimate(
            flops=2 * place_hot.size * parts * size_z, bytes_accessed=cells.size * 4, transcendentals=0
        ),
        name="pool",
    )(cells, place_hot, gains, half_column, slot_hot)


def stencil(planes, fences, slabs, crosses, velocity, halos):
    parts, size_x, size_y, size_z = velocity.shape
    edges = len(halos) > 2
    return pl.pallas_call(
        functools.partial(stencil_kernel, planes, edges, len(fences), slabs, crosses),
        out_shape=jax.ShapeDtypeStruct((parts, len(planes), size_y, size_z), F32),
        in_specs=[ANY] * len(fences) + vmem(1 + len(halos)),
        out_specs=vmem(1)[0],
        compiler_params=pltpu.CompilerParams(vmem_limit_bytes=4 << 20),
        cost_estimate=pl.CostEstimate(
            flops=1000 * velocity.size * len(planes) // size_x,
            bytes_accessed=8 * velocity.size * len(planes) // size_x,
            transcendentals=0,
        ),
        name="stencil",
    )(*fences, velocity, *halos)


def key_matrix(rotors, fences, slots, sub, keys):
    entries = slots.shape[0] * TILE
    return pl.pallas_call(
        functools.partial(key_kernel, rotors, len(fences)),
        out_shape=jax.ShapeDtypeStruct((entries, keys), BF16),
        in_specs=[ANY] * len(fences) + vmem(2),
        out_specs=vmem(1)[0],
        compiler_params=pltpu.CompilerParams(vmem_limit_bytes=4 << 20),
        cost_estimate=pl.CostEstimate(
            flops=1000 * entries * keys, bytes_accessed=2 * entries * keys, transcendentals=0
        ),
        name="keys",
    )(*fences, slots, sub)


def place_matrix(fence, tile, columns, halves):
    entries = tile.shape[0] * TILE
    return pl.pallas_call(
        functools.partial(place_kernel, halves),
        out_shape=jax.ShapeDtypeStruct((columns, entries), BF16),
        in_specs=[ANY] + vmem(1),
        out_specs=vmem(1)[0],
        compiler_params=pltpu.CompilerParams(vmem_limit_bytes=4 << 20),
        cost_estimate=pl.CostEstimate(
            flops=1000 * entries * columns, bytes_accessed=2 * entries * columns, transcendentals=0
        ),
        name="places",
    )(fence, tile)


def join(bits, fences, keep, other, states, cells):
    parts, _, size_y, size_z = cells.shape
    rows = keep.shape[0] + states.size // 2 // TILE
    return pl.pallas_call(
        functools.partial(join_kernel, bits, len(fences)),
        out_shape=(
            jax.ShapeDtypeStruct((rows, TILE), F32),
            jax.ShapeDtypeStruct((parts, size_y, size_z), BF16),
            jax.ShapeDtypeStruct((parts, size_y, size_z), BF16),
        ),
        in_specs=[ANY] * len(fences) + vmem(4),
        out_specs=tuple(vmem(3)),
        compiler_params=pltpu.CompilerParams(vmem_limit_bytes=4 << 20),
        name="join",
    )(*fences, keep, other, states, cells)


def merge(fences, shift, rows, width, pooled_rows, packed, pooled):
    total = pooled_rows + len(packed) * (packed[0].shape[0] - pooled_rows)
    return pl.pallas_call(
        functools.partial(
            merge_kernel, len(fences), len(packed), shift, rows, width, pooled_rows
        ),
        out_shape=jax.ShapeDtypeStruct((total, TILE), F32),
        in_specs=[ANY] * len(fences) + vmem(len(packed) + len(pooled)),
        out_specs=vmem(1)[0],
        compiler_params=pltpu.CompilerParams(vmem_limit_bytes=4 << 20),
        name="merge",
    )(*fences, *packed, *pooled)


def rotors_step(
    slabs, bits, runs, tile, sub, w_in, w_out, decay, key_hot, place_hot, keep, other, fields
):
    width = w_in.shape[1]
    parts, _, size_y, size_z = fields[0].shape
    size_x = sum(field.shape[1] for field in fields)
    keys = key_hot.shape[1]
    rows = keys // (w_out.shape[1] // (2 * TILE)) // slabs
    chunks = 2
    return pl.pallas_call(
        functools.partial(rotor_kernel, bits, runs),
        out_shape=(
            jax.ShapeDtypeStruct((parts, size_x, size_y, size_z), F32),
            jax.ShapeDtypeStruct((rows, width), F32),
        ),
        in_specs=vmem(9 + len(fields)),
        out_specs=(HBM, HBM),
        scratch_shapes=[
            pltpu.VMEM((slabs, rows, width), F32),
            pltpu.VMEM((keys, 2 * TILE), BF16),
            pltpu.VMEM((size_x, size_y, size_z), F32),
            pltpu.SemaphoreType.DMA((len(runs) + chunks,)),
            pltpu.SemaphoreType.DMA,
        ],
        compiler_params=pltpu.CompilerParams(vmem_limit_bytes=10 << 20),
        cost_estimate=pl.CostEstimate(
            flops=4 * place_hot.size * size_z, bytes_accessed=w_out.size * 2, transcendentals=0
        ),
        name="rotors",
    )(tile, sub, w_in, w_out, decay, key_hot, place_hot, keep, other, *fields)


def on_device(
    slabs,
    crosses,
    velocity,
    shape_weight,
    w_in,
    w_out,
    decay,
    rotor_states,
    slot_of_rotor,
    entry_rotor,
    entry_tile,
    entry_sub,
):
    size_x, size_y, size_z = velocity.shape[1:]
    entries = entry_tile.shape[0]
    width = w_in.shape[1]
    count = slabs * crosses
    tile = entry_tile.reshape(entries // TILE, TILE)
    rotor = entry_rotor.reshape(entries // TILE, TILE)
    sub = entry_sub.reshape(entries // TILE, TILE)

    bits = count.bit_length() - 1
    slots, cells, *loaded = load(tile, rotor, sub, slot_of_rotor, shape_weight, velocity)
    keep, send, y_even, y_odd = pool(bits, cells, *loaded)
    y_even = swap_pairs(y_even, "cross", (slabs, crosses), 0)
    y_odd = swap_pairs(y_odd, "cross", (slabs, crosses), 1)
    pooled_rows = keep.shape[0]

    middle = size_x // 4
    inner, outer = tuple(range(1, middle)), (0,) + tuple(range(middle, size_x))
    runs = ((1, middle - 1, 0, 0), (0, 1, 1, 0), (middle, size_x - middle, 1, 1))
    packed, x_even, x_odd = join(
        bits, (), keep, swap(send, BOTH, count, 1), rotor_states, cells
    )
    x_even = swap_pairs(x_even, "slab", (slabs, crosses), 0)
    x_odd = swap_pairs(x_odd, "slab", (slabs, crosses), 1)
    slab_bit = crosses.bit_length() - 1
    steps = [tuple(range(b, min(b + 2, bits))) for b in range(1, bits, 2)][::-1]
    fields = []
    for step in steps:
        made = []
        if step == steps[0]:
            rotors = slot_of_rotor.shape[0]
            keys = w_out.shape[1] // (2 * TILE) * rotors
            key_hot = key_matrix(rotors, (packed,), slots, sub, keys)
            fields.append(stencil(inner, (packed,), slabs, crosses, cells, (y_even, y_odd)))
            made += [key_hot, fields[-1]]
        if step == steps[-1]:
            place_hot = place_matrix(packed, tile, size_x * size_y, size_z // TILE)
            halos = (y_even, y_odd, x_even, x_odd)
            fields.append(stencil(outer, (packed,), slabs, crosses, cells, halos))
            made += [place_hot, fields[-1]]
        slab_bits = [b for b in step if b >= slab_bit]
        across = [1 << b | 1 for b in slab_bits]
        if len(slab_bits) == 2:
            across.append(sum(1 << b for b in step))
            within = []
        else:
            within = [1 << b | 1 for b in step if b < slab_bit]
            within += [sum(1 << b for b in step)] if len(step) == 2 else []
        sums = packed[:pooled_rows]
        packed = merge(
            made,
            slab_bits[0] - slab_bit,
            rotor_states.shape[0],
            width // 2,
            pooled_rows,
            [packed] + [swap(packed, BOTH, count, offset) for offset in across],
            [swap(sums, BOTH, count, offset) for offset in within],
        )
    other = swap(packed, BOTH, count, 1)
    return rotors_step(
        slabs,
        bits,
        runs,
        tile,
        sub,
        w_in,
        w_out,
        decay[None, :],
        key_hot,
        place_hot,
        packed,
        other,
        fields,
    )


def solution(mesh):
    slabs, crosses = mesh.shape["slab"], mesh.shape["cross"]
    in_specs = (
        P(None, "slab", "cross", None),
        P(),
        P(),
        P(),
        P(),
        P("slab", None),
        P(),
        P(("slab", "cross"), None),
        P(("slab", "cross")),
        P(("slab", "cross")),
    )
    out_specs = (P(None, "slab", "cross", None), P("slab", None))
    return jax.shard_map(
        functools.partial(on_device, slabs, crosses),
        mesh=mesh,
        in_specs=in_specs,
        out_specs=out_specs,
        check_vma=False,
    )
```

```python
import functools

import jax
import jax.numpy as jnp
from jax import lax
from jax.experimental import pallas as pl
from jax.experimental.pallas import tpu as pltpu
from jax.sharding import PartitionSpec as P

TILE = 128

time_step = 0.1
viscosity = 0.3
pool_scale = 1.0 / 64.0
state_step = 0.5
force_scale = 0.5

BOTH = ("slab", "cross")
F32 = jnp.float32
BF16 = jnp.bfloat16


def lanes(rows):
    return lax.broadcasted_iota(jnp.int32, (rows, TILE), 1)


def sublanes(rows):
    return lax.broadcasted_iota(jnp.int32, (rows, TILE), 0)


def as_column(row):
    return jnp.transpose(jnp.broadcast_to(row, (TILE, TILE)))


def hot(mask):
    return jnp.where(mask, 1.0, 0.0).astype(BF16)


def slots_of(rotors, slot_ref):
    slots = jnp.zeros_like(rotors)
    for rotor in range(slot_ref.shape[0]):
        slots = jnp.where(rotors == rotor, slot_ref[rotor], slots)
    return slots


def load_kernel(
    tile_ref,
    rotor_ref,
    sub_ref,
    slot_ref,
    weight_ref,
    velocity_ref,
    slots_ref,
    cells,
    place_hot,
    gains,
    half_column,
    slot_hot,
    tiles,
    rotor_rows,
    sub_rows,
    slot_table,
    weights,
    sems,
    small_sems,
):
    parts, size_x, size_y, size_z = velocity_ref.shape
    columns = size_x * size_y
    halves = size_z // TILE
    groups = tile_ref.shape[0]
    rotors = slot_ref.shape[0]
    subs = weight_ref.shape[0]
    small = [
        pltpu.make_async_copy(source, target, small_sems.at[i])
        for i, (source, target) in enumerate(
            (
                (tile_ref, tiles),
                (sub_ref, sub_rows),
                (weight_ref, weights),
                (rotor_ref, rotor_rows),
                (slot_ref, slot_table),
            )
        )
    ]
    copies = [
        pltpu.make_async_copy(velocity_ref.at[c], cells.at[c], sems.at[c]) for c in range(parts)
    ]
    for copy in small + copies:
        copy.start()
    for copy in small:
        copy.wait()
    weight = weights[...]
    high = weight.astype(BF16)
    rest = weight - high.astype(F32)
    middle = rest.astype(BF16)
    low = (rest - middle.astype(F32)).astype(BF16)
    weight_parts = jnp.concatenate([high, middle, low], axis=0)
    sub_hot = []
    place_rows = tiles[...] // halves
    half_rows = tiles[...] % halves
    for group in range(groups):
        half_column[pl.ds(group * TILE, TILE), :] = as_column(half_rows[group : group + 1, :])
        place = as_column(place_rows[group : group + 1, :])
        for block in range(columns // TILE):
            place_hot[pl.ds(group * TILE, TILE), pl.ds(block * TILE, TILE)] = hot(
                place == lanes(TILE) + block * TILE
            )
        sub = as_column(sub_rows[group : group + 1, :])
        wide = jnp.concatenate([sub[:, :subs]] * 3, axis=1)
        index = lax.broadcasted_iota(jnp.int32, (TILE, subs), 1)
        sub_hot.append(hot(wide == jnp.concatenate([index] * 3, axis=1)))
    gains[...] = jnp.dot(
        jnp.concatenate(sub_hot, axis=0), weight_parts, preferred_element_type=F32
    )
    slots = slots_of(rotor_rows[...], slot_table)
    slots_ref[...] = slots
    slot_hot[...] = jnp.concatenate(
        [hot(slots[g : g + 1, :] == sublanes(rotors)) for g in range(groups)], axis=1
    )
    for copy in copies:
        copy.wait()


def first_half(bits):
    index = lax.axis_index("slab") * lax.axis_size("cross") + lax.axis_index("cross")
    parity = index
    for bit in range(1, bits):
        parity = parity ^ (index >> bit)
    return parity % 2 == 0


def pool_kernel(
    bits,
    cells,
    place_hot,
    gains,
    half_column,
    slot_hot,
    keep_ref,
    send_ref,
    y_even_ref,
    y_odd_ref,
    total,
):
    parts, size_x, size_y, size_z = cells.shape
    columns = size_x * size_y
    halves = size_z // TILE
    rotors = slot_hot.shape[0]
    half = half_column[...]
    even_y = lax.axis_index("cross") % 2 == 0
    flat = jnp.concatenate(
        [cells[c].reshape(columns, size_z).astype(BF16) for c in range(parts)], axis=1
    )
    found = jnp.dot(place_hot[...], flat, preferred_element_type=F32)
    for c in range(parts):
        sample = found[:, c * size_z : c * size_z + TILE]
        for h in range(1, halves):
            at = c * size_z + h * TILE
            sample = jnp.where(half == h, found[:, at : at + TILE], sample)
        weighted = sample * gains[:, c * TILE : (c + 1) * TILE]
        high = weighted.astype(BF16)
        low = (weighted - high.astype(F32)).astype(BF16)
        sums = jnp.dot(
            slot_hot[...], jnp.concatenate([high, low], axis=1), preferred_element_type=F32
        )
        total[c * rotors : (c + 1) * rotors, :] = sums[:, TILE:] + sums[:, :TILE]
        first, last = cells[c, :, 0, :], cells[c, :, size_y - 1, :]
        y_even_ref[c] = jnp.where(even_y, last, first).astype(BF16)
        y_odd_ref[c] = jnp.where(even_y, first, last).astype(BF16)
    rows = keep_ref.shape[0]
    first, second = total[:rows, :], total[rows:, :]
    keep_ref[...] = jnp.where(first_half(bits), first, second)
    send_ref[...] = jnp.where(first_half(bits), second, first)


def pack_rows(target_ref, start, blocks):
    rows, width = blocks[0].shape
    count = rows * len(blocks)
    for j in range(width // TILE):
        for k, block in enumerate(blocks):
            at = start + j * count + k * rows
            target_ref[at : at + rows, :] = block[:, j * TILE : (j + 1) * TILE]


def unpack_rows(source_ref, start, width):
    count = (source_ref.shape[0] - start) // (width // TILE)
    return jnp.concatenate(
        [source_ref[start + j * count : start + (j + 1) * count, :] for j in range(width // TILE)],
        axis=1,
    )


def stencil_kernel(planes, edges, fences, slabs, crosses, *refs):
    refs, out_ref = refs[fences:-1], refs[-1]
    velocity_ref, y_even_ref, y_odd_ref = refs[:3]
    if edges:
        x_even_ref, x_odd_ref = refs[3:]
    parts, size_x, size_y, size_z = velocity_ref.shape
    row = lax.broadcasted_iota(jnp.int32, (size_y, size_z), 0)
    lane = lax.broadcasted_iota(jnp.int32, (size_y, size_z), 1)
    slab, cross = lax.axis_index("slab"), lax.axis_index("cross")
    even_x, even_y = slab % 2 == 0, cross % 2 == 0
    inner_x = jnp.logical_and(slab > 0, slab < slabs - 1)
    inner_y = jnp.logical_and(cross > 0, cross < crosses - 1)
    souths, norths = [], []
    for c in range(parts):
        near = y_even_ref[c].astype(F32)
        far = jnp.where(inner_y, y_odd_ref[c].astype(F32), 0.0)
        souths.append(jnp.where(even_y, far, near))
        norths.append(jnp.where(even_y, near, far))
    spread = time_step * viscosity
    for at, x in enumerate(planes):
        drift = [(0.5 * time_step) * velocity_ref[d, x] for d in range(parts)]
        to_east, to_west = spread - drift[0], spread + drift[0]
        to_north, to_south = spread - drift[1], spread + drift[1]
        to_upper = jnp.where(lane == size_z - 1, 0.0, spread - drift[2])
        to_lower = jnp.where(lane == 0, 0.0, spread + drift[2])
        for c in range(parts):
            here = velocity_ref[c, x]
            if x > 0:
                west = velocity_ref[c, x - 1]
            else:
                far_x = jnp.where(inner_x, x_odd_ref[c].astype(F32), 0.0)
                west = jnp.where(even_x, far_x, x_even_ref[c].astype(F32))
            if x + 1 < size_x:
                east = velocity_ref[c, x + 1]
            else:
                far_x = jnp.where(inner_x, x_odd_ref[c].astype(F32), 0.0)
                east = jnp.where(even_x, x_even_ref[c].astype(F32), far_x)
            south = jnp.where(row == 0, souths[c][x : x + 1, :], pltpu.roll(here, 1, 0))
            north = jnp.where(
                row == size_y - 1, norths[c][x : x + 1, :], pltpu.roll(here, size_y - 1, 0)
            )
            out_ref[c, at] = (
                (1.0 - 6.0 * spread) * here
                + (to_east * east + to_west * west)
                + (to_north * north + to_south * south)
                + (to_upper * pltpu.roll(here, size_z - 1, 1) + to_lower * pltpu.roll(here, 1, 1))
            )


def key_kernel(rotors, fences, *refs):
    slots_ref, sub_ref, key_ref = refs[fences:]
    keys = sub_ref[...] // 2 * rotors + slots_ref[...]
    for group in range(keys.shape[0]):
        key = as_column(keys[group : group + 1, :])
        for block in range(key_ref.shape[1] // TILE):
            key_ref[pl.ds(group * TILE, TILE), pl.ds(block * TILE, TILE)] = hot(
                key == lanes(TILE) + block * TILE
            )


def place_kernel(halves, fence_ref, tile_ref, place_ref):
    del fence_ref
    places = tile_ref[...] // halves
    low, high = (places % TILE).astype(F32), (places // TILE).astype(F32)
    rows = sublanes(TILE).astype(F32).astype(BF16)
    zeros = jnp.zeros((TILE, TILE), BF16)
    for group in range(places.shape[0]):
        row = jnp.broadcast_to(low[group : group + 1, :], (TILE, TILE)).astype(BF16)
        part = jnp.broadcast_to(high[group : group + 1, :], (TILE, TILE)).astype(BF16)
        found = jnp.where(row == rows, jnp.ones((TILE, TILE), BF16), zeros)
        for block in range(place_ref.shape[0] // TILE):
            place_ref[pl.ds(block * TILE, TILE), pl.ds(group * TILE, TILE)] = jnp.where(
                part == jnp.asarray(block, BF16), found, zeros
            )


def join_kernel(bits, fences, *refs):
    keep_ref, other_ref, states_ref, cells, out_ref, x_even_ref, x_odd_ref = refs[fences:]
    even_x = lax.axis_index("slab") % 2 == 0
    for c in range(cells.shape[0]):
        first, last = cells[c, 0], cells[c, cells.shape[1] - 1]
        x_even_ref[c] = jnp.where(even_x, last, first).astype(BF16)
        x_odd_ref[c] = jnp.where(even_x, first, last).astype(BF16)
    rows = keep_ref.shape[0]
    out_ref[:rows, :] = keep_ref[...] + other_ref[...]
    half = states_ref.shape[1] // 2
    pack_rows(
        out_ref, rows, [jnp.where(first_half(bits), states_ref[:, :half], states_ref[:, half:])]
    )


def merge_kernel(fences, packs, shift, rows, width, pooled_rows, *refs):
    refs, out_ref = refs[fences:-1], refs[-1]
    total = refs[0][:pooled_rows, :]
    for other in refs[1:]:
        total = total + other[:pooled_rows, :]
    out_ref[:pooled_rows, :] = total
    mine = (lax.axis_index("slab") >> shift) % packs
    blocks = [unpack_rows(ref, pooled_rows, width) for ref in refs[:packs]]
    ordered = []
    for place in range(packs):
        block = blocks[0]
        for k in range(1, packs):
            block = jnp.where((mine ^ k) == place, blocks[k], block)
        ordered.append(block)
    pieces = []
    for at in range(0, blocks[0].shape[0], rows):
        pieces += [block[at : at + rows] for block in ordered]
    pack_rows(out_ref, pooled_rows, pieces)


def rotor_kernel(
    bits,
    runs,
    tile_ref,
    sub_ref,
    w_in_ref,
    w_out_ref,
    decay_ref,
    key_hot,
    place_hot,
    keep_ref,
    other_ref,
    *rest,
):
    count = 1 + max(run[2] for run in runs)
    field_refs, rest = rest[:count], rest[count:]
    out_ref, new_ref, by_slab, source_rows, wind, sems, new_sem = rest
    slabs, rows, width = by_slab.shape
    rotors = slabs * rows
    size_x, size_y, size_z = wind.shape
    parts = w_in_ref.shape[0] // TILE
    halves = size_z // TILE
    groups = tile_ref.shape[0]
    subs = w_out_ref.shape[1] // TILE
    stores = []
    for k, (first, number, which, at) in enumerate(runs):
        stores.append(
            pltpu.make_async_copy(
                field_refs[which].at[1:, pl.ds(at, number)],
                out_ref.at[1:, pl.ds(first, number)],
                sems.at[k],
            )
        )
        stores[-1].start()
    split = parts * rotors // 2
    first = first_half(bits)
    keep, other = keep_ref[:split, :], other_ref[:split, :]
    pooled = jnp.concatenate(
        [jnp.where(first, keep, other), jnp.where(first, other, keep)], axis=0
    )
    pooled = (pooled * pool_scale).astype(BF16)
    pooled = jnp.concatenate([pooled[c * rotors : (c + 1) * rotors] for c in range(parts)], axis=1)
    keep, other = [unpack_rows(ref, split, width // 2) for ref in (keep_ref, other_ref)]
    old = jnp.concatenate(
        [jnp.where(first, keep, other), jnp.where(first, other, keep)], axis=1
    )
    drive = jnp.dot(pooled, w_in_ref[...], preferred_element_type=F32)
    new = old + state_step * (drive - decay_ref[...] * old)
    for j in range(slabs):
        by_slab[j] = new[j * rows : (j + 1) * rows, :]
    own = pltpu.make_async_copy(by_slab.at[lax.axis_index("slab")], new_ref, new_sem)
    own.start()
    stores.append(own)
    new_b = new.astype(BF16)

    half_rows = tile_ref[...] % halves
    new_b = jnp.concatenate([new_b, jnp.zeros((max(TILE - rotors, 0), width), BF16)], axis=0)
    sources = jnp.dot(new_b, w_out_ref[...], preferred_element_type=F32)[:rotors].astype(BF16)
    for pair in range(subs // 2):
        source_rows[pair * rotors : (pair + 1) * rotors, :] = sources[
            :, pair * 2 * TILE : (pair + 1) * 2 * TILE
        ]
    taken = jnp.dot(key_hot[...], source_rows[...], preferred_element_type=F32)
    second = jnp.concatenate(
        [as_column(sub_ref[g : g + 1, :] % 2) for g in range(groups)], axis=0
    )
    taken = jnp.where(second == 1, taken[:, TILE:], taken[:, :TILE])
    half = jnp.concatenate([as_column(half_rows[g : g + 1, :]) for g in range(groups)], axis=0)
    spread = jnp.concatenate(
        [jnp.where(half == h, taken, 0.0).astype(BF16) for h in range(halves)], axis=1
    )
    chunks = sems.shape[0] - len(runs)
    step = size_x // chunks
    for k in range(chunks):
        forcing = jnp.dot(
            place_hot[pl.ds(k * step * size_y, step * size_y), :],
            spread,
            preferred_element_type=F32,
        ).reshape(step, size_y, size_z)
        for first, number, which, at in runs:
            begin, end = max(first, k * step), min(first + number, (k + 1) * step)
            if begin < end:
                field = field_refs[which][0, at + begin - first : at + end - first]
                wind[begin:end] = field - force_scale * forcing[begin - k * step : end - k * step]
        at = pl.ds(k * step, step)
        stores.append(
            pltpu.make_async_copy(wind.at[at], out_ref.at[0, at], sems.at[len(runs) + k])
        )
        stores[-1].start()
    for store in stores:
        store.wait()


def swap(value, axis, count, offset):
    return lax.ppermute(value, axis, [(i, i ^ offset) for i in range(count)])


def swap_pairs(value, axis, counts, first):
    slabs, crosses = counts
    if axis == "cross":
        pairs = [(i, (i + 1) % crosses) for i in range(first, crosses, 2)]
        return lax.ppermute(value, axis, pairs + [(j, i) for i, j in pairs])
    partner = {i: i + 1 for i in range(first, slabs - 1, 2)}
    partner.update({j: i for i, j in partner.items()})
    pairs = []
    for slab in range(slabs):
        for cross in range(crosses):
            to = (partner[slab], cross) if slab in partner else (slab, cross ^ 1)
            pairs.append((slab * crosses + cross, to[0] * crosses + to[1]))
    return lax.ppermute(value, BOTH, pairs)


def vmem(count):
    return [pl.BlockSpec(memory_space=pltpu.VMEM)] * count


def in_hbm(value):
    return pltpu.with_memory_space_constraint(value, pltpu.HBM)


SMEM = pl.BlockSpec(memory_space=pltpu.SMEM)
HBM = pl.BlockSpec(memory_space=pltpu.HBM)
ANY = pl.BlockSpec(memory_space=pl.ANY)


def load(tile, rotor, sub, slot_of_rotor, shape_weight, velocity):
    parts, size_x, size_y, size_z = velocity.shape
    columns = size_x * size_y
    groups = tile.shape[0]
    entries = groups * TILE
    rotors = slot_of_rotor.shape[0]
    return pl.pallas_call(
        load_kernel,
        out_shape=(
            jax.ShapeDtypeStruct((groups, TILE), jnp.int32),
            jax.ShapeDtypeStruct(velocity.shape, F32),
            jax.ShapeDtypeStruct((entries, columns), BF16),
            jax.ShapeDtypeStruct((entries, parts * TILE), F32),
            jax.ShapeDtypeStruct((entries, TILE), jnp.int32),
            jax.ShapeDtypeStruct((rotors, entries), BF16),
        ),
        in_specs=[HBM] * 6,
        out_specs=tuple(vmem(6)),
        scratch_shapes=[
            pltpu.VMEM((groups, TILE), jnp.int32),
            pltpu.VMEM((groups, TILE), jnp.int32),
            pltpu.VMEM((groups, TILE), jnp.int32),
            pltpu.SMEM((rotors,), jnp.int32),
            pltpu.VMEM(shape_weight.shape, F32),
            pltpu.SemaphoreType.DMA((parts,)),
            pltpu.SemaphoreType.DMA((5,)),
        ],
        compiler_params=pltpu.CompilerParams(vmem_limit_bytes=8 << 20),
        cost_estimate=pl.CostEstimate(
            flops=2 * entries * columns * size_z,
            bytes_accessed=velocity.size * 4,
            transcendentals=0,
        ),
        name="load",
    )(*(in_hbm(value) for value in (tile, rotor, sub, slot_of_rotor, shape_weight, velocity)))


def pool(bits, cells, place_hot, gains, half_column, slot_hot):
    parts, size_x, size_y, size_z = cells.shape
    rows = parts * slot_hot.shape[0]
    part = jax.ShapeDtypeStruct((rows // 2, TILE), F32)
    return pl.pallas_call(
        functools.partial(pool_kernel, bits),
        out_shape=(
            part,
            part,
            jax.ShapeDtypeStruct((parts, size_x, size_z), BF16),
            jax.ShapeDtypeStruct((parts, size_x, size_z), BF16),
        ),
        in_specs=vmem(5),
        out_specs=tuple(vmem(4)),
        scratch_shapes=[pltpu.VMEM((rows, TILE), F32)],
        compiler_params=pltpu.CompilerParams(vmem_limit_bytes=12 << 20),
        cost_estimate=pl.CostEstimate(
            flops=2 * place_hot.size * parts * size_z, bytes_accessed=cells.size * 4, transcendentals=0
        ),
        name="pool",
    )(cells, place_hot, gains, half_column, slot_hot)


def stencil(planes, fences, slabs, crosses, velocity, halos):
    parts, size_x, size_y, size_z = velocity.shape
    edges = len(halos) > 2
    return pl.pallas_call(
        functools.partial(stencil_kernel, planes, edges, len(fences), slabs, crosses),
        out_shape=jax.ShapeDtypeStruct((parts, len(planes), size_y, size_z), F32),
        in_specs=[ANY] * len(fences) + vmem(1 + len(halos)),
        out_specs=vmem(1)[0],
        compiler_params=pltpu.CompilerParams(vmem_limit_bytes=4 << 20),
        cost_estimate=pl.CostEstimate(
            flops=1000 * velocity.size * len(planes) // size_x,
            bytes_accessed=8 * velocity.size * len(planes) // size_x,
            transcendentals=0,
        ),
        name="stencil",
    )(*fences, velocity, *halos)


def key_matrix(rotors, fences, slots, sub, keys):
    entries = slots.shape[0] * TILE
    return pl.pallas_call(
        functools.partial(key_kernel, rotors, len(fences)),
        out_shape=jax.ShapeDtypeStruct((entries, keys), BF16),
        in_specs=[ANY] * len(fences) + vmem(2),
        out_specs=vmem(1)[0],
        compiler_params=pltpu.CompilerParams(vmem_limit_bytes=4 << 20),
        cost_estimate=pl.CostEstimate(
            flops=1000 * entries * keys, bytes_accessed=2 * entries * keys, transcendentals=0
        ),
        name="keys",
    )(*fences, slots, sub)


def place_matrix(fence, tile, columns, halves):
    entries = tile.shape[0] * TILE
    return pl.pallas_call(
        functools.partial(place_kernel, halves),
        out_shape=jax.ShapeDtypeStruct((columns, entries), BF16),
        in_specs=[ANY] + vmem(1),
        out_specs=vmem(1)[0],
        compiler_params=pltpu.CompilerParams(vmem_limit_bytes=4 << 20),
        cost_estimate=pl.CostEstimate(
            flops=1000 * entries * columns, bytes_accessed=2 * entries * columns, transcendentals=0
        ),
        name="places",
    )(fence, tile)


def join(bits, fences, keep, other, states, cells):
    parts, _, size_y, size_z = cells.shape
    rows = keep.shape[0] + states.size // 2 // TILE
    return pl.pallas_call(
        functools.partial(join_kernel, bits, len(fences)),
        out_shape=(
            jax.ShapeDtypeStruct((rows, TILE), F32),
            jax.ShapeDtypeStruct((parts, size_y, size_z), BF16),
            jax.ShapeDtypeStruct((parts, size_y, size_z), BF16),
        ),
        in_specs=[ANY] * len(fences) + vmem(4),
        out_specs=tuple(vmem(3)),
        compiler_params=pltpu.CompilerParams(vmem_limit_bytes=4 << 20),
        name="join",
    )(*fences, keep, other, states, cells)


def merge(fences, shift, rows, width, pooled_rows, packed, pooled):
    total = pooled_rows + len(packed) * (packed[0].shape[0] - pooled_rows)
    return pl.pallas_call(
        functools.partial(
            merge_kernel, len(fences), len(packed), shift, rows, width, pooled_rows
        ),
        out_shape=jax.ShapeDtypeStruct((total, TILE), F32),
        in_specs=[ANY] * len(fences) + vmem(len(packed) + len(pooled)),
        out_specs=vmem(1)[0],
        compiler_params=pltpu.CompilerParams(vmem_limit_bytes=4 << 20),
        name="merge",
    )(*fences, *packed, *pooled)


def rotors_step(
    slabs, bits, runs, tile, sub, w_in, w_out, decay, key_hot, place_hot, keep, other, fields
):
    width = w_in.shape[1]
    parts, _, size_y, size_z = fields[0].shape
    size_x = sum(field.shape[1] for field in fields)
    keys = key_hot.shape[1]
    rows = keys // (w_out.shape[1] // (2 * TILE)) // slabs
    chunks = 2
    return pl.pallas_call(
        functools.partial(rotor_kernel, bits, runs),
        out_shape=(
            jax.ShapeDtypeStruct((parts, size_x, size_y, size_z), F32),
            jax.ShapeDtypeStruct((rows, width), F32),
        ),
        in_specs=vmem(9 + len(fields)),
        out_specs=(HBM, HBM),
        scratch_shapes=[
            pltpu.VMEM((slabs, rows, width), F32),
            pltpu.VMEM((keys, 2 * TILE), BF16),
            pltpu.VMEM((size_x, size_y, size_z), F32),
            pltpu.SemaphoreType.DMA((len(runs) + chunks,)),
            pltpu.SemaphoreType.DMA,
        ],
        compiler_params=pltpu.CompilerParams(vmem_limit_bytes=10 << 20),
        cost_estimate=pl.CostEstimate(
            flops=4 * place_hot.size * size_z, bytes_accessed=w_out.size * 2, transcendentals=0
        ),
        name="rotors",
    )(tile, sub, w_in, w_out, decay, key_hot, place_hot, keep, other, *fields)


def on_device(
    slabs,
    crosses,
    velocity,
    shape_weight,
    w_in,
    w_out,
    decay,
    rotor_states,
    slot_of_rotor,
    entry_rotor,
    entry_tile,
    entry_sub,
):
    size_x, size_y, size_z = velocity.shape[1:]
    entries = entry_tile.shape[0]
    width = w_in.shape[1]
    count = slabs * crosses
    tile = entry_tile.reshape(entries // TILE, TILE)
    rotor = entry_rotor.reshape(entries // TILE, TILE)
    sub = entry_sub.reshape(entries // TILE, TILE)

    bits = count.bit_length() - 1
    slots, cells, *loaded = load(tile, rotor, sub, slot_of_rotor, shape_weight, velocity)
    keep, send, y_even, y_odd = pool(bits, cells, *loaded)
    y_even = swap_pairs(y_even, "cross", (slabs, crosses), 0)
    y_odd = swap_pairs(y_odd, "cross", (slabs, crosses), 1)
    pooled_rows = keep.shape[0]

    middle = size_x * 5 // 16
    inner, outer = tuple(range(1, middle)), (0,) + tuple(range(middle, size_x))
    runs = ((1, middle - 1, 0, 0), (0, 1, 1, 0), (middle, size_x - middle, 1, 1))
    packed, x_even, x_odd = join(
        bits, (), keep, swap(send, BOTH, count, 1), rotor_states, cells
    )
    x_even = swap_pairs(x_even, "slab", (slabs, crosses), 0)
    x_odd = swap_pairs(x_odd, "slab", (slabs, crosses), 1)
    slab_bit = crosses.bit_length() - 1
    steps = [tuple(range(b, min(b + 2, bits))) for b in range(1, bits, 2)][::-1]
    fields = []
    for step in steps:
        made = []
        if step == steps[0]:
            rotors = slot_of_rotor.shape[0]
            keys = w_out.shape[1] // (2 * TILE) * rotors
            key_hot = key_matrix(rotors, (packed,), slots, sub, keys)
            fields.append(stencil(inner, (packed,), slabs, crosses, cells, (y_even, y_odd)))
            made += [key_hot, fields[-1]]
        if step == steps[-1]:
            place_hot = place_matrix(packed, tile, size_x * size_y, size_z // TILE)
            halos = (y_even, y_odd, x_even, x_odd)
            fields.append(stencil(outer, (packed,), slabs, crosses, cells, halos))
            made += [place_hot, fields[-1]]
        slab_bits = [b for b in step if b >= slab_bit]
        across = [1 << b | 1 for b in slab_bits]
        if len(slab_bits) == 2:
            across.append(sum(1 << b for b in step))
            within = []
        else:
            within = [1 << b | 1 for b in step if b < slab_bit]
            within += [sum(1 << b for b in step)] if len(step) == 2 else []
        sums = packed[:pooled_rows]
        packed = merge(
            made,
            slab_bits[0] - slab_bit,
            rotor_states.shape[0],
            width // 2,
            pooled_rows,
            [packed] + [swap(packed, BOTH, count, offset) for offset in across],
            [swap(sums, BOTH, count, offset) for offset in within],
        )
    other = swap(packed, BOTH, count, 1)
    return rotors_step(
        slabs,
        bits,
        runs,
        tile,
        sub,
        w_in,
        w_out,
        decay[None, :],
        key_hot,
        place_hot,
        packed,
        other,
        fields,
    )


def solution(mesh):
    slabs, crosses = mesh.shape["slab"], mesh.shape["cross"]
    in_specs = (
        P(None, "slab", "cross", None),
        P(),
        P(),
        P(),
        P(),
        P("slab", None),
        P(),
        P(("slab", "cross"), None),
        P(("slab", "cross")),
        P(("slab", "cross")),
    )
    out_specs = (P(None, "slab", "cross", None), P("slab", None))
    return jax.shard_map(
        functools.partial(on_device, slabs, crosses),
        mesh=mesh,
        in_specs=in_specs,
        out_specs=out_specs,
        check_vma=False,
    )
```
